512 devices in a mesh: ctx: 64 (over z, y_hi, core), tp: 8 (over x, y_lo).
Axes of the slice: x: 4, y: 4 (y_hi: 2, y_lo: 2; y = y_hi * 2 + y_lo), z: 16, core: 2. Of those that a mesh axis runs over, the one named last changes fastest.
Arguments:
- out_grad: bfloat16 [16384, 4096], P('ctx', 'tp'), may hold values from -6 to 6
- out_weight: bfloat16 [8192, 4096], P('tp', 'ctx'), may hold values from -0.0625 to 0.0625
- signal: bfloat16 [16384, 8192], P('ctx', 'tp'), may hold values from -6 to 6
- gate_input: bfloat16 [16384, 8192], P('ctx', 'tp'), may hold values from -6 to 6
- filter_taps: float32 [128, 8192], P(None, ('tp', 'ctx')), may hold values from -0.5 to 0.5
Outputs:
- signal_grad: bfloat16 [16384, 8192], P('ctx', 'tp')
- gate_grad: bfloat16 [16384, 8192], P('ctx', 'tp')
- filter_grad: float32 [128, 8192], P(None, ('tp', 'ctx'))
The draws below stay inside these ranges and needn't reach their ends.
All inputs are finite; a program needn't handle non-finite values.
Results may differ from the reference program's by a relative error of at most 0.0057.
Values may be sent and summed in bfloat16 or wider, within the bound.
No kernel may reach another device: no remote copies, remote signals or barrier semaphores. Data moves between devices by JAX's collectives and lax.ppermute only.
A program may use at most 128 MiB of HBM per device.

```python
import jax
import jax.numpy as jnp
from jax import lax

D = 8192
K = 128
DO = 4096
TOKENS = 16384
LEN = 8192
SEQS = 2


def level_of(own_key, shape, cuts, low, high):
    factor_of = 1.0
    for position, blocks in cuts:
        heights = jax.random.uniform(jax.random.fold_in(jax.random.fold_in(own_key, 6), position), (blocks,), jnp.float32, low / len(cuts), high / len(cuts))
        factor_of = factor_of * jnp.repeat(jnp.exp(heights), shape[position] // blocks).reshape((-1,) + (1,) * (len(shape) - 1 - position))
    return factor_of


def noise(key, dims, scale, reach, split=(), kind=jnp.bfloat16):
    drawn = scale * jax.random.normal(key, dims, jnp.float32)
    if split:
        drawn = drawn * level_of(key, dims, split, -0.22, 0.18)
    return jnp.clip(drawn, -reach, reach).astype(kind)


def setup_inputs(seed: int = 0) -> dict:
    seeds = jax.random.split(jax.random.key(seed), 6)
    return {
        "out_grad": noise(seeds[0], (TOKENS, DO), 1.0, 6.0, ((0, 64), (1, 8))),
        "out_weight": noise(seeds[1], (D, DO), D ** -0.5, 0.0625, ((0, 8), (1, 64))),
        "signal": noise(seeds[2], (TOKENS, D), 1.0, 6.0, ((0, 64), (1, 8))),
        "gate_input": noise(seeds[3], (TOKENS, D), 1.0, 6.0, ((0, 64), (1, 8))),
        "filter_taps": noise(seeds[4], (K, D), K ** -0.5, 0.5, ((1, 512),), jnp.float32),
    }


def sequence_grads(parts):
    sig, gate_part, mix, taps = parts
    size = 2 * LEN
    sig_freq = jnp.fft.rfft(sig.astype(jnp.float32), n=size, axis=1)
    tap_freq = jnp.fft.rfft(taps, n=size, axis=0)
    conv_out = jnp.fft.irfft(sig_freq * tap_freq[None], n=size, axis=1)[:, :LEN]
    mix_wide = mix.astype(jnp.float32)
    gate_part_grad = (mix_wide * conv_out).astype(jnp.bfloat16)
    conv_grad = (mix_wide * gate_part.astype(jnp.float32)).astype(jnp.bfloat16)
    grad_freq = jnp.fft.rfft(conv_grad.astype(jnp.float32), n=size, axis=1)
    sig_part_grad = jnp.fft.irfft(grad_freq * jnp.conj(tap_freq)[None], n=size, axis=1)[:, :LEN].astype(jnp.bfloat16)
    lagged = jnp.fft.irfft(grad_freq * jnp.conj(sig_freq), n=size, axis=1)[:, :K]
    tap_grads = jnp.sum(lagged, axis=0).astype(jnp.float32)
    return sig_part_grad, gate_part_grad, tap_grads


def reference(out_grad, out_weight, signal, gate_input, filter_taps):
    mixed = jnp.dot(out_grad, out_weight.T, preferred_element_type=jnp.float32).astype(jnp.bfloat16)
    groups = D // 128

    def split_groups(values):
        return values.reshape(SEQS, LEN, groups, 128).transpose(2, 0, 1, 3)

    def join_groups(values):
        return values.transpose(1, 2, 0, 3).reshape(TOKENS, D)

    taps = filter_taps.reshape(K, groups, 128).transpose(1, 0, 2)
    sig_grads, gate_grads, tap_grads = lax.map(sequence_grads, (split_groups(signal), split_groups(gate_input), split_groups(mixed), taps))
    return join_groups(sig_grads), join_groups(gate_grads), tap_grads.transpose(1, 0, 2).reshape(K, D)
```

```python
import jax
import jax.numpy as jnp
import numpy as np
from jax import lax
from jax.sharding import Mesh, PartitionSpec as P

K = 128
TOK = 256
SPAN = 8192
N = K + TOK
HALF = N // 2

BF = jnp.bfloat16
F32 = jnp.float32


def transforms():
    freq = 2.0 * np.pi * (np.arange(HALF) + 0.5) / N
    angle = freq[:, None] * np.arange(N + K)[None, :]
    forward = np.concatenate([np.cos(angle), -np.sin(angle)], axis=0)
    angle = angle[:, :N].T
    inverse = np.concatenate([np.cos(angle), -np.sin(angle)], axis=1) * (2.0 / N)
    return forward.astype(np.float32), inverse.astype(np.float32)


def two(values):
    values = np.asarray(values, np.float32)
    upper = values.astype(jnp.bfloat16)
    lower = (values - upper.astype(np.float32)).astype(jnp.bfloat16)
    return upper, lower


def split(values):
    upper = lax.optimization_barrier(values.astype(BF))
    return upper, (values - upper.astype(F32)).astype(BF)


def dot(a, b, dims=((1,), (0,))):
    return lax.dot_general(a, b, (dims, ((), ())), preferred_element_type=F32)


def exact_side(matrix, values, dims=((1,), (0,))):
    upper, lower = matrix
    return dot(upper, values, dims) + dot(lower, values, dims)


def both_sides(matrix, values, dims=((1,), (0,))):
    upper, lower = matrix
    high, low = split(values)
    return dot(upper, high, dims) + dot(lower, high, dims) + dot(upper, low, dims)


def times(a, b):
    ar, ai, br, bi = a[:HALF], a[HALF:], b[:HALF], b[HALF:]
    return jnp.concatenate([ar * br - ai * bi, ar * bi + ai * br], axis=0)


def times_conj(a, b):
    ar, ai, br, bi = a[:HALF], a[HALF:], b[:HALF], b[HALF:]
    return jnp.concatenate([ar * br + ai * bi, ai * br - ar * bi], axis=0)


def on_device(out_grad, out_weight, signal, gate_input, filter_taps):
    ctx = ("z", "h", "c")
    n_ctx = 64
    period = SPAN // TOK
    forward, inverse = transforms()
    fwd = two(forward)
    inv = two(inverse)

    turned = out_weight.T.reshape(64, 2, 512).transpose(1, 0, 2)
    tap_rows = filter_taps.T
    tap_high, tap_low = split(tap_rows)
    tap_pack = jnp.concatenate([tap_high, tap_low, jnp.zeros((16, 256), BF)], axis=1)
    message = jnp.concatenate([turned, jnp.broadcast_to(tap_pack[None], (2, 16, 512))], axis=1)
    got = lax.all_to_all(message, "h", split_axis=0, concat_axis=0)
    block = jnp.concatenate(
        [
            got[:, :64].reshape(128, 512),
            jnp.concatenate([got[0, 64:, :256], got[1, 64:, :256]], axis=1),
        ],
        axis=0,
    )
    gathered = lax.all_gather(block, "z", axis=0, tiled=False)

    ahead = [(i, i + 1) for i in range(n_ctx - 1) if (i + 1) % period]
    back = [(j, i) for i, j in ahead]
    sig_halo = lax.ppermute(signal[TOK - K :], ctx, ahead)

    cols = out_grad.reshape(TOK, 4, 2, 64).transpose(2, 0, 1, 3).reshape(2, TOK, 256)
    cols = lax.all_to_all(cols, "c", split_axis=0, concat_axis=0).reshape(2 * TOK, 256)
    cols = lax.all_to_all(
        jnp.broadcast_to(cols[None], (4, 2 * TOK, 256)), ("h", "l"), split_axis=0, concat_axis=0
    )
    cols = lax.all_to_all(
        jnp.broadcast_to(cols[None], (4, 4, 2 * TOK, 256)), "x", split_axis=0, concat_axis=0
    )
    cols = cols.reshape(4, 2, 2, 512, 256)

    window = jnp.concatenate([sig_halo, signal], axis=0)
    sig_freq = exact_side((fwd[0][:, :N], fwd[1][:, :N]), window)

    weights = gathered[:, :128].reshape(4, 2, 256, 512)
    partial = jnp.einsum("xhltf,xlfn->htn", cols, weights, preferred_element_type=F32)
    partial = lax.all_to_all(partial.reshape(2, 2, TOK, 512), "c", split_axis=1, concat_axis=1)
    half = (partial[:, 0] + partial[:, 1]).astype(BF)
    half = lax.all_to_all(half, "h", split_axis=0, concat_axis=0)
    mixed = jnp.concatenate([half[0], half[1]], axis=1)

    tap_part = gathered[:, 128:].reshape(16, 16, 2, 2, K)
    tap_all = lax.all_gather(tap_part, "c", axis=0)
    tap_all = tap_all.transpose(4, 1, 3, 0, 2, 5)
    tap_all = tap_all.reshape(2, 1024, K)
    head = (fwd[0][:, :K], fwd[1][:, :K])
    across = ((1,), (1,))
    tap_freq = (
        dot(head[0], tap_all[0], across)
        + dot(head[1], tap_all[0], across)
        + dot(head[0], tap_all[1], across)
    )
    own = (inv[0][K:], inv[1][K:])
    conv_out = both_sides(own, times(sig_freq, tap_freq))

    wide = mixed.astype(F32)
    gate_grad = (wide * conv_out).astype(BF)
    conv_grad = (wide * gate_input.astype(F32)).astype(BF)
    grad_halo = lax.ppermute(conv_grad[:K], ctx, back)

    own_freq = exact_side((fwd[0][:, K:N], fwd[1][:, K:N]), conv_grad)
    cross = times_conj(own_freq, sig_freq)
    lag = (inv[0][:K], inv[1][:K])
    high, low = split(cross)
    turn = ((0,), (1,))
    tap_grad = dot(high, lag[0], turn) + dot(high, lag[1], turn) + dot(low, lag[0], turn)
    tap_grad = tap_grad.astype(BF).reshape(16, 4, 16, K).transpose(1, 0, 2, 3)
    tap_grad = lax.all_to_all(tap_grad, ("h", "c"), split_axis=0, concat_axis=0)
    tap_grad = jnp.sum(tap_grad.astype(F32), axis=0).astype(BF)
    tap_grad = lax.all_to_all(tap_grad, "z", split_axis=0, concat_axis=0)
    filter_grad = jnp.sum(tap_grad.astype(F32), axis=0).T

    full_freq = own_freq + exact_side((fwd[0][:, N:], fwd[1][:, N:]), grad_halo)
    signal_grad = both_sides(own, times_conj(full_freq, tap_freq)).astype(BF)
    return signal_grad, gate_grad, filter_grad


def solution(mesh):
    fine = Mesh(mesh.devices.reshape(16, 2, 2, 4, 2), ("z", "h", "c", "x", "l"))
    ctx, tp = ("z", "h", "c"), ("x", "l")
    in_specs = (P(ctx, tp), P(tp, ctx), P(ctx, tp), P(ctx, tp), P(None, tp + ctx))
    out_specs = (P(ctx, tp), P(ctx, tp), P(None, tp + ctx))
    return jax.shard_map(
        on_device, mesh=fine, in_specs=in_specs, out_specs=out_specs, check_vma=False
    )
```

```python
import jax
import jax.numpy as jnp
import numpy as np
from jax import lax
from jax.experimental import pallas as pl
from jax.experimental.pallas import tpu as pltpu
from jax.sharding import Mesh, PartitionSpec as P

K = 128
TOK = 256
CH = 1024
SPAN = 8192
N = K + TOK
HALF = N // 2
TILE = 256

BF = jnp.bfloat16
F32 = jnp.float32
ROWS = ((1,), (0,))
LANES = ((1,), (1,))


def transforms():
    freq = 2.0 * np.pi * (np.arange(HALF) + 0.5) / N
    angle = freq[:, None] * np.arange(N + K)[None, :]
    forward = np.concatenate([np.cos(angle), -np.sin(angle)], axis=0)
    angle = angle[:, :N].T
    inverse = np.concatenate([np.cos(angle), -np.sin(angle)], axis=1) * (2.0 / N)
    return two(forward), two(inverse)


def two(values):
    values = np.asarray(values, np.float32)
    upper = values.astype(jnp.bfloat16)
    lower = (values - upper.astype(np.float32)).astype(jnp.bfloat16)
    return np.stack([upper, lower])


def dot(a, b, dims=ROWS):
    return lax.dot_general(a, b, (dims, ((), ())), preferred_element_type=F32)


def exact_side(matrix, values):
    return dot(matrix[0], values) + dot(matrix[1], values)


def both_sides(matrix, values):
    high = values.astype(BF)
    low = (values - high.astype(F32)).astype(BF)
    return dot(matrix[0], high) + dot(matrix[1], high) + dot(matrix[0], low)


def times(a, b):
    ar, ai, br, bi = a[:HALF], a[HALF:], b[:HALF], b[HALF:]
    return jnp.concatenate([ar * br - ai * bi, ar * bi + ai * br], axis=0)


def times_conj(a, b):
    ar, ai, br, bi = a[:HALF], a[HALF:], b[:HALF], b[HALF:]
    return jnp.concatenate([ar * br + ai * bi, ai * br - ar * bi], axis=0)


def params():
    return pltpu.CompilerParams(
        dimension_semantics=("arbitrary",), vmem_limit_bytes=40 * 1024 * 1024
    )


def product_kernel(cols_ref, weight_ref, out_ref):
    weight = weight_ref[:, :K, :].reshape(2 * K, 512)

    @pl.when(pl.program_id(0) == 0)
    def _():
        out_ref[...] = jnp.zeros_like(out_ref)

    for h in range(2):
        for c in range(2):
            out_ref[c, h] += dot(cols_ref[0, h, 0, c * TOK : (c + 1) * TOK, :], weight)


def product(cols, weights):
    return pl.pallas_call(
        product_kernel,
        grid=(8,),
        in_specs=[
            pl.BlockSpec((1, 2, 1, 512, 256), lambda i: (i // 2, 0, i % 2, 0, 0)),
            pl.BlockSpec((2, 144, 512), lambda i: (i, 0, 0)),
        ],
        out_specs=pl.BlockSpec((2, 2, TOK, 512), lambda i: (0, 0, 0, 0)),
        out_shape=jax.ShapeDtypeStruct((2, 2, TOK, 512), F32),
        compiler_params=params(),
        cost_estimate=pl.CostEstimate(
            flops=2 * 1024 * 2048 * 512, bytes_accessed=9 << 20, transcendentals=0
        ),
    )(cols, weights)


def grad_kernel(mix_ref, gate_ref, freq_ref, own_ref, lag_ref, head_ref, spec_ref, tap_ref):
    mixed = mix_ref[0].astype(F32)
    conv_grad = (mixed * gate_ref[...].astype(F32)).astype(BF)
    head_ref[...] = conv_grad[:K]
    spec = exact_side(own_ref, conv_grad)
    spec_ref[...] = spec
    taps = both_sides(lag_ref, times_conj(spec, freq_ref[...]))
    taps = taps.T.reshape(8, 2, 16, K)
    tap_ref[0] = taps[:, 0]
    tap_ref[1] = taps[:, 1]


def whole(shape):
    return pl.BlockSpec(shape, lambda j: (0,) * len(shape))


def tile(rows):
    return pl.BlockSpec((rows, TILE), lambda j: (0, j))


MIX_TILE = pl.BlockSpec((1, TOK, TILE), lambda j: (j // 2, 0, j % 2))


def grad_part(mix, gate, sig_freq, own, lag):
    return pl.pallas_call(
        grad_kernel,
        grid=(CH // TILE,),
        in_specs=[MIX_TILE, tile(TOK), tile(N), whole((2, N, TOK)), whole((2, K, N))],
        out_specs=[
            tile(K),
            tile(N),
            pl.BlockSpec((2, 8, 16, K), lambda j: (0, j, 0, 0)),
        ],
        out_shape=[
            jax.ShapeDtypeStruct((K, CH), BF),
            jax.ShapeDtypeStruct((N, CH), F32),
            jax.ShapeDtypeStruct((2, 32, 16, K), F32),
        ],
        compiler_params=params(),
        cost_estimate=pl.CostEstimate(
            flops=2 * CH * N * (2 * TOK + 3 * K), bytes_accessed=6 << 20, transcendentals=0
        ),
    )(mix, gate, sig_freq, own, lag)


def out_kernel(
    mix_ref, freq_ref, spec_ref, halo_ref, tap_ref, head_ref, tail_ref, inv_ref, gate_ref, sig_ref
):
    upper, lower = tap_ref[0], tap_ref[1]
    tap_freq = (
        dot(head_ref[0], upper, LANES)
        + dot(head_ref[1], upper, LANES)
        + dot(head_ref[0], lower, LANES)
    )
    conv_out = both_sides(inv_ref, times(freq_ref[...], tap_freq))
    gate_ref[...] = (mix_ref[0].astype(F32) * conv_out).astype(BF)
    full = spec_ref[...] + exact_side(tail_ref, halo_ref[...])
    sig_ref[...] = both_sides(inv_ref, times_conj(full, tap_freq)).astype(BF)


def out_part(mix, sig_freq, spec, halo, taps, head, tail, inv):
    return pl.pallas_call(
        out_kernel,
        grid=(CH // TILE,),
        in_specs=[
            MIX_TILE,
            tile(N),
            tile(N),
            tile(K),
            pl.BlockSpec((2, TILE, K), lambda j: (0, j, 0)),
            whole((2, N, K)),
            whole((2, N, K)),
            whole((2, TOK, N)),
        ],
        out_specs=[tile(TOK), tile(TOK)],
        out_shape=[jax.ShapeDtypeStruct((TOK, CH), BF)] * 2,
        compiler_params=params(),
        cost_estimate=pl.CostEstimate(
            flops=2 * CH * N * (5 * K + 6 * TOK), bytes_accessed=6 << 20, transcendentals=0
        ),
    )(mix, sig_freq, spec, halo, taps, head, tail, inv)


def on_device(out_grad, out_weight, signal, gate_input, filter_taps):
    ctx = ("z", "h", "c")
    n_ctx = 64
    period = SPAN // TOK
    fwd, inv = transforms()

    turned = out_weight.T.reshape(64, 2, 512).transpose(1, 0, 2)
    tap_rows = filter_taps.T
    tap_high = lax.optimization_barrier(tap_rows.astype(BF))
    tap_low = (tap_rows - tap_high.astype(F32)).astype(BF)
    tap_pack = jnp.concatenate([tap_high, tap_low, jnp.zeros((16, 256), BF)], axis=1)
    message = jnp.concatenate([turned, jnp.broadcast_to(tap_pack[None], (2, 16, 512))], axis=1)
    got = lax.all_to_all(message, "h", split_axis=0, concat_axis=0)
    block = jnp.concatenate(
        [
            got[:, :64].reshape(128, 512),
            jnp.concatenate([got[0, 64:, :256], got[1, 64:, :256]], axis=1),
        ],
        axis=0,
    )
    gathered = lax.all_gather(block, "z", axis=0, tiled=False)

    ahead = [(i, i + 1) for i in range(n_ctx - 1) if (i + 1) % period]
    back = [(j, i) for i, j in ahead]
    sig_halo = lax.ppermute(signal[TOK - K :], ctx, ahead)

    cols = out_grad.reshape(TOK, 4, 2, 64).transpose(2, 0, 1, 3).reshape(2, TOK, 256)
    cols = lax.all_to_all(cols, "c", split_axis=0, concat_axis=0).reshape(2 * TOK, 256)
    cols = lax.all_to_all(
        jnp.broadcast_to(cols[None], (4, 2 * TOK, 256)), ("h", "l"), split_axis=0, concat_axis=0
    )
    cols = lax.all_to_all(
        jnp.broadcast_to(cols[None], (4, 4, 2 * TOK, 256)), "x", split_axis=0, concat_axis=0
    )
    cols = cols.reshape(4, 2, 2, 512, 256)

    window = jnp.concatenate([sig_halo, signal], axis=0)
    sig_freq = exact_side(fwd[:, :, :N], window)

    partial = product(cols, gathered)
    partial = lax.all_to_all(partial, "c", split_axis=0, concat_axis=0)
    half = (partial[0] + partial[1]).astype(BF)
    half = lax.all_to_all(half, "h", split_axis=0, concat_axis=0)

    grad_head, spec, tap_grad = grad_part(
        half, gate_input, sig_freq, fwd[:, :, K:N], inv[:, :K]
    )
    grad_halo = lax.ppermute(grad_head, ctx, back)
    tap_grad = lax.all_to_all(tap_grad, "c", split_axis=0, concat_axis=0)
    tap_grad = (tap_grad[0] + tap_grad[1]).astype(BF)
    tap_grad = lax.all_to_all(tap_grad, ("z", "h"), split_axis=0, concat_axis=0)
    filter_grad = jnp.sum(tap_grad.astype(F32), axis=0).T

    tap_part, _ = lax.optimization_barrier((gathered[:, 128:], half))
    tap_all = lax.all_gather(tap_part.reshape(16, 16, 2, 2, K), "c", axis=0)
    tap_all = tap_all.transpose(4, 1, 3, 0, 2, 5).reshape(2, CH, K)
    gate_grad, signal_grad = out_part(
        half, sig_freq, spec, grad_halo, tap_all, fwd[:, :, :K], fwd[:, :, N:], inv[:, K:]
    )
    return signal_grad, gate_grad, filter_grad


def solution(mesh):
    fine = Mesh(mesh.devices.reshape(16, 2, 2, 4, 2), ("z", "h", "c", "x", "l"))
    ctx, tp = ("z", "h", "c"), ("x", "l")
    in_specs = (P(ctx, tp), P(tp, ctx), P(ctx, tp), P(ctx, tp), P(None, tp + ctx))
    out_specs = (P(ctx, tp), P(ctx, tp), P(None, tp + ctx))
    return jax.shard_map(
        on_device, mesh=fine, in_specs=in_specs, out_specs=out_specs, check_vma=False
    )
```

```python
import jax
import jax.numpy as jnp
import numpy as np
from jax import lax
from jax.experimental import pallas as pl
from jax.experimental.pallas import tpu as pltpu
from jax.sharding import Mesh, PartitionSpec as P

K = 128
TOK = 256
CH = 1024
SPAN = 8192
N = K + TOK
HALF = N // 2
TILE = 256

BF = jnp.bfloat16
F32 = jnp.float32
ROWS = ((1,), (0,))
LANES = ((1,), (1,))


def transforms():
    freq = 2.0 * np.pi * (np.arange(HALF) + 0.5) / N
    angle = freq[:, None] * np.arange(N + K)[None, :]
    forward = np.concatenate([np.cos(angle), -np.sin(angle)], axis=0)
    angle = angle[:, :N].T
    inverse = np.concatenate([np.cos(angle), -np.sin(angle)], axis=1) * (2.0 / N)
    return two(forward), two(inverse)


def two(values):
    values = np.asarray(values, np.float32)
    upper = values.astype(jnp.bfloat16)
    lower = (values - upper.astype(np.float32)).astype(jnp.bfloat16)
    return np.stack([upper, lower])


def dot(a, b, dims=ROWS):
    return lax.dot_general(a, b, (dims, ((), ())), preferred_element_type=F32)


def exact_side(matrix, values):
    return dot(matrix[0], values) + dot(matrix[1], values)


def both_sides(matrix, values):
    high = values.astype(BF)
    low = (values - high.astype(F32)).astype(BF)
    return dot(matrix[0], high) + dot(matrix[1], high) + dot(matrix[0], low)


def times(a, b):
    ar, ai, br, bi = a[:HALF], a[HALF:], b[:HALF], b[HALF:]
    return jnp.concatenate([ar * br - ai * bi, ar * bi + ai * br], axis=0)


def times_conj(a, b):
    ar, ai, br, bi = a[:HALF], a[HALF:], b[:HALF], b[HALF:]
    return jnp.concatenate([ar * br + ai * bi, ai * br - ar * bi], axis=0)


def params():
    return pltpu.CompilerParams(
        dimension_semantics=("arbitrary",), vmem_limit_bytes=40 * 1024 * 1024
    )


def product_kernel(core_ref, own_ref, other_ref, weight_ref, out_ref):
    weight = weight_ref[...].reshape(8 * K, 512)

    def run(source):
        rows = jnp.concatenate([source[i, 0] for i in range(8)], axis=1)
        out_ref[0, 0] = dot(rows, weight).astype(BF)

    @pl.when(pl.program_id(0) == 0)
    def _():
        run(own_ref)

    @pl.when(pl.program_id(0) == 1)
    def _():
        run(other_ref)


def product(core, own, other, weights):
    def place(i, j, core_ref):
        return (j, jnp.where(i == 0, core_ref[0], 1 - core_ref[0]), 0, 0)

    return pl.pallas_call(
        product_kernel,
        grid_spec=pltpu.PrefetchScalarGridSpec(
            num_scalar_prefetch=1,
            grid=(2, 4),
            in_specs=[
                pl.BlockSpec((8, 1, TOK, K), lambda i, j, s: (0, jnp.where(i == 0, j, 3), 0, 0)),
                pl.BlockSpec((8, 1, TOK, K), lambda i, j, s: (0, jnp.where(i == 1, j, 0), 0, 0)),
                pl.BlockSpec((8, K, 512), lambda i, j, s: (0, 0, 0)),
            ],
            out_specs=pl.BlockSpec((1, 1, TOK, 512), place),
        ),
        out_shape=jax.ShapeDtypeStruct((4, 2, TOK, 512), BF),
        compiler_params=pltpu.CompilerParams(
            dimension_semantics=("arbitrary", "arbitrary"), vmem_limit_bytes=40 * 1024 * 1024
        ),
        cost_estimate=pl.CostEstimate(
            flops=2 * 2048 * 1024 * 512, bytes_accessed=7 << 20, transcendentals=0
        ),
    )(core, own, other, weights)


def whole(shape):
    return pl.BlockSpec(shape, lambda j: (0,) * len(shape))


def tile(rows):
    return pl.BlockSpec((rows, TILE), lambda j: (0, j))


def front_kernel(window_ref, tap_ref, forward_ref, inv_ref, freq_ref, tap_freq_ref, conv_ref):
    upper, lower = tap_ref[0], tap_ref[1]
    high, low = forward_ref[0, :, :K], forward_ref[1, :, :K]
    tap_freq = dot(high, upper, LANES) + dot(low, upper, LANES) + dot(high, lower, LANES)
    tap_freq_ref[...] = tap_freq
    freq = exact_side(forward_ref, window_ref[...])
    freq_ref[...] = freq
    conv_ref[...] = both_sides(inv_ref, times(freq, tap_freq))


def front_part(window, taps, forward, inv):
    return pl.pallas_call(
        front_kernel,
        grid=(CH // TILE,),
        in_specs=[
            tile(N),
            pl.BlockSpec((2, TILE, K), lambda j: (0, j, 0)),
            whole((2, N, N)),
            whole((2, TOK, N)),
        ],
        out_specs=[tile(N), tile(N), tile(TOK)],
        out_shape=[
            jax.ShapeDtypeStruct((N, CH), F32),
            jax.ShapeDtypeStruct((N, CH), F32),
            jax.ShapeDtypeStruct((TOK, CH), F32),
        ],
        compiler_params=params(),
        cost_estimate=pl.CostEstimate(
            flops=2 * CH * N * (3 * K + 2 * N + 3 * TOK), bytes_accessed=8 << 20, transcendentals=0
        ),
    )(window, taps, forward, inv)


def grad_kernel(
    mix_ref,
    gate_ref,
    conv_ref,
    freq_ref,
    own_ref,
    lag_ref,
    gate_grad_ref,
    head_ref,
    spec_ref,
    tap_ref,
):
    parts = mix_ref[:, 0].astype(F32)
    mixed = (parts[0] + parts[1] + (parts[2] + parts[3])).astype(BF).astype(F32)
    gate_grad_ref[...] = (mixed * conv_ref[...]).astype(BF)
    conv_grad = (mixed * gate_ref[...].astype(F32)).astype(BF)
    head_ref[...] = conv_grad[:K]
    spec = exact_side(own_ref, conv_grad)
    spec_ref[...] = spec
    taps = both_sides(lag_ref, times_conj(spec, freq_ref[...]))
    taps = taps.T.reshape(8, 2, 16, K)
    tap_ref[0] = taps[:, 0]
    tap_ref[1] = taps[:, 1]


def grad_part(mix, gate, conv, sig_freq, own, lag):
    return pl.pallas_call(
        grad_kernel,
        grid=(CH // TILE,),
        in_specs=[
            pl.BlockSpec((4, 1, TOK, TILE), lambda j: (0, j // 2, 0, j % 2)),
            tile(TOK),
            tile(TOK),
            tile(N),
            whole((2, N, TOK)),
            whole((2, K, N)),
        ],
        out_specs=[
            tile(TOK),
            tile(K),
            tile(N),
            pl.BlockSpec((2, 8, 16, K), lambda j: (0, j, 0, 0)),
        ],
        out_shape=[
            jax.ShapeDtypeStruct((TOK, CH), BF),
            jax.ShapeDtypeStruct((K, CH), BF),
            jax.ShapeDtypeStruct((N, CH), F32),
            jax.ShapeDtypeStruct((2, 32, 16, K), F32),
        ],
        compiler_params=params(),
        cost_estimate=pl.CostEstimate(
            flops=2 * CH * N * (2 * TOK + 3 * K), bytes_accessed=9 << 20, transcendentals=0
        ),
    )(mix, gate, conv, sig_freq, own, lag)


def out_kernel(spec_ref, halo_ref, tap_ref, tail_ref, inv_ref, sig_ref):
    full = spec_ref[...] + exact_side(tail_ref, halo_ref[...])
    sig_ref[...] = both_sides(inv_ref, times_conj(full, tap_ref[...])).astype(BF)


def out_part(spec, halo, tap_freq, tail, inv):
    return pl.pallas_call(
        out_kernel,
        grid=(CH // TILE,),
        in_specs=[tile(N), tile(K), tile(N), whole((2, N, K)), whole((2, TOK, N))],
        out_specs=tile(TOK),
        out_shape=jax.ShapeDtypeStruct((TOK, CH), BF),
        compiler_params=params(),
        cost_estimate=pl.CostEstimate(
            flops=2 * CH * N * (2 * K + 3 * TOK), bytes_accessed=5 << 20, transcendentals=0
        ),
    )(spec, halo, tap_freq, tail, inv)


def on_device(out_grad, out_weight, signal, gate_input, filter_taps):
    ctx = ("m", "p", "h", "c")
    n_ctx = 64
    period = SPAN // TOK
    fwd, inv = transforms()
    core = lax.axis_index("c")

    turned = out_weight.T.reshape(64, 2, 512).transpose(1, 0, 2)
    turned = lax.all_to_all(turned, "c", split_axis=0, concat_axis=0).reshape(K, 512)

    tap_rows = filter_taps.T
    tap_high = lax.optimization_barrier(tap_rows.astype(BF))
    tap_low = (tap_rows - tap_high.astype(F32)).astype(BF)
    tap_pack = jnp.concatenate([tap_high, tap_low], axis=0)
    cols = out_grad.reshape(TOK, 4, K).transpose(1, 0, 2)
    cols = jnp.concatenate([cols, jnp.broadcast_to(tap_pack[None], (4, 32, K))], axis=1)
    turned, cols = lax.optimization_barrier((turned, cols))
    weights = lax.all_gather(turned, "m", axis=0, tiled=False)
    cols = lax.all_to_all(cols, ("p", "h"), split_axis=0, concat_axis=0)
    tap_part = cols[:, TOK:]
    cols = lax.all_gather(cols[:, :TOK], "l", axis=0, tiled=False)
    cols = lax.all_to_all(
        jnp.broadcast_to(cols[None], (4, 2, 4, TOK, K)), "x", split_axis=0, concat_axis=0
    ).reshape(8, 4, TOK, K)
    cols_other = lax.ppermute(cols, "c", [(0, 1), (1, 0)])

    ahead = [(i, i + 1) for i in range(n_ctx - 1) if (i + 1) % period]
    back = [(j, i) for i, j in ahead]
    sig_halo = lax.ppermute(signal[TOK - K :], ctx, ahead)
    window = jnp.concatenate([sig_halo, signal], axis=0)
    taps = lax.all_gather(tap_part, "m", axis=0, tiled=False)
    taps = lax.all_gather(taps, "c", axis=0, tiled=False)
    taps = taps.reshape(2, 8, 4, 2, 16, K).transpose(3, 1, 2, 0, 4, 5).reshape(2, CH, K)
    sig_freq, tap_freq, conv = front_part(window, taps, fwd[:, :, :N], inv[:, K:])

    partial = product(core.reshape(1), cols, cols_other, weights)
    mix = lax.all_to_all(
        partial.reshape(8, TOK, 512), ("p", "h", "c"), split_axis=0, concat_axis=0
    ).reshape(4, 2, TOK, 512)

    gate_grad, grad_head, spec, tap_grad = grad_part(
        mix, gate_input, conv, sig_freq, fwd[:, :, K:N], inv[:, :K]
    )
    grad_halo = lax.ppermute(grad_head, ctx, back)
    tap_grad = lax.all_to_all(tap_grad, "c", split_axis=0, concat_axis=0)
    tap_grad = (tap_grad[0] + tap_grad[1]).astype(BF)
    tap_grad = lax.all_to_all(tap_grad, ("m", "p", "h"), split_axis=0, concat_axis=0)
    filter_grad = jnp.sum(tap_grad.astype(F32), axis=0).T

    signal_grad = out_part(spec, grad_halo, tap_freq, fwd[:, :, N:], inv[:, K:])
    return signal_grad, gate_grad, filter_grad


def solution(mesh):
    fine = Mesh(mesh.devices.reshape(8, 2, 2, 2, 4, 2), ("m", "p", "h", "c", "x", "l"))
    ctx, tp = ("m", "p", "h", "c"), ("x", "l")
    in_specs = (P(ctx, tp), P(tp, ctx), P(ctx, tp), P(ctx, tp), P(None, tp + ctx))
    out_specs = (P(ctx, tp), P(ctx, tp), P(None, tp + ctx))
    return jax.shard_map(
        on_device, mesh=fine, in_specs=in_specs, out_specs=out_specs, check_vma=False
    )
```

```python
import jax
import jax.numpy as jnp
import numpy as np
from jax import lax
from jax.experimental import pallas as pl
from jax.experimental.pallas import tpu as pltpu
from jax.sharding import Mesh, PartitionSpec as P

K = 128
TOK = 256
CH = 1024
SPAN = 8192
N = K + TOK
HALF = N // 2
TILE = 256
VMEM = 56 * 1024 * 1024

BF = jnp.bfloat16
F32 = jnp.float32
ROWS = ((1,), (0,))
LANES = ((1,), (1,))


def transforms():
    freq = 2.0 * np.pi * (np.arange(HALF) + 0.5) / N
    angle = freq[:, None] * np.arange(N + K)[None, :]
    forward = np.concatenate([np.cos(angle), -np.sin(angle)], axis=0)
    angle = angle[:, :N].T
    inverse = np.concatenate([np.cos(angle), -np.sin(angle)], axis=1) * (2.0 / N)
    return two(forward), two(inverse)


def two(values):
    values = np.asarray(values, np.float32)
    upper = values.astype(jnp.bfloat16)
    lower = (values - upper.astype(np.float32)).astype(jnp.bfloat16)
    return np.stack([upper, lower])


def dot(a, b, dims=ROWS):
    return lax.dot_general(a, b, (dims, ((), ())), preferred_element_type=F32)


def exact_side(matrix, values):
    return dot(matrix[0], values) + dot(matrix[1], values)


def both_sides(matrix, values):
    high = values.astype(BF)
    low = (values - high.astype(F32)).astype(BF)
    return dot(matrix[0], high) + dot(matrix[1], high) + dot(matrix[0], low)


def times(a, b):
    ar, ai, br, bi = a[:HALF], a[HALF:], b[:HALF], b[HALF:]
    return jnp.concatenate([ar * br - ai * bi, ar * bi + ai * br], axis=0)


def times_conj(a, b):
    ar, ai, br, bi = a[:HALF], a[HALF:], b[:HALF], b[HALF:]
    return jnp.concatenate([ar * br + ai * bi, ai * br - ar * bi], axis=0)


def params():
    return pltpu.CompilerParams(
        dimension_semantics=("arbitrary",), vmem_limit_bytes=VMEM
    )


def product_kernel(cols_ref, weight_ref, out_ref):
    weight = weight_ref[:, :K].reshape(8 * K, 512)
    rows = jnp.concatenate([cols_ref[0, i, 0] for i in range(8)], axis=1)
    out_ref[0] = dot(rows, weight).astype(BF)


def product(cols, weights):
    return pl.pallas_call(
        product_kernel,
        grid=(8,),
        in_specs=[
            pl.BlockSpec((1, 8, 1, TOK, K), lambda i: (i % 2, 0, i // 2, 0, 0)),
            pl.BlockSpec((8, K + 16, 512), lambda i: (0, 0, 0)),
        ],
        out_specs=pl.BlockSpec((1, TOK, 512), lambda i: (i, 0, 0)),
        out_shape=jax.ShapeDtypeStruct((8, TOK, 512), BF),
        compiler_params=params(),
        cost_estimate=pl.CostEstimate(
            flops=2 * 2048 * 1024 * 512, bytes_accessed=7 << 20, transcendentals=0
        ),
    )(cols, weights)


def whole(shape):
    return pl.BlockSpec(shape, lambda j: (0,) * len(shape))


def tile(rows):
    return pl.BlockSpec((rows, TILE), lambda j: (0, j))


def front_kernel(window_ref, forward_ref, freq_ref):
    freq_ref[...] = exact_side(forward_ref, window_ref[...])


def front_part(window, forward):
    return pl.pallas_call(
        front_kernel,
        grid=(CH // TILE,),
        in_specs=[tile(N), whole((2, N, N))],
        out_specs=tile(N),
        out_shape=jax.ShapeDtypeStruct((N, CH), F32),
        compiler_params=params(),
        cost_estimate=pl.CostEstimate(
            flops=2 * CH * N * 2 * N, bytes_accessed=3 << 20, transcendentals=0
        ),
    )(window, forward)


def grad_kernel(
    mix_ref, gate_ref, freq_ref, own_ref, lag_ref, mixed_ref, head_ref, spec_ref, tap_ref
):
    parts = mix_ref[:, 0].astype(F32)
    mixed = (parts[0] + parts[1] + (parts[2] + parts[3])).astype(BF)
    mixed_ref[...] = mixed
    conv_grad = (mixed.astype(F32) * gate_ref[...].astype(F32)).astype(BF)
    head_ref[...] = conv_grad[:K]
    spec = exact_side(own_ref, conv_grad)
    spec_ref[...] = spec
    taps = both_sides(lag_ref, times_conj(spec, freq_ref[...]))
    taps = taps.T.reshape(8, 2, 16, K)
    tap_ref[0] = taps[:, 0]
    tap_ref[1] = taps[:, 1]


def grad_part(mix, gate, sig_freq, own, lag):
    return pl.pallas_call(
        grad_kernel,
        grid=(CH // TILE,),
        in_specs=[
            pl.BlockSpec((4, 1, TOK, TILE), lambda j: (0, j // 2, 0, j % 2)),
            tile(TOK),
            tile(N),
            whole((2, N, TOK)),
            whole((2, K, N)),
        ],
        out_specs=[
            tile(TOK),
            tile(K),
            tile(N),
            pl.BlockSpec((2, 8, 16, K), lambda j: (0, j, 0, 0)),
        ],
        out_shape=[
            jax.ShapeDtypeStruct((TOK, CH), BF),
            jax.ShapeDtypeStruct((K, CH), BF),
            jax.ShapeDtypeStruct((N, CH), F32),
            jax.ShapeDtypeStruct((2, 32, 16, K), F32),
        ],
        compiler_params=params(),
        cost_estimate=pl.CostEstimate(
            flops=2 * CH * N * (2 * TOK + 3 * K), bytes_accessed=8 << 20, transcendentals=0
        ),
    )(mix, gate, sig_freq, own, lag)


def out_kernel(
    mixed_ref, freq_ref, spec_ref, halo_ref, tap_ref, head_ref, tail_ref, inv_ref, gate_ref, sig_ref
):
    upper, lower = tap_ref[0], tap_ref[1]
    high, low = head_ref[0], head_ref[1]
    tap_freq = dot(high, upper, LANES) + dot(low, upper, LANES) + dot(high, lower, LANES)
    conv_out = both_sides(inv_ref, times(freq_ref[...], tap_freq))
    gate_ref[...] = (mixed_ref[...].astype(F32) * conv_out).astype(BF)
    full = spec_ref[...] + exact_side(tail_ref, halo_ref[...])
    sig_ref[...] = both_sides(inv_ref, times_conj(full, tap_freq)).astype(BF)


def out_part(mixed, sig_freq, spec, halo, taps, head, tail, inv):
    return pl.pallas_call(
        out_kernel,
        grid=(CH // TILE,),
        in_specs=[
            tile(TOK),
            tile(N),
            tile(N),
            tile(K),
            pl.BlockSpec((2, TILE, K), lambda j: (0, j, 0)),
            whole((2, N, K)),
            whole((2, N, K)),
            whole((2, TOK, N)),
        ],
        out_specs=[tile(TOK), tile(TOK)],
        out_shape=[jax.ShapeDtypeStruct((TOK, CH), BF)] * 2,
        compiler_params=params(),
        cost_estimate=pl.CostEstimate(
            flops=2 * CH * N * (5 * K + 6 * TOK), bytes_accessed=6 << 20, transcendentals=0
        ),
    )(mixed, sig_freq, spec, halo, taps, head, tail, inv)


def with_partner(values, axis):
    other = lax.ppermute(values, axis, [(0, 1), (1, 0)])
    first = lax.axis_index(axis) == 0
    return jnp.stack([jnp.where(first, values, other), jnp.where(first, other, values)])


def on_device(out_grad, out_weight, signal, gate_input, filter_taps):
    ctx = ("m", "p", "h", "c")
    n_ctx = 64
    period = SPAN // TOK
    fwd, inv = transforms()

    turned = out_weight.T.reshape(64, 2, 512).transpose(1, 0, 2)
    turned = lax.all_to_all(turned, "c", split_axis=0, concat_axis=0).reshape(K, 512)
    tap_rows = filter_taps.T
    tap_high = lax.optimization_barrier(tap_rows.astype(BF))
    tap_low = (tap_rows - tap_high.astype(F32)).astype(BF)
    tap_pack = jnp.concatenate([tap_high, tap_low, jnp.zeros((16, 256), BF)], axis=1)
    block = jnp.concatenate([turned, tap_pack], axis=0)

    cols = out_grad.reshape(TOK, 4, K).transpose(1, 0, 2)
    block, cols = lax.optimization_barrier((block, cols))
    weights = lax.all_gather(block, "m", axis=0, tiled=False)
    cols = lax.all_to_all(cols, ("p", "h"), split_axis=0, concat_axis=0)

    ahead = [(i, i + 1) for i in range(n_ctx - 1) if (i + 1) % period]
    back = [(j, i) for i, j in ahead]
    sig_halo = lax.ppermute(signal[TOK - K :], ctx, ahead)
    window = jnp.concatenate([sig_halo, signal], axis=0)
    sig_freq = front_part(window, fwd[:, :, :N])

    cols, sig_freq = lax.optimization_barrier((cols, sig_freq))
    cols = lax.all_to_all(
        jnp.broadcast_to(cols[None], (8, 4, TOK, K)), ("x", "l"), split_axis=0, concat_axis=0
    )
    cols = lax.all_to_all(
        jnp.broadcast_to(cols[None], (2, 8, 4, TOK, K)), "c", split_axis=0, concat_axis=0
    )

    partial = product(cols, weights)
    weights, partial = lax.optimization_barrier((weights, partial))
    mix = lax.all_to_all(
        partial, ("p", "h", "c"), split_axis=0, concat_axis=0
    ).reshape(4, 2, TOK, 512)

    mixed, grad_head, spec, tap_grad = grad_part(
        mix, gate_input, sig_freq, fwd[:, :, K:N], inv[:, :K]
    )
    grad_halo = lax.ppermute(grad_head, ctx, back)
    tap_grad = lax.all_to_all(tap_grad, "c", split_axis=0, concat_axis=0)
    tap_grad = (tap_grad[0] + tap_grad[1]).astype(BF)
    tap_grad = lax.all_to_all(tap_grad, ("m", "p", "h"), split_axis=0, concat_axis=0)
    filter_grad = jnp.sum(tap_grad.astype(F32), axis=0).T

    taps = weights[:, K:, : 2 * K].reshape(8, 16, 2, K).transpose(2, 0, 1, 3)
    taps = with_partner(with_partner(with_partner(taps, "p"), "h"), "c")
    taps = taps.transpose(3, 4, 2, 1, 0, 5, 6).reshape(2, CH, K)
    gate_grad, signal_grad = out_part(
        mixed, sig_freq, spec, grad_halo, taps, fwd[:, :, :K], fwd[:, :, N:], inv[:, K:]
    )
    return signal_grad, gate_grad, filter_grad


def solution(mesh):
    fine = Mesh(mesh.devices.reshape(8, 2, 2, 2, 4, 2), ("m", "p", "h", "c", "x", "l"))
    ctx, tp = ("m", "p", "h", "c"), ("x", "l")
    in_specs = (P(ctx, tp), P(tp, ctx), P(ctx, tp), P(ctx, tp), P(None, tp + ctx))
    out_specs = (P(ctx, tp), P(ctx, tp), P(None, tp + ctx))
    return jax.shard_map(
        on_device, mesh=fine, in_specs=in_specs, out_specs=out_specs, check_vma=False
    )
```

```python
import jax
import jax.numpy as jnp
import numpy as np
from jax import lax
from jax.experimental import pallas as pl
from jax.experimental.pallas import tpu as pltpu
from jax.sharding import Mesh, PartitionSpec as P

K = 128
TOK = 256
CH = 1024
SPAN = 8192
N = K + TOK
HALF = N // 2
TILE = 256
VMEM = 56 * 1024 * 1024

BF = jnp.bfloat16
F32 = jnp.float32
ROWS = ((1,), (0,))
LANES = ((1,), (1,))


def transforms():
    freq = 2.0 * np.pi * (np.arange(HALF) + 0.5) / N
    angle = freq[:, None] * np.arange(N + K)[None, :]
    forward = np.concatenate([np.cos(angle), -np.sin(angle)], axis=0)
    angle = angle[:, :N].T
    inverse = np.concatenate([np.cos(angle), -np.sin(angle)], axis=1) * (2.0 / N)
    return two(forward), two(inverse)


def two(values):
    values = np.asarray(values, np.float32)
    upper = values.astype(jnp.bfloat16)
    lower = (values - upper.astype(np.float32)).astype(jnp.bfloat16)
    return np.stack([upper, lower])


def dot(a, b, dims=ROWS):
    return lax.dot_general(a, b, (dims, ((), ())), preferred_element_type=F32)


def exact_side(matrix, values):
    return dot(matrix[0], values) + dot(matrix[1], values)


def both_sides(matrix, values):
    high = values.astype(BF)
    low = (values - high.astype(F32)).astype(BF)
    return dot(matrix[0], high) + dot(matrix[1], high) + dot(matrix[0], low)


def times(a, b):
    ar, ai, br, bi = a[:HALF], a[HALF:], b[:HALF], b[HALF:]
    return jnp.concatenate([ar * br - ai * bi, ar * bi + ai * br], axis=0)


def times_conj(a, b):
    ar, ai, br, bi = a[:HALF], a[HALF:], b[:HALF], b[HALF:]
    return jnp.concatenate([ar * br + ai * bi, ai * br - ar * bi], axis=0)


def params():
    return pltpu.CompilerParams(
        dimension_semantics=("arbitrary",), vmem_limit_bytes=VMEM
    )


def product_kernel(cols_ref, weight_ref, out_ref):
    weight = weight_ref[:, :K].reshape(16 * K, 512)
    rows = jnp.concatenate([cols_ref[0, i, 0, j] for i in range(8) for j in range(2)], axis=1)
    out_ref[0] = dot(rows, weight).astype(BF)


def product(cols, weights):
    return pl.pallas_call(
        product_kernel,
        grid=(4,),
        in_specs=[
            pl.BlockSpec((1, 8, 1, 2, TOK, K), lambda i: (i % 2, 0, i // 2, 0, 0, 0)),
            pl.BlockSpec((16, K + 16, 512), lambda i: (0, 0, 0)),
        ],
        out_specs=pl.BlockSpec((1, TOK, 512), lambda i: (i, 0, 0)),
        out_shape=jax.ShapeDtypeStruct((4, TOK, 512), BF),
        compiler_params=params(),
        cost_estimate=pl.CostEstimate(
            flops=2 * 1024 * 2048 * 512, bytes_accessed=8 << 20, transcendentals=0
        ),
    )(cols, weights)


def whole(shape):
    return pl.BlockSpec(shape, lambda j: (0,) * len(shape))


def tile(rows):
    return pl.BlockSpec((rows, TILE), lambda j: (0, j))


def front_kernel(window_ref, forward_ref, freq_ref):
    freq_ref[...] = exact_side(forward_ref, window_ref[...])


def front_part(window, forward):
    return pl.pallas_call(
        front_kernel,
        grid=(CH // TILE,),
        in_specs=[tile(N), whole((2, N, N))],
        out_specs=tile(N),
        out_shape=jax.ShapeDtypeStruct((N, CH), F32),
        compiler_params=params(),
        cost_estimate=pl.CostEstimate(
            flops=2 * CH * N * 2 * N, bytes_accessed=3 << 20, transcendentals=0
        ),
    )(window, forward)


def grad_kernel(
    mix_ref, gate_ref, freq_ref, own_ref, lag_ref, mixed_ref, head_ref, spec_ref, tap_ref
):
    mixed = (mix_ref[0, 0].astype(F32) + mix_ref[1, 0].astype(F32)).astype(BF)
    mixed_ref[...] = mixed
    conv_grad = (mixed.astype(F32) * gate_ref[...].astype(F32)).astype(BF)
    head_ref[...] = conv_grad[:K]
    spec = exact_side(own_ref, conv_grad)
    spec_ref[...] = spec
    taps = both_sides(lag_ref, times_conj(spec, freq_ref[...]))
    taps = taps.T.reshape(8, 2, 16, K)
    tap_ref[0] = taps[:, 0]
    tap_ref[1] = taps[:, 1]


def grad_part(mix, gate, sig_freq, own, lag):
    return pl.pallas_call(
        grad_kernel,
        grid=(CH // TILE,),
        in_specs=[
            pl.BlockSpec((2, 1, TOK, TILE), lambda j: (0, j // 2, 0, j % 2)),
            tile(TOK),
            tile(N),
            whole((2, N, TOK)),
            whole((2, K, N)),
        ],
        out_specs=[
            tile(TOK),
            tile(K),
            tile(N),
            pl.BlockSpec((2, 8, 16, K), lambda j: (0, j, 0, 0)),
        ],
        out_shape=[
            jax.ShapeDtypeStruct((TOK, CH), BF),
            jax.ShapeDtypeStruct((K, CH), BF),
            jax.ShapeDtypeStruct((N, CH), F32),
            jax.ShapeDtypeStruct((2, 32, 16, K), F32),
        ],
        compiler_params=params(),
        cost_estimate=pl.CostEstimate(
            flops=2 * CH * N * (2 * TOK + 3 * K), bytes_accessed=8 << 20, transcendentals=0
        ),
    )(mix, gate, sig_freq, own, lag)


def out_kernel(
    mixed_ref, freq_ref, spec_ref, halo_ref, tap_ref, head_ref, tail_ref, inv_ref, gate_ref, sig_ref
):
    upper, lower = tap_ref[0], tap_ref[1]
    high, low = head_ref[0], head_ref[1]
    tap_freq = dot(high, upper, LANES) + dot(low, upper, LANES) + dot(high, lower, LANES)
    conv_out = both_sides(inv_ref, times(freq_ref[...], tap_freq))
    gate_ref[...] = (mixed_ref[...].astype(F32) * conv_out).astype(BF)
    full = spec_ref[...] + exact_side(tail_ref, halo_ref[...])
    sig_ref[...] = both_sides(inv_ref, times_conj(full, tap_freq)).astype(BF)


def out_part(mixed, sig_freq, spec, halo, taps, head, tail, inv):
    return pl.pallas_call(
        out_kernel,
        grid=(CH // TILE,),
        in_specs=[
            tile(TOK),
            tile(N),
            tile(N),
            tile(K),
            pl.BlockSpec((2, TILE, K), lambda j: (0, j, 0)),
            whole((2, N, K)),
            whole((2, N, K)),
            whole((2, TOK, N)),
        ],
        out_specs=[tile(TOK), tile(TOK)],
        out_shape=[jax.ShapeDtypeStruct((TOK, CH), BF)] * 2,
        compiler_params=params(),
        cost_estimate=pl.CostEstimate(
            flops=2 * CH * N * (5 * K + 6 * TOK), bytes_accessed=6 << 20, transcendentals=0
        ),
    )(mixed, sig_freq, spec, halo, taps, head, tail, inv)


def on_device(out_grad, out_weight, signal, gate_input, filter_taps):
    ctx = ("z", "h", "c")
    n_ctx = 64
    period = SPAN // TOK
    fwd, inv = transforms()

    turned = out_weight.T.reshape(64, 2, 512).transpose(1, 0, 2)
    tap_rows = filter_taps.T
    tap_high = lax.optimization_barrier(tap_rows.astype(BF))
    tap_low = (tap_rows - tap_high.astype(F32)).astype(BF)
    tap_pack = jnp.concatenate([tap_high, tap_low, jnp.zeros((16, 256), BF)], axis=1)
    message = jnp.concatenate([turned, jnp.broadcast_to(tap_pack[None], (2, 16, 512))], axis=1)
    got = lax.all_to_all(message, "c", split_axis=0, concat_axis=0)
    block = jnp.concatenate(
        [
            got[:, :64].reshape(K, 512),
            jnp.concatenate([got[0, 64:, :256], got[1, 64:, :256]], axis=1),
        ],
        axis=0,
    )

    cols = out_grad.reshape(TOK, 2, 2, K).transpose(2, 1, 0, 3)
    block, cols = lax.optimization_barrier((block, cols))
    weights = lax.all_gather(block, "z", axis=0, tiled=False)
    cols = lax.all_to_all(cols, "h", split_axis=0, concat_axis=0)

    ahead = [(i, i + 1) for i in range(n_ctx - 1) if (i + 1) % period]
    back = [(j, i) for i, j in ahead]
    sig_halo = lax.ppermute(signal[TOK - K :], ctx, ahead)
    window = jnp.concatenate([sig_halo, signal], axis=0)
    sig_freq = front_part(window, fwd[:, :, :N])

    cols, sig_freq = lax.optimization_barrier((cols, sig_freq))
    cols = lax.all_to_all(
        jnp.broadcast_to(cols[None], (8, 2, 2, TOK, K)), ("x", "l"), split_axis=0, concat_axis=0
    )
    cols = lax.all_to_all(
        jnp.broadcast_to(cols[None], (2, 8, 2, 2, TOK, K)), "c", split_axis=0, concat_axis=0
    )

    partial = product(cols, weights)
    mix = lax.all_to_all(partial, ("h", "c"), split_axis=0, concat_axis=0)
    mixed, grad_head, spec, tap_grad = grad_part(
        mix.reshape(2, 2, TOK, 512), gate_input, sig_freq, fwd[:, :, K:N], inv[:, :K]
    )
    grad_halo = lax.ppermute(grad_head, ctx, back)

    weights, spec = lax.optimization_barrier((weights, spec))
    taps = weights[:, K:].reshape(16, 16, 2, 2, K).transpose(3, 0, 2, 1, 4)
    other = lax.ppermute(taps, "h", [(0, 1), (1, 0)])
    first = lax.axis_index("h") == 0
    taps = jnp.stack(
        [jnp.where(first, taps, other), jnp.where(first, other, taps)], axis=2
    ).reshape(2, CH, K)

    tap_grad = lax.all_to_all(tap_grad, "c", split_axis=0, concat_axis=0)
    tap_grad = (tap_grad[0] + tap_grad[1]).astype(BF)
    tap_grad = lax.all_to_all(tap_grad, ("z", "h"), split_axis=0, concat_axis=0)
    filter_grad = jnp.sum(tap_grad.astype(F32), axis=0).T

    gate_grad, signal_grad = out_part(
        mixed, sig_freq, spec, grad_halo, taps, fwd[:, :, :K], fwd[:, :, N:], inv[:, K:]
    )
    return signal_grad, gate_grad, filter_grad


def solution(mesh):
    fine = Mesh(mesh.devices.reshape(16, 2, 2, 4, 2), ("z", "h", "c", "x", "l"))
    ctx, tp = ("z", "h", "c"), ("x", "l")
    in_specs = (P(ctx, tp), P(tp, ctx), P(ctx, tp), P(ctx, tp), P(None, tp + ctx))
    out_specs = (P(ctx, tp), P(ctx, tp), P(None, tp + ctx))
    return jax.shard_map(
        on_device, mesh=fine, in_specs=in_specs, out_specs=out_specs, check_vma=False
    )
```

```python
import jax
import jax.numpy as jnp
import numpy as np
from jax import lax
from jax.experimental import pallas as pl
from jax.experimental.pallas import tpu as pltpu
from jax.sharding import Mesh, PartitionSpec as P

K = 128
TOK = 256
CH = 1024
SPAN = 8192
N = K + TOK
HALF = N // 2
TILE = 256
VMEM = 56 * 1024 * 1024

BF = jnp.bfloat16
F32 = jnp.float32
ROWS = ((1,), (0,))
LANES = ((1,), (1,))


def transforms():
    freq = 2.0 * np.pi * (np.arange(HALF) + 0.5) / N
    angle = freq[:, None] * np.arange(N + K)[None, :]
    forward = np.concatenate([np.cos(angle), -np.sin(angle)], axis=0)
    angle = angle[:, :N].T
    inverse = np.concatenate([np.cos(angle), -np.sin(angle)], axis=1) * (2.0 / N)
    return two(forward), two(inverse)


def two(values):
    values = np.asarray(values, np.float32)
    upper = values.astype(jnp.bfloat16)
    lower = (values - upper.astype(np.float32)).astype(jnp.bfloat16)
    return np.stack([upper, lower])


def dot(a, b, dims=ROWS):
    return lax.dot_general(a, b, (dims, ((), ())), preferred_element_type=F32)


def exact_side(matrix, values):
    return dot(matrix[0], values) + dot(matrix[1], values)


def both_sides(matrix, values):
    high = values.astype(BF)
    low = (values - high.astype(F32)).astype(BF)
    return dot(matrix[0], high) + dot(matrix[1], high) + dot(matrix[0], low)


def times(a, b):
    ar, ai, br, bi = a[:HALF], a[HALF:], b[:HALF], b[HALF:]
    return jnp.concatenate([ar * br - ai * bi, ar * bi + ai * br], axis=0)


def times_conj(a, b):
    ar, ai, br, bi = a[:HALF], a[HALF:], b[:HALF], b[HALF:]
    return jnp.concatenate([ar * br + ai * bi, ai * br - ar * bi], axis=0)


def params():
    return pltpu.CompilerParams(
        dimension_semantics=("arbitrary",), vmem_limit_bytes=VMEM
    )


def product_kernel(cols_ref, weight_ref, out_ref):
    weight = weight_ref[:, :K].reshape(16 * K, 512)
    rows = jnp.concatenate([cols_ref[0, i, 0, j] for i in range(8) for j in range(2)], axis=1)
    out_ref[0] = dot(rows, weight).astype(BF)


def product(cols, weights):
    return pl.pallas_call(
        product_kernel,
        grid=(4,),
        in_specs=[
            pl.BlockSpec((1, 8, 1, 2, TOK, K), lambda i: (i % 2, 0, i // 2, 0, 0, 0)),
            pl.BlockSpec((16, K + 16, 512), lambda i: (0, 0, 0)),
        ],
        out_specs=pl.BlockSpec((1, TOK, 512), lambda i: (i, 0, 0)),
        out_shape=jax.ShapeDtypeStruct((4, TOK, 512), BF),
        compiler_params=params(),
        cost_estimate=pl.CostEstimate(
            flops=2 * 1024 * 2048 * 512, bytes_accessed=8 << 20, transcendentals=0
        ),
    )(cols, weights)


def whole(shape):
    return pl.BlockSpec(shape, lambda j: (0,) * len(shape))


TILES = 512 // K
PAIR = pl.BlockSpec((1, TOK, 2 * K), lambda j: (j, 0, 0))
FREQ = pl.BlockSpec((1, N, 2 * K), lambda j: (j, 0, 0))


def front_kernel(halo_ref, tok_ref, forward_ref, freq_ref):
    first, second = tok_ref[0, 0], tok_ref[1, 0]
    window = jnp.concatenate(
        [
            jnp.concatenate([halo_ref[...], first[K:]], axis=1),
            jnp.concatenate([first[:K], second[:K]], axis=1),
            jnp.concatenate([first[K:], second[K:]], axis=1),
        ],
        axis=0,
    )
    freq_ref[0] = exact_side(forward_ref, window)


def front_part(halo, tokens, forward):
    return pl.pallas_call(
        front_kernel,
        grid=(TILES,),
        in_specs=[
            pl.BlockSpec((K, K), lambda j: (0, j)),
            pl.BlockSpec((2, 1, TOK, K), lambda j: (0, 0, 0, j)),
            whole((2, N, N)),
        ],
        out_specs=FREQ,
        out_shape=jax.ShapeDtypeStruct((TILES, N, 2 * K), F32),
        compiler_params=params(),
        cost_estimate=pl.CostEstimate(
            flops=2 * CH * N * 2 * N, bytes_accessed=3 << 20, transcendentals=0
        ),
    )(halo, tokens, forward)


def grad_kernel(
    mix_ref, tok_ref, freq_ref, own_ref, lag_ref, mixed_ref, first_ref, second_ref, spec_ref, tap_ref
):
    mixed = (mix_ref[0].astype(F32) + mix_ref[1].astype(F32)).astype(BF)
    mixed = jnp.concatenate([mixed[0], mixed[1]], axis=1)
    mixed_ref[0] = mixed
    gate = jnp.concatenate([tok_ref[0, 0], tok_ref[1, 0]], axis=1)
    conv_grad = (mixed.astype(F32) * gate.astype(F32)).astype(BF)
    first_ref[...] = conv_grad[:K, :K]
    second_ref[...] = conv_grad[:K, K:]
    spec = exact_side(own_ref, conv_grad)
    spec_ref[0] = spec
    cross = times_conj(spec, freq_ref[0])
    taps = both_sides(lag_ref, cross[:, :K] + cross[:, K:])
    tap_ref[...] = taps.T.reshape(8, 16, K).astype(BF)


def grad_part(mix, tokens, sig_freq, own, lag):
    return pl.pallas_call(
        grad_kernel,
        grid=(TILES,),
        in_specs=[
            pl.BlockSpec((2, 2, TOK, K), lambda j: (0, 0, 0, j)),
            pl.BlockSpec((2, 1, TOK, K), lambda j: (0, 1, 0, j)),
            FREQ,
            whole((2, N, TOK)),
            whole((2, K, N)),
        ],
        out_specs=[
            PAIR,
            pl.BlockSpec((K, K), lambda j: (0, j)),
            pl.BlockSpec((K, K), lambda j: (0, j)),
            FREQ,
            pl.BlockSpec((8, 16, K), lambda j: (j, 0, 0)),
        ],
        out_shape=[
            jax.ShapeDtypeStruct((TILES, TOK, 2 * K), BF),
            jax.ShapeDtypeStruct((K, 512), BF),
            jax.ShapeDtypeStruct((K, 512), BF),
            jax.ShapeDtypeStruct((TILES, N, 2 * K), F32),
            jax.ShapeDtypeStruct((32, 16, K), BF),
        ],
        compiler_params=params(),
        cost_estimate=pl.CostEstimate(
            flops=2 * CH * N * (2 * TOK + 2 * K), bytes_accessed=7 << 20, transcendentals=0
        ),
    )(mix, tokens, sig_freq, own, lag)


def out_kernel(
    mixed_ref,
    freq_ref,
    spec_ref,
    inner_ref,
    outer_ref,
    tap_ref,
    head_ref,
    tail_ref,
    inv_ref,
    out_ref,
):
    upper, lower = tap_ref[0], tap_ref[1]
    high, low = head_ref[0], head_ref[1]
    tap_freq = dot(high, upper, LANES) + dot(low, upper, LANES) + dot(high, lower, LANES)
    tap_freq = jnp.concatenate([tap_freq, tap_freq], axis=1)
    conv_out = both_sides(inv_ref, times(freq_ref[0], tap_freq))
    gate = mixed_ref[0].astype(F32) * conv_out
    halo = jnp.concatenate([inner_ref[...], outer_ref[...]], axis=1)
    full = spec_ref[0] + exact_side(tail_ref, halo)
    sig = both_sides(inv_ref, times_conj(full, tap_freq))
    for i, values in enumerate((sig, gate)):
        out_ref[0, i] = values[:, :K].astype(BF)
        out_ref[1, i] = values[:, K:].astype(BF)


def out_part(mixed, sig_freq, spec, inner, outer, taps, head, tail, inv):
    return pl.pallas_call(
        out_kernel,
        grid=(TILES,),
        in_specs=[
            PAIR,
            FREQ,
            FREQ,
            pl.BlockSpec((K, K), lambda j: (0, j)),
            pl.BlockSpec((K, K), lambda j: (0, j)),
            pl.BlockSpec((2, K, K), lambda j: (0, j, 0)),
            whole((2, N, K)),
            whole((2, N, K)),
            whole((2, TOK, N)),
        ],
        out_specs=pl.BlockSpec((2, 2, TOK, K), lambda j: (0, 0, 0, j)),
        out_shape=jax.ShapeDtypeStruct((2, 2, TOK, 512), BF),
        compiler_params=params(),
        cost_estimate=pl.CostEstimate(
            flops=2 * CH * N * (5 * K + 6 * TOK), bytes_accessed=6 << 20, transcendentals=0
        ),
    )(mixed, sig_freq, spec, inner, outer, taps, head, tail, inv)


def join_kernel(parts_ref, place_ref, sig_ref, gate_ref):
    for i, out_ref in enumerate((sig_ref, gate_ref)):
        rows = jnp.concatenate([parts_ref[0, i], parts_ref[1, i]], axis=1)
        out_ref[...] = dot(rows, place_ref[...]).astype(BF)


def join_part(parts, place):
    out = pl.BlockSpec((TOK, 2 * K), lambda j: (0, j))
    return pl.pallas_call(
        join_kernel,
        grid=(TILES,),
        in_specs=[
            pl.BlockSpec((2, 2, TOK, K), lambda j: (0, 0, 0, j)),
            whole((2 * K, 2 * K)),
        ],
        out_specs=[out, out],
        out_shape=[jax.ShapeDtypeStruct((TOK, CH), BF)] * 2,
        compiler_params=params(),
        cost_estimate=pl.CostEstimate(
            flops=4 * TOK * CH * 256, bytes_accessed=2 << 20, transcendentals=0
        ),
    )(parts, place)


def chooser():
    source = np.arange(2 * K).reshape(8, 2, 16).transpose(1, 0, 2).reshape(-1)
    matrix = np.zeros((2 * K, 2 * K), np.float32)
    matrix[source, np.arange(2 * K)] = 1.0
    return matrix.astype(jnp.bfloat16)


def by_core(values, place):
    rows = values.shape[0]
    chosen = dot(values.reshape(rows * 4, 2 * K), place).astype(BF)
    return chosen.reshape(rows, 4, 2, K).transpose(2, 0, 1, 3).reshape(2, rows, 512)


def on_device(out_grad, out_weight, signal, gate_input, filter_taps):
    chips = ("z", "h")
    period = SPAN // (2 * TOK)
    fwd, inv = transforms()
    place = chooser()

    turned = by_core(out_weight.T, place)
    tap_rows = filter_taps.T
    tap_high = lax.optimization_barrier(tap_rows.astype(BF))
    tap_low = (tap_rows - tap_high.astype(F32)).astype(BF)
    tap_pack = jnp.concatenate([tap_high, tap_low, jnp.zeros((16, 256), BF)], axis=1)
    turned = lax.all_to_all(turned, "c", split_axis=0, concat_axis=0).reshape(K, 512)
    block = jnp.concatenate([turned, tap_pack], axis=0)

    cols = out_grad.reshape(TOK, 2, 2, K).transpose(2, 1, 0, 3)
    block, cols, signal, gate_input = lax.optimization_barrier((block, cols, signal, gate_input))
    weights = lax.all_gather(block, "z", axis=0, tiled=False)
    cols = lax.all_to_all(cols, "h", split_axis=0, concat_axis=0)

    tokens = jnp.concatenate([by_core(signal, place), by_core(gate_input, place)], axis=1)
    tokens = lax.all_to_all(
        tokens.reshape(2, 2, TOK, 512), "c", split_axis=0, concat_axis=0
    )
    ahead = [(i, i + 1) for i in range(31) if (i + 1) % period]
    back = [(j, i) for i, j in ahead]
    sig_halo = lax.ppermute(tokens[1, 0, TOK - K :], chips, ahead)
    sig_freq = front_part(sig_halo, tokens, fwd[:, :, :N])

    cols, sig_freq = lax.optimization_barrier((cols, sig_freq))
    cols = lax.all_to_all(
        jnp.broadcast_to(cols[None], (8, 2, 2, TOK, K)), ("x", "l"), split_axis=0, concat_axis=0
    )
    cols = lax.all_to_all(
        jnp.broadcast_to(cols[None], (2, 8, 2, 2, TOK, K)), "c", split_axis=0, concat_axis=0
    )

    partial = product(cols, weights)
    mix = lax.all_to_all(
        partial.reshape(2, 2, TOK, 512), "h", split_axis=0, concat_axis=0
    )
    mixed, first_head, inner, spec, tap_grad = grad_part(
        mix, tokens, sig_freq, fwd[:, :, K:N], inv[:, :K]
    )
    outer = lax.ppermute(first_head, chips, back)
    tap_grad = lax.all_to_all(tap_grad, chips, split_axis=0, concat_axis=0)
    filter_grad = jnp.sum(tap_grad.astype(F32), axis=0).T

    weights, spec = lax.optimization_barrier((weights, spec))
    taps = weights[:, K:, : 2 * K].reshape(16, 16, 2, K).transpose(2, 0, 1, 3)
    other = lax.ppermute(taps, "h", [(0, 1), (1, 0)])
    upper_half = lax.axis_index("h") == 0
    taps = jnp.stack(
        [jnp.where(upper_half, taps, other), jnp.where(upper_half, other, taps)], axis=2
    ).reshape(2, 512, K)

    own = out_part(
        mixed, sig_freq, spec, inner, outer, taps, fwd[:, :, :K], fwd[:, :, N:], inv[:, K:]
    )
    other = lax.all_to_all(own, "c", split_axis=0, concat_axis=0)
    signal_grad, gate_grad = join_part(other, place.T)
    return signal_grad, gate_grad, filter_grad


def solution(mesh):
    fine = Mesh(mesh.devices.reshape(16, 2, 2, 4, 2), ("z", "h", "c", "x", "l"))
    ctx, tp = ("z", "h", "c"), ("x", "l")
    in_specs = (P(ctx, tp), P(tp, ctx), P(ctx, tp), P(ctx, tp), P(None, tp + ctx))
    out_specs = (P(ctx, tp), P(ctx, tp), P(None, tp + ctx))
    return jax.shard_map(
        on_device, mesh=fine, in_specs=in_specs, out_specs=out_specs, check_vma=False
    )
```

```python
import jax
import jax.numpy as jnp
import numpy as np
from jax import lax
from jax.experimental import pallas as pl
from jax.experimental.pallas import tpu as pltpu
from jax.sharding import Mesh, PartitionSpec as P

K = 128
TOK = 256
CH = 1024
SPAN = 8192
N = K + TOK
HALF = N // 2
TILE = 256
VMEM = 56 * 1024 * 1024

BF = jnp.bfloat16
F32 = jnp.float32
ROWS = ((1,), (0,))
LANES = ((1,), (1,))


def transforms():
    freq = 2.0 * np.pi * (np.arange(HALF) + 0.5) / N
    angle = freq[:, None] * np.arange(N + K)[None, :]
    forward = np.concatenate([np.cos(angle), -np.sin(angle)], axis=0)
    angle = angle[:, :N].T
    inverse = np.concatenate([np.cos(angle), -np.sin(angle)], axis=1) * (2.0 / N)
    return two(forward), two(inverse)


def two(values):
    values = np.asarray(values, np.float32)
    upper = values.astype(jnp.bfloat16)
    lower = (values - upper.astype(np.float32)).astype(jnp.bfloat16)
    return np.stack([upper, lower])


def dot(a, b, dims=ROWS):
    return lax.dot_general(a, b, (dims, ((), ())), preferred_element_type=F32)


def exact_side(matrix, values):
    return dot(matrix[0], values) + dot(matrix[1], values)


def both_sides(matrix, values):
    high = values.astype(BF)
    low = (values - high.astype(F32)).astype(BF)
    return dot(matrix[0], high) + dot(matrix[1], high) + dot(matrix[0], low)


def times(a, b):
    ar, ai, br, bi = a[:HALF], a[HALF:], b[:HALF], b[HALF:]
    return jnp.concatenate([ar * br - ai * bi, ar * bi + ai * br], axis=0)


def times_conj(a, b):
    ar, ai, br, bi = a[:HALF], a[HALF:], b[:HALF], b[HALF:]
    return jnp.concatenate([ar * br + ai * bi, ai * br - ar * bi], axis=0)


def params():
    return pltpu.CompilerParams(
        dimension_semantics=("arbitrary",), vmem_limit_bytes=VMEM
    )


def product_kernel(cols_ref, weight_ref, out_ref):
    weight = weight_ref[:, :K].reshape(16 * K, 512)
    rows = jnp.concatenate([cols_ref[0, i, 0, j] for i in range(8) for j in range(2)], axis=1)
    out_ref[0] = dot(rows, weight).astype(BF)


def product(cols, weights):
    return pl.pallas_call(
        product_kernel,
        grid=(4,),
        in_specs=[
            pl.BlockSpec((1, 8, 1, 2, TOK, K), lambda i: (i % 2, 0, i // 2, 0, 0, 0)),
            pl.BlockSpec((16, K + 16, 512), lambda i: (0, 0, 0)),
        ],
        out_specs=pl.BlockSpec((1, TOK, 512), lambda i: (i, 0, 0)),
        out_shape=jax.ShapeDtypeStruct((4, TOK, 512), BF),
        compiler_params=params(),
        cost_estimate=pl.CostEstimate(
            flops=2 * 1024 * 2048 * 512, bytes_accessed=8 << 20, transcendentals=0
        ),
    )(cols, weights)


def whole(shape):
    return pl.BlockSpec(shape, lambda j: (0,) * len(shape))


def scalar():
    return pl.BlockSpec(memory_space=pltpu.SMEM)


TILES = 512 // K
PAIR = pl.BlockSpec((1, TOK, 2 * K), lambda j: (j, 0, 0))
FREQ = pl.BlockSpec((1, N, 2 * K), lambda j: (j, 0, 0))


def plain_kernel(window_ref, forward_ref, freq_ref):
    freq_ref[...] = exact_side(forward_ref, window_ref[...])


def plain_part(window, forward):
    tile = pl.BlockSpec((N, 2 * K), lambda j: (0, j))
    return pl.pallas_call(
        plain_kernel,
        grid=(TILES,),
        in_specs=[tile, whole((2, N, N))],
        out_specs=tile,
        out_shape=jax.ShapeDtypeStruct((N, CH), F32),
        compiler_params=params(),
        cost_estimate=pl.CostEstimate(
            flops=2 * CH * N * 2 * N, bytes_accessed=3 << 20, transcendentals=0
        ),
    )(window, forward)


def front_kernel(halo_ref, tok_ref, forward_ref, freq_ref):
    first, second = tok_ref[0, 0], tok_ref[1, 0]
    window = jnp.concatenate(
        [
            jnp.concatenate([halo_ref[...], first[K:]], axis=1),
            jnp.concatenate([first[:K], second[:K]], axis=1),
            jnp.concatenate([first[K:], second[K:]], axis=1),
        ],
        axis=0,
    )
    freq_ref[0] = exact_side(forward_ref, window)


def front_part(halo, tokens, forward):
    return pl.pallas_call(
        front_kernel,
        grid=(TILES,),
        in_specs=[
            pl.BlockSpec((K, K), lambda j: (0, j)),
            pl.BlockSpec((2, 1, TOK, K), lambda j: (0, 0, 0, j)),
            whole((2, N, N)),
        ],
        out_specs=FREQ,
        out_shape=jax.ShapeDtypeStruct((TILES, N, 2 * K), F32),
        compiler_params=params(),
        cost_estimate=pl.CostEstimate(
            flops=2 * CH * N * 2 * N, bytes_accessed=3 << 20, transcendentals=0
        ),
    )(halo, tokens, forward)


def grad_kernel(
    core_ref,
    mix_ref,
    tok_ref,
    freq_ref,
    own_ref,
    lag_ref,
    keep_ref,
    send_ref,
    first_ref,
    inner_ref,
    cross_ref,
    tap_ref,
):
    is_first = core_ref[0] == 0
    early = (mix_ref[0, 0].astype(F32) + mix_ref[1, 0].astype(F32)).astype(BF).astype(F32)
    late = (mix_ref[0, 1].astype(F32) + mix_ref[1, 1].astype(F32)).astype(BF).astype(F32)
    keep_ref[...] = jnp.where(is_first, early, late).astype(BF)
    send_ref[...] = jnp.where(is_first, late, early).astype(BF)
    early = early * tok_ref[0, 0].astype(F32)
    late = late * tok_ref[1, 0].astype(F32)
    first_ref[...] = early[:K].astype(BF)
    inner_ref[...] = late[:K].astype(BF)
    cross_ref[...] = jnp.where(is_first, early[:K], late[:K]).astype(BF)
    conv_grad = jnp.concatenate([early, late], axis=1).astype(BF)
    cross = times_conj(exact_side(own_ref, conv_grad), freq_ref[0])
    taps = both_sides(lag_ref, cross[:, :K] + cross[:, K:])
    tap_ref[...] = taps.T.reshape(8, 16, K).astype(tap_ref.dtype)


def grad_part(core, mix, tokens, sig_freq, own, lag):
    head = pl.BlockSpec((K, K), lambda j: (0, j))
    half = pl.BlockSpec((TOK, K), lambda j: (0, j))
    return pl.pallas_call(
        grad_kernel,
        grid=(TILES,),
        in_specs=[
            scalar(),
            pl.BlockSpec((2, 2, TOK, K), lambda j: (0, 0, 0, j)),
            pl.BlockSpec((2, 1, TOK, K), lambda j: (0, 1, 0, j)),
            FREQ,
            whole((2, N, TOK)),
            whole((2, K, N)),
        ],
        out_specs=[half, half, head, head, head, pl.BlockSpec((8, 16, K), lambda j: (j, 0, 0))],
        out_shape=[jax.ShapeDtypeStruct((TOK, 512), BF)] * 2
        + [jax.ShapeDtypeStruct((K, 512), BF)] * 3
        + [jax.ShapeDtypeStruct((32, 16, K), BF)],
        compiler_params=params(),
        cost_estimate=pl.CostEstimate(
            flops=2 * CH * N * (2 * TOK + 2 * K), bytes_accessed=5 << 20, transcendentals=0
        ),
    )(core, mix, tokens, sig_freq, own, lag)


def out_kernel(
    core_ref,
    keep_ref,
    other_ref,
    inner_ref,
    near_ref,
    far_ref,
    gate_in_ref,
    freq_ref,
    tap_ref,
    forward_ref,
    inv_ref,
    place_ref,
    gate_ref,
    sig_ref,
):
    is_first = core_ref[0] == 0

    def joined(left, right):
        return dot(jnp.concatenate([left, right], axis=1), place_ref[...])

    keep, other = keep_ref[...], other_ref[...]
    mixed = joined(jnp.where(is_first, keep, other), jnp.where(is_first, other, keep))
    near = near_ref[...]
    halo = joined(
        jnp.where(is_first, inner_ref[...], near), jnp.where(is_first, near, far_ref[...])
    ).astype(BF)
    conv_grad = (mixed * gate_in_ref[...].astype(F32)).astype(BF)
    window = jnp.concatenate([conv_grad, halo], axis=0)
    full = exact_side(forward_ref[:, :, K:], window)
    upper, lower = tap_ref[0], tap_ref[1]
    high, low = forward_ref[0, :, :K], forward_ref[1, :, :K]
    tap_freq = dot(high, upper, LANES) + dot(low, upper, LANES) + dot(high, lower, LANES)
    conv_out = both_sides(inv_ref, times(freq_ref[...], tap_freq))
    gate_ref[...] = (mixed * conv_out).astype(BF)
    sig_ref[...] = both_sides(inv_ref, times_conj(full, tap_freq)).astype(BF)


def out_part(core, keep, other, inner, near, far, gate, sig_freq, taps, forward, inv, place):
    head = pl.BlockSpec((K, K), lambda j: (0, j))
    half = pl.BlockSpec((TOK, K), lambda j: (0, j))

    def tile(rows):
        return pl.BlockSpec((rows, 2 * K), lambda j: (0, j))

    return pl.pallas_call(
        out_kernel,
        grid=(TILES,),
        in_specs=[
            scalar(),
            half,
            half,
            head,
            head,
            head,
            tile(TOK),
            tile(N),
            pl.BlockSpec((2, 2 * K, K), lambda j: (0, j, 0)),
            whole((2, N, N + K)),
            whole((2, TOK, N)),
            whole((2 * K, 2 * K)),
        ],
        out_specs=[tile(TOK), tile(TOK)],
        out_shape=[jax.ShapeDtypeStruct((TOK, CH), BF)] * 2,
        compiler_params=params(),
        cost_estimate=pl.CostEstimate(
            flops=2 * CH * N * (5 * K + 8 * TOK), bytes_accessed=6 << 20, transcendentals=0
        ),
    )(core, keep, other, inner, near, far, gate, sig_freq, taps, forward, inv, place)


def chooser():
    source = np.arange(2 * K).reshape(8, 2, 16).transpose(1, 0, 2).reshape(-1)
    matrix = np.zeros((2 * K, 2 * K), np.float32)
    matrix[source, np.arange(2 * K)] = 1.0
    return matrix.astype(jnp.bfloat16)


def by_core(values, place):
    rows = values.shape[0]
    chosen = dot(values.reshape(rows * 4, 2 * K), place).astype(BF)
    return chosen.reshape(rows, 4, 2, K).transpose(2, 0, 1, 3).reshape(2, rows, 512)


def on_device(out_grad, out_weight, signal, gate_input, filter_taps):
    chips, ctx = ("z", "h"), ("z", "h", "c")
    period = SPAN // TOK
    fwd, inv = transforms()
    place = chooser()
    core = lax.axis_index("c").reshape(1)

    turned = by_core(out_weight.T, place)
    tap_rows = filter_taps.T
    tap_high = lax.optimization_barrier(tap_rows.astype(BF))
    tap_low = (tap_rows - tap_high.astype(F32)).astype(BF)
    tap_pack = jnp.concatenate([tap_high, tap_low, jnp.zeros((16, 256), BF)], axis=1)
    message = jnp.concatenate([turned, jnp.broadcast_to(tap_pack[None], (2, 16, 512))], axis=1)
    got = lax.all_to_all(message, "c", split_axis=0, concat_axis=0)
    block = jnp.concatenate(
        [
            got[:, :64].reshape(K, 512),
            jnp.concatenate([got[0, 64:, :256], got[1, 64:, :256]], axis=1),
        ],
        axis=0,
    )

    cols = out_grad.reshape(TOK, 2, 2, K).transpose(2, 1, 0, 3)
    block, cols, signal, gate_input = lax.optimization_barrier((block, cols, signal, gate_input))
    weights = lax.all_gather(block, "z", axis=0, tiled=False)
    cols = lax.all_to_all(cols, "h", split_axis=0, concat_axis=0)

    ahead = [(i, i + 1) for i in range(63) if (i + 1) % period]
    window = jnp.concatenate([lax.ppermute(signal[TOK - K :], ctx, ahead), signal], axis=0)
    sig_freq = plain_part(window, fwd[:, :, :N])
    tokens = jnp.concatenate([by_core(signal, place), by_core(gate_input, place)], axis=1)
    tokens = lax.all_to_all(
        tokens.reshape(2, 2, TOK, 512), "c", split_axis=0, concat_axis=0
    )
    ahead = [(i, i + 1) for i in range(31) if (i + 1) % (period // 2)]
    sig_halo = lax.ppermute(tokens[1, 0, TOK - K :], chips, ahead)
    own_freq = front_part(sig_halo, tokens, fwd[:, :, :N])

    cols, sig_freq, own_freq = lax.optimization_barrier((cols, sig_freq, own_freq))
    cols = lax.all_to_all(
        jnp.broadcast_to(cols[None], (8, 2, 2, TOK, K)), ("x", "l"), split_axis=0, concat_axis=0
    )
    cols = lax.all_to_all(
        jnp.broadcast_to(cols[None], (2, 8, 2, 2, TOK, K)), "c", split_axis=0, concat_axis=0
    )

    partial = product(cols, weights)
    mix = lax.all_to_all(
        partial.reshape(2, 2, TOK, 512), "h", split_axis=0, concat_axis=0
    )
    keep, send, first, inner, cross, tap_grad = grad_part(
        core, mix, tokens, own_freq, fwd[:, :, K:N], inv[:, :K]
    )
    tap_grad = lax.all_to_all(tap_grad, chips, split_axis=0, concat_axis=0)
    filter_grad = jnp.sum(tap_grad.astype(F32), axis=0).T

    other = lax.ppermute(send, "c", [(0, 1), (1, 0)])
    follows = [(2 * i + 2, 2 * i + 1) for i in range(31) if (i + 1) % (period // 2)]
    near = lax.ppermute(cross, ctx, follows + [(2 * i + 1, 2 * i) for i in range(32)])
    far = lax.ppermute(first, ctx, [(i + 1, j) for i, j in follows])

    weights, keep = lax.optimization_barrier((weights, keep))
    taps = weights[:, K:].reshape(16, 16, 2, 2, K).transpose(3, 0, 2, 1, 4)
    more = lax.ppermute(taps, "h", [(0, 1), (1, 0)])
    upper_half = lax.axis_index("h") == 0
    taps = jnp.stack(
        [jnp.where(upper_half, taps, more), jnp.where(upper_half, more, taps)], axis=2
    ).reshape(2, CH, K)

    gate_grad, signal_grad = out_part(
        core, keep, other, inner, near, far, gate_input, sig_freq, taps, fwd, inv[:, K:], place.T
    )
    return signal_grad, gate_grad, filter_grad


def solution(mesh):
    fine = Mesh(mesh.devices.reshape(16, 2, 2, 4, 2), ("z", "h", "c", "x", "l"))
    ctx, tp = ("z", "h", "c"), ("x", "l")
    in_specs = (P(ctx, tp), P(tp, ctx), P(ctx, tp), P(ctx, tp), P(None, tp + ctx))
    out_specs = (P(ctx, tp), P(ctx, tp), P(None, tp + ctx))
    return jax.shard_map(
        on_device, mesh=fine, in_specs=in_specs, out_specs=out_specs, check_vma=False
    )
```

```python
import jax
import jax.numpy as jnp
import numpy as np
from jax import lax
from jax.experimental import pallas as pl
from jax.experimental.pallas import tpu as pltpu
from jax.sharding import Mesh, PartitionSpec as P

K = 128
TOK = 256
CH = 1024
SPAN = 8192
N = K + TOK
HALF = N // 2
TILE = 256
VMEM = 60 * 1024 * 1024

BF = jnp.bfloat16
F32 = jnp.float32
ROWS = ((1,), (0,))
LANES = ((1,), (1,))


def transforms():
    freq = 2.0 * np.pi * (np.arange(HALF) + 0.5) / N
    angle = freq[:, None] * np.arange(N + K)[None, :]
    forward = np.concatenate([np.cos(angle), -np.sin(angle)], axis=0)
    angle = angle[:, :N].T
    inverse = np.concatenate([np.cos(angle), -np.sin(angle)], axis=1) * (2.0 / N)
    return two(forward), two(inverse)


def two(values):
    values = np.asarray(values, np.float32)
    upper = values.astype(jnp.bfloat16)
    lower = (values - upper.astype(np.float32)).astype(jnp.bfloat16)
    return np.stack([upper, lower])


def dot(a, b, dims=ROWS):
    return lax.dot_general(a, b, (dims, ((), ())), preferred_element_type=F32)


def exact_side(matrix, values):
    return dot(matrix[0], values) + dot(matrix[1], values)


def both_sides(matrix, values):
    high = values.astype(BF)
    low = (values - high.astype(F32)).astype(BF)
    return dot(matrix[0], high) + dot(matrix[1], high) + dot(matrix[0], low)


def times(a, b):
    ar, ai, br, bi = a[:HALF], a[HALF:], b[:HALF], b[HALF:]
    return jnp.concatenate([ar * br - ai * bi, ar * bi + ai * br], axis=0)


def times_conj(a, b):
    ar, ai, br, bi = a[:HALF], a[HALF:], b[:HALF], b[HALF:]
    return jnp.concatenate([ar * br + ai * bi, ai * br - ar * bi], axis=0)


def params():
    return pltpu.CompilerParams(
        dimension_semantics=("arbitrary",), vmem_limit_bytes=VMEM
    )


def product_kernel(cols_ref, weight_ref, out_ref):
    weight = weight_ref[:, :, :64].reshape(16 * K, 512)
    rows = jnp.concatenate([cols_ref[0, i, 0, j] for i in range(8) for j in range(2)], axis=1)
    out_ref[0] = dot(rows, weight).astype(BF)


def product(cols, weights):
    return pl.pallas_call(
        product_kernel,
        grid=(4,),
        in_specs=[
            pl.BlockSpec((1, 8, 1, 2, TOK, K), lambda i: (i % 2, 0, i // 2, 0, 0, 0)),
            pl.BlockSpec((16, 2, 80, 512), lambda i: (0, 0, 0, 0)),
        ],
        out_specs=pl.BlockSpec((1, TOK, 512), lambda i: (i, 0, 0)),
        out_shape=jax.ShapeDtypeStruct((4, TOK, 512), BF),
        compiler_params=params(),
        cost_estimate=pl.CostEstimate(
            flops=2 * 1024 * 2048 * 512, bytes_accessed=8 << 20, transcendentals=0
        ),
    )(cols, weights)


def whole(shape):
    return pl.BlockSpec(shape, lambda j: (0,) * len(shape))


def scalar():
    return pl.BlockSpec(memory_space=pltpu.SMEM)


TILES = 512 // K
PAIR = pl.BlockSpec((1, TOK, 2 * K), lambda j: (j, 0, 0))
FREQ = pl.BlockSpec((1, N, 2 * K), lambda j: (j, 0, 0))


def plain_kernel(window_ref, forward_ref, freq_ref):
    freq_ref[...] = exact_side(forward_ref, window_ref[...])


def plain_part(window, forward):
    tile = pl.BlockSpec((N, 2 * K), lambda j: (0, j))
    return pl.pallas_call(
        plain_kernel,
        grid=(TILES,),
        in_specs=[tile, whole((2, N, N))],
        out_specs=tile,
        out_shape=jax.ShapeDtypeStruct((N, CH), F32),
        compiler_params=params(),
        cost_estimate=pl.CostEstimate(
            flops=2 * CH * N * 2 * N, bytes_accessed=3 << 20, transcendentals=0
        ),
    )(window, forward)


def front_kernel(halo_ref, tok_ref, forward_ref, freq_ref):
    first, second = tok_ref[0, 0], tok_ref[1, 0]
    window = jnp.concatenate(
        [
            jnp.concatenate([halo_ref[...], first[K:]], axis=1),
            jnp.concatenate([first[:K], second[:K]], axis=1),
            jnp.concatenate([first[K:], second[K:]], axis=1),
        ],
        axis=0,
    )
    freq_ref[0] = exact_side(forward_ref, window)


def front_part(halo, tokens, forward):
    return pl.pallas_call(
        front_kernel,
        grid=(TILES,),
        in_specs=[
            pl.BlockSpec((K, K), lambda j: (0, j)),
            pl.BlockSpec((2, 1, TOK, K), lambda j: (0, 0, 0, j)),
            whole((2, N, N)),
        ],
        out_specs=FREQ,
        out_shape=jax.ShapeDtypeStruct((TILES, N, 2 * K), F32),
        compiler_params=params(),
        cost_estimate=pl.CostEstimate(
            flops=2 * CH * N * 2 * N, bytes_accessed=3 << 20, transcendentals=0
        ),
    )(halo, tokens, forward)


def grad_kernel(
    core_ref,
    mix_ref,
    tok_ref,
    freq_ref,
    own_ref,
    lag_ref,
    keep_ref,
    send_ref,
    first_ref,
    inner_ref,
    cross_ref,
    tap_ref,
):
    is_first = core_ref[0] == 0
    early = (mix_ref[0, 0].astype(F32) + mix_ref[1, 0].astype(F32)).astype(BF).astype(F32)
    late = (mix_ref[0, 1].astype(F32) + mix_ref[1, 1].astype(F32)).astype(BF).astype(F32)
    keep_ref[...] = jnp.where(is_first, early, late).astype(BF)
    send_ref[...] = jnp.where(is_first, late, early).astype(BF)
    early = early * tok_ref[0, 0].astype(F32)
    late = late * tok_ref[1, 0].astype(F32)
    first_ref[...] = early[:K].astype(BF)
    inner_ref[...] = late[:K].astype(BF)
    cross_ref[...] = jnp.where(is_first, early[:K], late[:K]).astype(BF)
    conv_grad = jnp.concatenate([early, late], axis=1).astype(BF)
    cross = times_conj(exact_side(own_ref, conv_grad), freq_ref[0])
    taps = both_sides(lag_ref, cross[:, :K] + cross[:, K:])
    tap_ref[...] = taps.T.reshape(8, 16, K).astype(tap_ref.dtype)


def grad_part(core, mix, tokens, sig_freq, own, lag):
    head = pl.BlockSpec((K, K), lambda j: (0, j))
    half = pl.BlockSpec((TOK, K), lambda j: (0, j))
    return pl.pallas_call(
        grad_kernel,
        grid=(TILES,),
        in_specs=[
            scalar(),
            pl.BlockSpec((2, 2, TOK, K), lambda j: (0, 0, 0, j)),
            pl.BlockSpec((2, 1, TOK, K), lambda j: (0, 1, 0, j)),
            FREQ,
            whole((2, N, TOK)),
            whole((2, K, N)),
        ],
        out_specs=[half, half, head, head, head, pl.BlockSpec((8, 16, K), lambda j: (j, 0, 0))],
        out_shape=[jax.ShapeDtypeStruct((TOK, 512), BF)] * 2
        + [jax.ShapeDtypeStruct((K, 512), BF)] * 3
        + [jax.ShapeDtypeStruct((32, 16, K), BF)],
        compiler_params=params(),
        cost_estimate=pl.CostEstimate(
            flops=2 * CH * N * (2 * TOK + 2 * K), bytes_accessed=5 << 20, transcendentals=0
        ),
    )(core, mix, tokens, sig_freq, own, lag)


def out_kernel(
    core_ref,
    keep_ref,
    other_ref,
    inner_ref,
    near_ref,
    far_ref,
    gate_in_ref,
    freq_ref,
    tap_ref,
    forward_ref,
    inv_ref,
    place_ref,
    gate_ref,
    sig_ref,
):
    is_first = core_ref[0] == 0

    def joined(left, right):
        return dot(jnp.concatenate([left, right], axis=1), place_ref[...])

    keep, other = keep_ref[...], other_ref[...]
    mixed = joined(jnp.where(is_first, keep, other), jnp.where(is_first, other, keep))
    near = near_ref[...]
    halo = joined(
        jnp.where(is_first, inner_ref[...], near), jnp.where(is_first, near, far_ref[...])
    ).astype(BF)
    conv_grad = (mixed * gate_in_ref[...].astype(F32)).astype(BF)
    window = jnp.concatenate([conv_grad, halo], axis=0)
    full = exact_side(forward_ref[:, :, K:], window)
    upper, lower = tap_ref[0], tap_ref[1]
    high, low = forward_ref[0, :, :K], forward_ref[1, :, :K]
    tap_freq = dot(high, upper, LANES) + dot(low, upper, LANES) + dot(high, lower, LANES)
    conv_out = both_sides(inv_ref, times(freq_ref[...], tap_freq))
    gate_ref[...] = (mixed * conv_out).astype(BF)
    sig_ref[...] = both_sides(inv_ref, times_conj(full, tap_freq)).astype(BF)


def out_part(core, keep, other, inner, near, far, gate, sig_freq, taps, forward, inv, place):
    head = pl.BlockSpec((K, K), lambda j: (0, j))
    half = pl.BlockSpec((TOK, K), lambda j: (0, j))

    def tile(rows):
        return pl.BlockSpec((rows, 2 * K), lambda j: (0, j))

    return pl.pallas_call(
        out_kernel,
        grid=(TILES,),
        in_specs=[
            scalar(),
            half,
            half,
            head,
            head,
            head,
            tile(TOK),
            tile(N),
            pl.BlockSpec((2, 2 * K, K), lambda j: (0, j, 0)),
            whole((2, N, N + K)),
            whole((2, TOK, N)),
            whole((2 * K, 2 * K)),
        ],
        out_specs=[tile(TOK), tile(TOK)],
        out_shape=[jax.ShapeDtypeStruct((TOK, CH), BF)] * 2,
        compiler_params=params(),
        cost_estimate=pl.CostEstimate(
            flops=1024, bytes_accessed=1024, transcendentals=0
        ),
    )(core, keep, other, inner, near, far, gate, sig_freq, taps, forward, inv, place)


def chooser():
    source = np.arange(2 * K).reshape(8, 2, 16).transpose(1, 0, 2).reshape(-1)
    matrix = np.zeros((2 * K, 2 * K), np.float32)
    matrix[source, np.arange(2 * K)] = 1.0
    return matrix.astype(jnp.bfloat16)


def send_kernel(weight_ref, tap_ref, place_ref, out_ref):
    out_ref[...] = jnp.zeros_like(out_ref)
    taps = tap_ref[...]
    high = taps.astype(BF)
    low = (taps - high.astype(F32)).astype(BF)
    for c in range(2):
        out_ref[c, 64:, :K] = high
        out_ref[c, 64:, K : 2 * K] = low
    for i in range(4):
        lanes = slice(i * 2 * K, (i + 1) * 2 * K)
        chosen = dot(weight_ref[:, lanes], place_ref[...]).astype(BF)
        out_ref[0, :64, i * K : (i + 1) * K] = chosen[:, :K]
        out_ref[1, :64, i * K : (i + 1) * K] = chosen[:, K:]


def send_part(weights, taps, place):
    return pl.pallas_call(
        send_kernel,
        out_shape=jax.ShapeDtypeStruct((2, 80, 512), BF),
        compiler_params=pltpu.CompilerParams(vmem_limit_bytes=VMEM),
        cost_estimate=pl.CostEstimate(flops=1 << 25, bytes_accessed=1 << 19, transcendentals=0),
    )(weights, taps, place)


def by_core(values, place):
    rows = values.shape[0]
    chosen = dot(values.reshape(rows * 4, 2 * K), place).astype(BF)
    return chosen.reshape(rows, 4, 2, K).transpose(2, 0, 1, 3).reshape(2, rows, 512)


def on_device(out_grad, out_weight, signal, gate_input, filter_taps):
    chips, ctx = ("z", "h"), ("z", "h", "c")
    period = SPAN // TOK
    fwd, inv = transforms()
    place = chooser()
    core = lax.axis_index("c").reshape(1)

    message = send_part(out_weight.T, filter_taps.T, place)
    block = lax.all_to_all(message, "c", split_axis=0, concat_axis=0)

    cols = out_grad.reshape(TOK, 2, 2, K).transpose(2, 1, 0, 3)
    block, cols, signal, gate_input = lax.optimization_barrier((block, cols, signal, gate_input))
    weights = lax.all_gather(block, "z", axis=0, tiled=False)
    cols = lax.all_to_all(cols, "h", split_axis=0, concat_axis=0)

    ahead = [(i, i + 1) for i in range(63) if (i + 1) % period]
    window = jnp.concatenate([lax.ppermute(signal[TOK - K :], ctx, ahead), signal], axis=0)
    sig_freq = plain_part(window, fwd[:, :, :N])
    tokens = jnp.concatenate([by_core(signal, place), by_core(gate_input, place)], axis=1)
    tokens = lax.all_to_all(
        tokens.reshape(2, 2, TOK, 512), "c", split_axis=0, concat_axis=0
    )
    ahead = [(i, i + 1) for i in range(31) if (i + 1) % (period // 2)]
    sig_halo = lax.ppermute(tokens[1, 0, TOK - K :], chips, ahead)
    own_freq = front_part(sig_halo, tokens, fwd[:, :, :N])

    cols, sig_freq, own_freq = lax.optimization_barrier((cols, sig_freq, own_freq))
    cols = lax.all_to_all(
        jnp.broadcast_to(cols[None], (8, 2, 2, TOK, K)), ("x", "l"), split_axis=0, concat_axis=0
    )
    cols = lax.all_to_all(
        jnp.broadcast_to(cols[None], (2, 8, 2, 2, TOK, K)), "c", split_axis=0, concat_axis=0
    )

    partial = product(cols, weights)
    mix = lax.all_to_all(
        partial.reshape(2, 2, TOK, 512), "h", split_axis=0, concat_axis=0
    )
    keep, send, first, inner, cross, tap_grad = grad_part(
        core, mix, tokens, own_freq, fwd[:, :, K:N], inv[:, :K]
    )
    tap_grad = lax.all_to_all(tap_grad, chips, split_axis=0, concat_axis=0)
    filter_grad = jnp.sum(tap_grad.astype(F32), axis=0).T

    other = lax.ppermute(send, "c", [(0, 1), (1, 0)])
    follows = [(2 * i + 2, 2 * i + 1) for i in range(31) if (i + 1) % (period // 2)]
    near = lax.ppermute(cross, ctx, follows + [(2 * i + 1, 2 * i) for i in range(32)])
    far = lax.ppermute(first, ctx, [(i + 1, j) for i, j in follows])

    weights, keep = lax.optimization_barrier((weights, keep))
    taps = weights[:, :, 64:, : 2 * K].reshape(16, 2, 16, 2, K).transpose(3, 0, 1, 2, 4)
    more = lax.ppermute(taps, "h", [(0, 1), (1, 0)])
    upper_half = lax.axis_index("h") == 0
    taps = jnp.stack(
        [jnp.where(upper_half, taps, more), jnp.where(upper_half, more, taps)], axis=2
    ).reshape(2, CH, K)

    gate_grad, signal_grad = out_part(
        core, keep, other, inner, near, far, gate_input, sig_freq, taps, fwd, inv[:, K:], place.T
    )
    return signal_grad, gate_grad, filter_grad


def solution(mesh):
    fine = Mesh(mesh.devices.reshape(16, 2, 2, 4, 2), ("z", "h", "c", "x", "l"))
    ctx, tp = ("z", "h", "c"), ("x", "l")
    in_specs = (P(ctx, tp), P(tp, ctx), P(ctx, tp), P(ctx, tp), P(None, tp + ctx))
    out_specs = (P(ctx, tp), P(ctx, tp), P(None, tp + ctx))
    return jax.shard_map(
        on_device, mesh=fine, in_specs=in_specs, out_specs=out_specs, check_vma=False
    )
```

```python
import jax
import jax.numpy as jnp
import numpy as np
from jax import lax
from jax.experimental import pallas as pl
from jax.experimental.pallas import tpu as pltpu
from jax.sharding import Mesh, PartitionSpec as P

K = 128
TOK = 256
CH = 1024
SPAN = 8192
N = K + TOK
HALF = N // 2
TILE = 256
VMEM = 60 * 1024 * 1024

BF = jnp.bfloat16
F32 = jnp.float32
ROWS = ((1,), (0,))
LANES = ((1,), (1,))


def transforms():
    freq = 2.0 * np.pi * (np.arange(HALF) + 0.5) / N
    angle = freq[:, None] * np.arange(N + K)[None, :]
    forward = np.concatenate([np.cos(angle), -np.sin(angle)], axis=0)
    angle = angle[:, :N].T
    inverse = np.concatenate([np.cos(angle), -np.sin(angle)], axis=1) * (2.0 / N)
    return two(forward), two(inverse)


def two(values):
    values = np.asarray(values, np.float32)
    upper = values.astype(jnp.bfloat16)
    lower = (values - upper.astype(np.float32)).astype(jnp.bfloat16)
    return np.stack([upper, lower])


def dot(a, b, dims=ROWS):
    return lax.dot_general(a, b, (dims, ((), ())), preferred_element_type=F32)


def exact_side(matrix, values):
    return dot(matrix[0], values) + dot(matrix[1], values)


def both_sides(matrix, values):
    high = values.astype(BF)
    low = (values - high.astype(F32)).astype(BF)
    return dot(matrix[0], high) + dot(matrix[1], high) + dot(matrix[0], low)


def times(a, b):
    ar, ai, br, bi = a[:HALF], a[HALF:], b[:HALF], b[HALF:]
    return jnp.concatenate([ar * br - ai * bi, ar * bi + ai * br], axis=0)


def times_conj(a, b):
    ar, ai, br, bi = a[:HALF], a[HALF:], b[:HALF], b[HALF:]
    return jnp.concatenate([ar * br + ai * bi, ai * br - ar * bi], axis=0)


def params(limit=VMEM):
    return pltpu.CompilerParams(
        dimension_semantics=("arbitrary",), vmem_limit_bytes=limit
    )


def product_kernel(cols_ref, weight_ref, out_ref):
    weight = weight_ref[:, :, :64].reshape(16 * K, 512)
    rows = jnp.concatenate([cols_ref[0, i, 0, j] for i in range(8) for j in range(2)], axis=1)
    out_ref[0] = dot(rows, weight).astype(BF)


def product(cols, weights):
    return pl.pallas_call(
        product_kernel,
        grid=(4,),
        in_specs=[
            pl.BlockSpec((1, 8, 1, 2, TOK, K), lambda i: (i % 2, 0, i // 2, 0, 0, 0)),
            pl.BlockSpec((16, 2, 80, 512), lambda i: (0, 0, 0, 0)),
        ],
        out_specs=pl.BlockSpec((1, TOK, 512), lambda i: (i, 0, 0)),
        out_shape=jax.ShapeDtypeStruct((4, TOK, 512), BF),
        compiler_params=params(),
        cost_estimate=pl.CostEstimate(
            flops=2 * 1024 * 2048 * 512, bytes_accessed=8 << 20, transcendentals=0
        ),
    )(cols, weights)


def whole(shape):
    return pl.BlockSpec(shape, lambda j: (0,) * len(shape))


def scalar():
    return pl.BlockSpec(memory_space=pltpu.SMEM)


TILES = 512 // K
PAIR = pl.BlockSpec((1, TOK, 2 * K), lambda j: (j, 0, 0))
FREQ = pl.BlockSpec((1, N, 2 * K), lambda j: (j, 0, 0))


def plain_kernel(window_ref, forward_ref, freq_ref):
    freq_ref[...] = exact_side(forward_ref, window_ref[...])


def plain_part(window, forward):
    tile = pl.BlockSpec((N, 2 * K), lambda j: (0, j))
    return pl.pallas_call(
        plain_kernel,
        grid=(TILES,),
        in_specs=[tile, whole((2, N, N))],
        out_specs=tile,
        out_shape=jax.ShapeDtypeStruct((N, CH), F32),
        compiler_params=params(),
        cost_estimate=pl.CostEstimate(
            flops=2 * CH * N * 2 * N, bytes_accessed=3 << 20, transcendentals=0
        ),
    )(window, forward)


def front_kernel(halo_ref, tok_ref, forward_ref, freq_ref):
    first, second = tok_ref[0, 0], tok_ref[1, 0]
    window = jnp.concatenate(
        [
            jnp.concatenate([halo_ref[...], first[K:]], axis=1),
            jnp.concatenate([first[:K], second[:K]], axis=1),
            jnp.concatenate([first[K:], second[K:]], axis=1),
        ],
        axis=0,
    )
    freq_ref[0] = exact_side(forward_ref, window)


def front_part(halo, tokens, forward):
    return pl.pallas_call(
        front_kernel,
        grid=(TILES,),
        in_specs=[
            pl.BlockSpec((K, K), lambda j: (0, j)),
            pl.BlockSpec((2, 1, TOK, K), lambda j: (0, 0, 0, j)),
            whole((2, N, N)),
        ],
        out_specs=FREQ,
        out_shape=jax.ShapeDtypeStruct((TILES, N, 2 * K), F32),
        compiler_params=params(),
        cost_estimate=pl.CostEstimate(
            flops=2 * CH * N * 2 * N, bytes_accessed=3 << 20, transcendentals=0
        ),
    )(halo, tokens, forward)


def grad_kernel(
    core_ref,
    mix_ref,
    tok_ref,
    freq_ref,
    own_ref,
    lag_ref,
    keep_ref,
    send_ref,
    first_ref,
    inner_ref,
    cross_ref,
    tap_ref,
):
    is_first = core_ref[0] == 0
    early = (mix_ref[0, 0].astype(F32) + mix_ref[1, 0].astype(F32)).astype(BF).astype(F32)
    late = (mix_ref[0, 1].astype(F32) + mix_ref[1, 1].astype(F32)).astype(BF).astype(F32)
    keep_ref[...] = jnp.where(is_first, early, late).astype(BF)
    send_ref[...] = jnp.where(is_first, late, early).astype(BF)
    early = early * tok_ref[0, 0].astype(F32)
    late = late * tok_ref[1, 0].astype(F32)
    first_ref[...] = early[:K].astype(BF)
    inner_ref[...] = late[:K].astype(BF)
    cross_ref[...] = jnp.where(is_first, early[:K], late[:K]).astype(BF)
    conv_grad = jnp.concatenate([early, late], axis=1).astype(BF)
    cross = times_conj(exact_side(own_ref, conv_grad), freq_ref[0])
    taps = both_sides(lag_ref, cross[:, :K] + cross[:, K:])
    tap_ref[...] = taps.T.reshape(8, 16, K).astype(tap_ref.dtype)


def grad_part(core, mix, tokens, sig_freq, own, lag):
    head = pl.BlockSpec((K, K), lambda j: (0, j))
    half = pl.BlockSpec((TOK, K), lambda j: (0, j))
    return pl.pallas_call(
        grad_kernel,
        grid=(TILES,),
        in_specs=[
            scalar(),
            pl.BlockSpec((2, 2, TOK, K), lambda j: (0, 0, 0, j)),
            pl.BlockSpec((2, 1, TOK, K), lambda j: (0, 1, 0, j)),
            FREQ,
            whole((2, N, TOK)),
            whole((2, K, N)),
        ],
        out_specs=[half, half, head, head, head, pl.BlockSpec((8, 16, K), lambda j: (j, 0, 0))],
        out_shape=[jax.ShapeDtypeStruct((TOK, 512), BF)] * 2
        + [jax.ShapeDtypeStruct((K, 512), BF)] * 3
        + [jax.ShapeDtypeStruct((32, 16, K), BF)],
        compiler_params=params(32 << 20),
        cost_estimate=pl.CostEstimate(
            flops=2 * CH * N * (2 * TOK + 2 * K), bytes_accessed=5 << 20, transcendentals=0
        ),
    )(core, mix, tokens, sig_freq, own, lag)


def conv_kernel(freq_ref, tap_ref, forward_ref, inv_ref, tap_freq_ref, conv_ref):
    upper, lower = tap_ref[0], tap_ref[1]
    high, low = forward_ref[0], forward_ref[1]
    tap_freq = dot(high, upper, LANES) + dot(low, upper, LANES) + dot(high, lower, LANES)
    tap_freq_ref[...] = tap_freq
    conv_ref[...] = both_sides(inv_ref, times(freq_ref[...], tap_freq))


def wide_tile(rows):
    return pl.BlockSpec((rows, 2 * K), lambda j: (0, j))


def conv_part(sig_freq, taps, forward, inv):
    return pl.pallas_call(
        conv_kernel,
        grid=(TILES,),
        in_specs=[
            wide_tile(N),
            pl.BlockSpec((2, 2 * K, K), lambda j: (0, j, 0)),
            whole((2, N, K)),
            whole((2, TOK, N)),
        ],
        out_specs=[wide_tile(N), wide_tile(TOK)],
        out_shape=[jax.ShapeDtypeStruct((N, CH), F32), jax.ShapeDtypeStruct((TOK, CH), F32)],
        compiler_params=params(),
        cost_estimate=pl.CostEstimate(flops=1024, bytes_accessed=1024, transcendentals=0),
    )(sig_freq, taps, forward, inv)


def out_kernel(
    core_ref,
    keep_ref,
    other_ref,
    inner_ref,
    near_ref,
    far_ref,
    gate_in_ref,
    conv_ref,
    tap_freq_ref,
    forward_ref,
    inv_ref,
    place_ref,
    gate_ref,
    sig_ref,
):
    is_first = core_ref[0] == 0

    def joined(left, right):
        return dot(jnp.concatenate([left, right], axis=1), place_ref[...])

    keep, other = keep_ref[...], other_ref[...]
    mixed = joined(jnp.where(is_first, keep, other), jnp.where(is_first, other, keep))
    near = near_ref[...]
    halo = joined(
        jnp.where(is_first, inner_ref[...], near), jnp.where(is_first, near, far_ref[...])
    ).astype(BF)
    gate_ref[...] = (mixed * conv_ref[...]).astype(BF)
    conv_grad = (mixed * gate_in_ref[...].astype(F32)).astype(BF)
    full = exact_side(forward_ref, jnp.concatenate([conv_grad, halo], axis=0))
    sig_ref[...] = both_sides(inv_ref, times_conj(full, tap_freq_ref[...])).astype(BF)


def out_part(core, keep, other, inner, near, far, gate, conv, tap_freq, forward, inv, place):
    head = pl.BlockSpec((K, K), lambda j: (0, j))
    half = pl.BlockSpec((TOK, K), lambda j: (0, j))
    return pl.pallas_call(
        out_kernel,
        grid=(TILES,),
        in_specs=[
            scalar(),
            half,
            half,
            head,
            head,
            head,
            wide_tile(TOK),
            wide_tile(TOK),
            wide_tile(N),
            whole((2, N, N)),
            whole((2, TOK, N)),
            whole((2 * K, 2 * K)),
        ],
        out_specs=[wide_tile(TOK), wide_tile(TOK)],
        out_shape=[jax.ShapeDtypeStruct((TOK, CH), BF)] * 2,
        compiler_params=params(),
        cost_estimate=pl.CostEstimate(flops=1024, bytes_accessed=1024, transcendentals=0),
    )(core, keep, other, inner, near, far, gate, conv, tap_freq, forward, inv, place)


def chooser():
    source = np.arange(2 * K).reshape(8, 2, 16).transpose(1, 0, 2).reshape(-1)
    matrix = np.zeros((2 * K, 2 * K), np.float32)
    matrix[source, np.arange(2 * K)] = 1.0
    return matrix.astype(jnp.bfloat16)


def send_kernel(weight_ref, tap_ref, place_ref, out_ref):
    out_ref[...] = jnp.zeros_like(out_ref)
    taps = tap_ref[...]
    high = taps.astype(BF)
    low = (taps - high.astype(F32)).astype(BF)
    for c in range(2):
        out_ref[c, 64:, :K] = high
        out_ref[c, 64:, K : 2 * K] = low
    for i in range(4):
        lanes = slice(i * 2 * K, (i + 1) * 2 * K)
        chosen = dot(weight_ref[:, lanes], place_ref[...]).astype(BF)
        out_ref[0, :64, i * K : (i + 1) * K] = chosen[:, :K]
        out_ref[1, :64, i * K : (i + 1) * K] = chosen[:, K:]


def send_part(weights, taps, place):
    return pl.pallas_call(
        send_kernel,
        out_shape=jax.ShapeDtypeStruct((2, 80, 512), BF),
        compiler_params=pltpu.CompilerParams(vmem_limit_bytes=VMEM),
        cost_estimate=pl.CostEstimate(flops=1 << 25, bytes_accessed=1 << 19, transcendentals=0),
    )(weights, taps, place)


def by_core(values, place):
    rows = values.shape[0]
    chosen = dot(values.reshape(rows * 4, 2 * K), place).astype(BF)
    return chosen.reshape(rows, 4, 2, K).transpose(2, 0, 1, 3).reshape(2, rows, 512)


def on_device(out_grad, out_weight, signal, gate_input, filter_taps):
    chips, ctx = ("z", "h"), ("z", "h", "c")
    period = SPAN // TOK
    fwd, inv = transforms()
    place = chooser()
    core = lax.axis_index("c").reshape(1)

    message = send_part(out_weight.T, filter_taps.T, place)
    block = lax.all_to_all(message, "c", split_axis=0, concat_axis=0)

    cols = out_grad.reshape(TOK, 2, 2, K).transpose(2, 1, 0, 3)
    block, cols, signal, gate_input = lax.optimization_barrier((block, cols, signal, gate_input))
    weights = lax.all_gather(block, "z", axis=0, tiled=False)
    cols = lax.all_to_all(cols, "h", split_axis=0, concat_axis=0)

    ahead = [(i, i + 1) for i in range(63) if (i + 1) % period]
    window = jnp.concatenate([lax.ppermute(signal[TOK - K :], ctx, ahead), signal], axis=0)
    sig_freq = plain_part(window, fwd[:, :, :N])
    tokens = jnp.concatenate([by_core(signal, place), by_core(gate_input, place)], axis=1)
    tokens = lax.all_to_all(
        tokens.reshape(2, 2, TOK, 512), "c", split_axis=0, concat_axis=0
    )
    ahead = [(i, i + 1) for i in range(31) if (i + 1) % (period // 2)]
    sig_halo = lax.ppermute(tokens[1, 0, TOK - K :], chips, ahead)
    own_freq = front_part(sig_halo, tokens, fwd[:, :, :N])

    cols, sig_freq, own_freq = lax.optimization_barrier((cols, sig_freq, own_freq))
    cols = lax.all_to_all(
        jnp.broadcast_to(cols[None], (8, 2, 2, TOK, K)), ("x", "l"), split_axis=0, concat_axis=0
    )
    cols = lax.all_to_all(
        jnp.broadcast_to(cols[None], (2, 8, 2, 2, TOK, K)), "c", split_axis=0, concat_axis=0
    )

    partial = product(cols, weights)
    weights, partial = lax.optimization_barrier((weights, partial))
    mix = lax.all_to_all(
        partial.reshape(2, 2, TOK, 512), "h", split_axis=0, concat_axis=0
    )
    keep, send, first, inner, cross, tap_grad = grad_part(
        core, mix, tokens, own_freq, fwd[:, :, K:N], inv[:, :K]
    )
    tap_grad = lax.all_to_all(tap_grad, chips, split_axis=0, concat_axis=0)
    filter_grad = jnp.sum(tap_grad.astype(F32), axis=0).T

    other = lax.ppermute(send, "c", [(0, 1), (1, 0)])
    follows = [(2 * i + 2, 2 * i + 1) for i in range(31) if (i + 1) % (period // 2)]
    near = lax.ppermute(cross, ctx, follows + [(2 * i + 1, 2 * i) for i in range(32)])
    far = lax.ppermute(first, ctx, [(i + 1, j) for i, j in follows])

    taps = weights[:, :, 64:, : 2 * K].reshape(16, 2, 16, 2, K).transpose(3, 0, 1, 2, 4)
    more = lax.ppermute(taps, "h", [(0, 1), (1, 0)])
    upper_half = lax.axis_index("h") == 0
    taps = jnp.stack(
        [jnp.where(upper_half, taps, more), jnp.where(upper_half, more, taps)], axis=2
    ).reshape(2, CH, K)

    tap_freq, conv = conv_part(sig_freq, taps, fwd[:, :, :K], inv[:, K:])
    gate_grad, signal_grad = out_part(
        core,
        keep,
        other,
        inner,
        near,
        far,
        gate_input,
        conv,
        tap_freq,
        fwd[:, :, K:],
        inv[:, K:],
        place.T,
    )
    return signal_grad, gate_grad, filter_grad


def solution(mesh):
    fine = Mesh(mesh.devices.reshape(16, 2, 2, 4, 2), ("z", "h", "c", "x", "l"))
    ctx, tp = ("z", "h", "c"), ("x", "l")
    in_specs = (P(ctx, tp), P(tp, ctx), P(ctx, tp), P(ctx, tp), P(None, tp + ctx))
    out_specs = (P(ctx, tp), P(ctx, tp), P(None, tp + ctx))
    return jax.shard_map(
        on_device, mesh=fine, in_specs=in_specs, out_specs=out_specs, check_vma=False
    )
```

```python
import jax
import jax.numpy as jnp
import numpy as np
from jax import lax
from jax.experimental import pallas as pl
from jax.experimental.pallas import tpu as pltpu
from jax.sharding import Mesh, PartitionSpec as P

K = 128
TOK = 256
CH = 1024
SPAN = 8192
N = K + TOK
HALF = N // 2
TILE = 256
VMEM = 60 * 1024 * 1024

BF = jnp.bfloat16
F32 = jnp.float32
ROWS = ((1,), (0,))
LANES = ((1,), (1,))


def transforms():
    freq = 2.0 * np.pi * (np.arange(HALF) + 0.5) / N
    angle = freq[:, None] * np.arange(N + K)[None, :]
    forward = np.concatenate([np.cos(angle), -np.sin(angle)], axis=0)
    angle = angle[:, :N].T
    inverse = np.concatenate([np.cos(angle), -np.sin(angle)], axis=1) * (2.0 / N)
    return two(forward), two(inverse)


def two(values):
    values = np.asarray(values, np.float32)
    upper = values.astype(jnp.bfloat16)
    lower = (values - upper.astype(np.float32)).astype(jnp.bfloat16)
    return np.stack([upper, lower])


def dot(a, b, dims=ROWS):
    return lax.dot_general(a, b, (dims, ((), ())), preferred_element_type=F32)


def exact_side(matrix, values):
    return dot(matrix[0], values) + dot(matrix[1], values)


def both_sides(matrix, values):
    high = values.astype(BF)
    low = (values - high.astype(F32)).astype(BF)
    return dot(matrix[0], high) + dot(matrix[1], high) + dot(matrix[0], low)


def times(a, b):
    ar, ai, br, bi = a[:HALF], a[HALF:], b[:HALF], b[HALF:]
    return jnp.concatenate([ar * br - ai * bi, ar * bi + ai * br], axis=0)


def times_conj(a, b):
    ar, ai, br, bi = a[:HALF], a[HALF:], b[:HALF], b[HALF:]
    return jnp.concatenate([ar * br + ai * bi, ai * br - ar * bi], axis=0)


def params():
    return pltpu.CompilerParams(
        dimension_semantics=("arbitrary",), vmem_limit_bytes=VMEM
    )


def product_kernel(cols_ref, weight_ref, out_ref):
    weight = weight_ref[:, :, :64].reshape(16 * K, 512)
    rows = jnp.concatenate([cols_ref[0, i, 0, j] for i in range(8) for j in range(2)], axis=1)
    out_ref[0] = dot(rows, weight).astype(BF)


def product(cols, weights):
    return pl.pallas_call(
        product_kernel,
        grid=(4,),
        in_specs=[
            pl.BlockSpec((1, 8, 1, 2, TOK, K), lambda i: (i % 2, 0, i // 2, 0, 0, 0)),
            pl.BlockSpec((16, 2, 80, 512), lambda i: (0, 0, 0, 0)),
        ],
        out_specs=pl.BlockSpec((1, TOK, 512), lambda i: (i, 0, 0)),
        out_shape=jax.ShapeDtypeStruct((4, TOK, 512), BF),
        compiler_params=params(),
        cost_estimate=pl.CostEstimate(
            flops=2 * 1024 * 2048 * 512, bytes_accessed=8 << 20, transcendentals=0
        ),
    )(cols, weights)


def whole(shape):
    return pl.BlockSpec(shape, lambda j: (0,) * len(shape))


def scalar():
    return pl.BlockSpec(memory_space=pltpu.SMEM)


TILES = 512 // K
PAIR = pl.BlockSpec((1, TOK, 2 * K), lambda j: (j, 0, 0))
FREQ = pl.BlockSpec((1, N, 2 * K), lambda j: (j, 0, 0))


def plain_kernel(window_ref, forward_ref, freq_ref):
    freq_ref[...] = exact_side(forward_ref, window_ref[...])


def plain_part(window, forward):
    tile = pl.BlockSpec((N, 2 * K), lambda j: (0, j))
    return pl.pallas_call(
        plain_kernel,
        grid=(TILES,),
        in_specs=[tile, whole((2, N, N))],
        out_specs=tile,
        out_shape=jax.ShapeDtypeStruct((N, CH), F32),
        compiler_params=params(),
        cost_estimate=pl.CostEstimate(
            flops=2 * CH * N * 2 * N, bytes_accessed=3 << 20, transcendentals=0
        ),
    )(window, forward)


def front_kernel(halo_ref, tok_ref, forward_ref, freq_ref):
    first, second = tok_ref[0, 0], tok_ref[1, 0]
    window = jnp.concatenate(
        [
            jnp.concatenate([halo_ref[...], first[K:]], axis=1),
            jnp.concatenate([first[:K], second[:K]], axis=1),
            jnp.concatenate([first[K:], second[K:]], axis=1),
        ],
        axis=0,
    )
    freq_ref[0] = exact_side(forward_ref, window)


def front_part(halo, tokens, forward):
    return pl.pallas_call(
        front_kernel,
        grid=(TILES,),
        in_specs=[
            pl.BlockSpec((K, K), lambda j: (0, j)),
            pl.BlockSpec((2, 1, TOK, K), lambda j: (0, 0, 0, j)),
            whole((2, N, N)),
        ],
        out_specs=FREQ,
        out_shape=jax.ShapeDtypeStruct((TILES, N, 2 * K), F32),
        compiler_params=params(),
        cost_estimate=pl.CostEstimate(
            flops=2 * CH * N * 2 * N, bytes_accessed=3 << 20, transcendentals=0
        ),
    )(halo, tokens, forward)


def grad_kernel(
    core_ref,
    mix_ref,
    tok_ref,
    freq_ref,
    own_ref,
    lag_ref,
    keep_ref,
    send_ref,
    first_ref,
    inner_ref,
    cross_ref,
    tap_ref,
):
    is_first = core_ref[0] == 0
    early = (mix_ref[0, 0].astype(F32) + mix_ref[1, 0].astype(F32)).astype(BF).astype(F32)
    late = (mix_ref[0, 1].astype(F32) + mix_ref[1, 1].astype(F32)).astype(BF).astype(F32)
    keep_ref[...] = jnp.where(is_first, early, late).astype(BF)
    send_ref[...] = jnp.where(is_first, late, early).astype(BF)
    early = early * tok_ref[0, 0].astype(F32)
    late = late * tok_ref[1, 0].astype(F32)
    first_ref[...] = early[:K].astype(BF)
    inner_ref[...] = late[:K].astype(BF)
    cross_ref[...] = jnp.where(is_first, early[:K], late[:K]).astype(BF)
    conv_grad = jnp.concatenate([early, late], axis=1).astype(BF)
    cross = times_conj(exact_side(own_ref, conv_grad), freq_ref[0])
    taps = both_sides(lag_ref, cross[:, :K] + cross[:, K:])
    tap_ref[...] = taps.T.reshape(8, 16, K).astype(tap_ref.dtype)


def grad_part(core, mix, tokens, sig_freq, own, lag):
    head = pl.BlockSpec((K, K), lambda j: (0, j))
    half = pl.BlockSpec((TOK, K), lambda j: (0, j))
    return pl.pallas_call(
        grad_kernel,
        grid=(TILES,),
        in_specs=[
            scalar(),
            pl.BlockSpec((2, 2, TOK, K), lambda j: (0, 0, 0, j)),
            pl.BlockSpec((2, 1, TOK, K), lambda j: (0, 1, 0, j)),
            FREQ,
            whole((2, N, TOK)),
            whole((2, K, N)),
        ],
        out_specs=[half, half, head, head, head, pl.BlockSpec((8, 16, K), lambda j: (j, 0, 0))],
        out_shape=[jax.ShapeDtypeStruct((TOK, 512), BF)] * 2
        + [jax.ShapeDtypeStruct((K, 512), BF)] * 3
        + [jax.ShapeDtypeStruct((32, 16, K), BF)],
        compiler_params=params(),
        cost_estimate=pl.CostEstimate(
            flops=2 * CH * N * (2 * TOK + 2 * K), bytes_accessed=5 << 20, transcendentals=0
        ),
    )(core, mix, tokens, sig_freq, own, lag)


def out_kernel(
    core_ref,
    keep_ref,
    other_ref,
    inner_ref,
    near_ref,
    far_ref,
    gate_in_ref,
    freq_ref,
    tap_ref,
    forward_ref,
    inv_ref,
    place_ref,
    gate_ref,
    sig_ref,
):
    is_first = core_ref[0] == 0

    def joined(left, right):
        return dot(jnp.concatenate([left, right], axis=1), place_ref[...])

    keep, other = keep_ref[...], other_ref[...]
    mixed = joined(jnp.where(is_first, keep, other), jnp.where(is_first, other, keep))
    near = near_ref[...]
    halo = joined(
        jnp.where(is_first, inner_ref[...], near), jnp.where(is_first, near, far_ref[...])
    ).astype(BF)
    conv_grad = (mixed * gate_in_ref[...].astype(F32)).astype(BF)
    window = jnp.concatenate([conv_grad, halo], axis=0)
    full = exact_side(forward_ref[:, :, K:], window)
    upper, lower = tap_ref[0], tap_ref[1]
    high, low = forward_ref[0, :, :K], forward_ref[1, :, :K]
    tap_freq = dot(high, upper, LANES) + dot(low, upper, LANES) + dot(high, lower, LANES)
    conv_out = both_sides(inv_ref, times(freq_ref[...], tap_freq))
    gate_ref[...] = (mixed * conv_out).astype(BF)
    sig_ref[...] = both_sides(inv_ref, times_conj(full, tap_freq)).astype(BF)


def out_part(core, keep, other, inner, near, far, gate, sig_freq, taps, forward, inv, place):
    head = pl.BlockSpec((K, K), lambda j: (0, j))
    half = pl.BlockSpec((TOK, K), lambda j: (0, j))

    def tile(rows):
        return pl.BlockSpec((rows, 2 * K), lambda j: (0, j))

    return pl.pallas_call(
        out_kernel,
        grid=(TILES,),
        in_specs=[
            scalar(),
            half,
            half,
            head,
            head,
            head,
            tile(TOK),
            tile(N),
            pl.BlockSpec((2, 2 * K, K), lambda j: (0, j, 0)),
            whole((2, N, N + K)),
            whole((2, TOK, N)),
            whole((2 * K, 2 * K)),
        ],
        out_specs=[tile(TOK), tile(TOK)],
        out_shape=[jax.ShapeDtypeStruct((TOK, CH), BF)] * 2,
        compiler_params=params(),
        cost_estimate=pl.CostEstimate(
            flops=1024, bytes_accessed=1024, transcendentals=0
        ),
    )(core, keep, other, inner, near, far, gate, sig_freq, taps, forward, inv, place)


def chooser():
    source = np.arange(2 * K).reshape(8, 2, 16).transpose(1, 0, 2).reshape(-1)
    matrix = np.zeros((2 * K, 2 * K), np.float32)
    matrix[source, np.arange(2 * K)] = 1.0
    return matrix.astype(jnp.bfloat16)


def send_kernel(weight_ref, tap_ref, place_ref, out_ref):
    out_ref[...] = jnp.zeros_like(out_ref)
    taps = tap_ref[...]
    high = taps.astype(BF)
    low = (taps - high.astype(F32)).astype(BF)
    for c in range(2):
        out_ref[c, 64:, :K] = high
        out_ref[c, 64:, K : 2 * K] = low
    for i in range(4):
        lanes = slice(i * 2 * K, (i + 1) * 2 * K)
        chosen = dot(weight_ref[:, lanes], place_ref[...]).astype(BF)
        out_ref[0, :64, i * K : (i + 1) * K] = chosen[:, :K]
        out_ref[1, :64, i * K : (i + 1) * K] = chosen[:, K:]


def send_part(weights, taps, place):
    return pl.pallas_call(
        send_kernel,
        out_shape=jax.ShapeDtypeStruct((2, 80, 512), BF),
        compiler_params=pltpu.CompilerParams(vmem_limit_bytes=VMEM),
        cost_estimate=pl.CostEstimate(flops=1 << 25, bytes_accessed=1 << 19, transcendentals=0),
    )(weights, taps, place)


def by_core(values, place):
    rows = values.shape[0]
    chosen = dot(values.reshape(rows * 4, 2 * K), place).astype(BF)
    return chosen.reshape(rows, 4, 2, K).transpose(2, 0, 1, 3).reshape(2, rows, 512)


def on_device(out_grad, out_weight, signal, gate_input, filter_taps):
    chips, ctx = ("z", "h"), ("z", "h", "c")
    period = SPAN // TOK
    fwd, inv = transforms()
    place = chooser()
    core = lax.axis_index("c").reshape(1)

    message = send_part(out_weight.T, filter_taps.T, place)
    block = lax.all_to_all(message, "c", split_axis=0, concat_axis=0)

    cols = out_grad.reshape(TOK, 2, 2, K).transpose(2, 1, 0, 3)
    block, cols, signal, gate_input = lax.optimization_barrier((block, cols, signal, gate_input))
    weights = lax.all_gather(block, "z", axis=0, tiled=False)
    cols = lax.all_to_all(cols, "h", split_axis=0, concat_axis=0)

    ahead = [(i, i + 1) for i in range(63) if (i + 1) % period]
    window = jnp.concatenate([lax.ppermute(signal[TOK - K :], ctx, ahead), signal], axis=0)
    sig_freq = plain_part(window, fwd[:, :, :N])
    tokens = jnp.concatenate([by_core(signal, place), by_core(gate_input, place)], axis=1)
    tokens = lax.all_to_all(
        tokens.reshape(2, 2, TOK, 512), "c", split_axis=0, concat_axis=0
    )
    ahead = [(i, i + 1) for i in range(31) if (i + 1) % (period // 2)]
    sig_halo = lax.ppermute(tokens[1, 0, TOK - K :], chips, ahead)
    own_freq = front_part(sig_halo, tokens, fwd[:, :, :N])

    cols, sig_freq, own_freq = lax.optimization_barrier((cols, sig_freq, own_freq))
    cols = lax.all_to_all(
        jnp.broadcast_to(cols[None], (8, 2, 2, TOK, K)), ("x", "l"), split_axis=0, concat_axis=0
    )
    cols = lax.all_to_all(
        jnp.broadcast_to(cols[None], (2, 8, 2, 2, TOK, K)), "c", split_axis=0, concat_axis=0
    )

    partial = product(cols, weights)
    weights, partial = lax.optimization_barrier((weights, partial))
    mix = lax.all_to_all(
        partial.reshape(2, 2, TOK, 512), "h", split_axis=0, concat_axis=0
    )
    keep, send, first, inner, cross, tap_grad = grad_part(
        core, mix, tokens, own_freq, fwd[:, :, K:N], inv[:, :K]
    )
    tap_grad = lax.all_to_all(tap_grad, chips, split_axis=0, concat_axis=0)
    filter_grad = jnp.sum(tap_grad.astype(F32), axis=0).T

    other = lax.ppermute(send, "c", [(0, 1), (1, 0)])
    follows = [(2 * i + 2, 2 * i + 1) for i in range(31) if (i + 1) % (period // 2)]
    near = lax.ppermute(cross, ctx, follows + [(2 * i + 1, 2 * i) for i in range(32)])
    far = lax.ppermute(first, ctx, [(i + 1, j) for i, j in follows])

    taps = weights[:, :, 64:, : 2 * K].reshape(16, 2, 16, 2, K).transpose(3, 0, 1, 2, 4)
    more = lax.ppermute(taps, "h", [(0, 1), (1, 0)])
    upper_half = lax.axis_index("h") == 0
    taps = jnp.stack(
        [jnp.where(upper_half, taps, more), jnp.where(upper_half, more, taps)], axis=2
    ).reshape(2, CH, K)

    gate_grad, signal_grad = out_part(
        core, keep, other, inner, near, far, gate_input, sig_freq, taps, fwd, inv[:, K:], place.T
    )
    return signal_grad, gate_grad, filter_grad


def solution(mesh):
    fine = Mesh(mesh.devices.reshape(16, 2, 2, 4, 2), ("z", "h", "c", "x", "l"))
    ctx, tp = ("z", "h", "c"), ("x", "l")
    in_specs = (P(ctx, tp), P(tp, ctx), P(ctx, tp), P(ctx, tp), P(None, tp + ctx))
    out_specs = (P(ctx, tp), P(ctx, tp), P(None, tp + ctx))
    return jax.shard_map(
        on_device, mesh=fine, in_specs=in_specs, out_specs=out_specs, check_vma=False
    )
```

```python
import jax
import jax.numpy as jnp
import numpy as np
from jax import lax
from jax.experimental import pallas as pl
from jax.experimental.pallas import tpu as pltpu
from jax.sharding import Mesh, PartitionSpec as P

K = 128
TOK = 256
CH = 1024
SPAN = 8192
N = K + TOK
HALF = N // 2
TILE = 256
VMEM = 60 * 1024 * 1024

BF = jnp.bfloat16
F32 = jnp.float32
ROWS = ((1,), (0,))
LANES = ((1,), (1,))


def transforms():
    freq = 2.0 * np.pi * (np.arange(HALF) + 0.5) / N
    angle = freq[:, None] * np.arange(N + K)[None, :]
    forward = np.concatenate([np.cos(angle), -np.sin(angle)], axis=0)
    angle = angle[:, :N].T
    inverse = np.concatenate([np.cos(angle), -np.sin(angle)], axis=1) * (2.0 / N)
    return two(forward), two(inverse)


def two(values):
    values = np.asarray(values, np.float32)
    upper = values.astype(jnp.bfloat16)
    lower = (values - upper.astype(np.float32)).astype(jnp.bfloat16)
    return np.stack([upper, lower])


def dot(a, b, dims=ROWS):
    return lax.dot_general(a, b, (dims, ((), ())), preferred_element_type=F32)


def exact_side(matrix, values):
    return dot(
        jnp.concatenate([matrix[0], matrix[1]], axis=1),
        jnp.concatenate([values, values], axis=0),
    )


def both_sides(matrix, values):
    high = values.astype(BF)
    low = (values - high.astype(F32)).astype(BF)
    return dot(
        jnp.concatenate([matrix[0], matrix[1], matrix[0]], axis=1),
        jnp.concatenate([high, high, low], axis=0),
    )


def times(a, b):
    ar, ai, br, bi = a[:HALF], a[HALF:], b[:HALF], b[HALF:]
    return jnp.concatenate([ar * br - ai * bi, ar * bi + ai * br], axis=0)


def times_conj(a, b):
    ar, ai, br, bi = a[:HALF], a[HALF:], b[:HALF], b[HALF:]
    return jnp.concatenate([ar * br + ai * bi, ai * br - ar * bi], axis=0)


def params(limit=VMEM):
    return pltpu.CompilerParams(
        dimension_semantics=("arbitrary",), vmem_limit_bytes=limit
    )


def product_kernel(cols_ref, weight_ref, out_ref):
    weight = weight_ref[:, :, :64].reshape(16 * K, 512)
    for b in range(2):
        rows = jnp.concatenate([cols_ref[b, i, 0, j] for i in range(8) for j in range(2)], axis=1)
        out_ref[b] = dot(rows, weight).astype(BF)


def product(cols, weights):
    return pl.pallas_call(
        product_kernel,
        grid=(2,),
        in_specs=[
            pl.BlockSpec((2, 8, 1, 2, TOK, K), lambda i: (0, 0, i, 0, 0, 0)),
            pl.BlockSpec((16, 2, 80, 512), lambda i: (0, 0, 0, 0)),
        ],
        out_specs=pl.BlockSpec((2, TOK, 512), lambda i: (i, 0, 0)),
        out_shape=jax.ShapeDtypeStruct((4, TOK, 512), BF),
        compiler_params=params(),
        cost_estimate=pl.CostEstimate(
            flops=2 * 1024 * 2048 * 512, bytes_accessed=8 << 20, transcendentals=0
        ),
    )(cols, weights)


def whole(shape):
    return pl.BlockSpec(shape, lambda j: (0,) * len(shape))


def scalar():
    return pl.BlockSpec(memory_space=pltpu.SMEM)


L = 256
TILES = 512 // L
PAIR = pl.BlockSpec((1, TOK, 2 * K), lambda j: (j, 0, 0))
FREQ = pl.BlockSpec((1, N, 2 * L), lambda j: (j, 0, 0))


def plain_kernel(window_ref, forward_ref, freq_ref):
    freq_ref[...] = exact_side(forward_ref, window_ref[...])


def plain_part(window, forward):
    tile = pl.BlockSpec((N, 2 * L), lambda j: (0, j))
    return pl.pallas_call(
        plain_kernel,
        grid=(TILES,),
        in_specs=[tile, whole((2, N, N))],
        out_specs=tile,
        out_shape=jax.ShapeDtypeStruct((N, CH), F32),
        compiler_params=params(),
        cost_estimate=pl.CostEstimate(
            flops=2 * CH * N * 2 * N, bytes_accessed=3 << 20, transcendentals=0
        ),
    )(window, forward)


def front_kernel(halo_ref, tok_ref, forward_ref, freq_ref):
    first, second = tok_ref[0, 0], tok_ref[1, 0]
    window = jnp.concatenate(
        [
            jnp.concatenate([halo_ref[...], first[K:]], axis=1),
            jnp.concatenate([first[:K], second[:K]], axis=1),
            jnp.concatenate([first[K:], second[K:]], axis=1),
        ],
        axis=0,
    )
    freq_ref[0] = exact_side(forward_ref, window)


def front_part(halo, tokens, forward):
    return pl.pallas_call(
        front_kernel,
        grid=(TILES,),
        in_specs=[
            pl.BlockSpec((K, L), lambda j: (0, j)),
            pl.BlockSpec((2, 1, TOK, L), lambda j: (0, 0, 0, j)),
            whole((2, N, N)),
        ],
        out_specs=FREQ,
        out_shape=jax.ShapeDtypeStruct((TILES, N, 2 * L), F32),
        compiler_params=params(),
        cost_estimate=pl.CostEstimate(
            flops=2 * CH * N * 2 * N, bytes_accessed=3 << 20, transcendentals=0
        ),
    )(halo, tokens, forward)


def grad_kernel(
    core_ref,
    mix_ref,
    tok_ref,
    freq_ref,
    own_ref,
    lag_ref,
    keep_ref,
    send_ref,
    first_ref,
    inner_ref,
    cross_ref,
    tap_ref,
):
    is_first = core_ref[0] == 0
    early = (mix_ref[0, 0].astype(F32) + mix_ref[1, 0].astype(F32)).astype(BF).astype(F32)
    late = (mix_ref[0, 1].astype(F32) + mix_ref[1, 1].astype(F32)).astype(BF).astype(F32)
    keep_ref[...] = jnp.where(is_first, early, late).astype(BF)
    send_ref[...] = jnp.where(is_first, late, early).astype(BF)
    early = early * tok_ref[0, 0].astype(F32)
    late = late * tok_ref[1, 0].astype(F32)
    first_ref[...] = early[:K].astype(BF)
    inner_ref[...] = late[:K].astype(BF)
    cross_ref[...] = jnp.where(is_first, early[:K], late[:K]).astype(BF)
    conv_grad = jnp.concatenate([early, late], axis=1).astype(BF)
    cross = times_conj(exact_side(own_ref, conv_grad), freq_ref[0])
    taps = both_sides(lag_ref, cross[:, :L] + cross[:, L:])
    tap_ref[...] = taps.T.reshape(L // 16, 16, K).astype(tap_ref.dtype)


def grad_part(core, mix, tokens, sig_freq, own, lag):
    head = pl.BlockSpec((K, L), lambda j: (0, j))
    half = pl.BlockSpec((TOK, L), lambda j: (0, j))
    return pl.pallas_call(
        grad_kernel,
        grid=(TILES,),
        in_specs=[
            scalar(),
            pl.BlockSpec((2, 2, TOK, L), lambda j: (0, 0, 0, j)),
            pl.BlockSpec((2, 1, TOK, L), lambda j: (0, 1, 0, j)),
            FREQ,
            whole((2, N, TOK)),
            whole((2, K, N)),
        ],
        out_specs=[half, half, head, head, head, pl.BlockSpec((L // 16, 16, K), lambda j: (j, 0, 0))],
        out_shape=[jax.ShapeDtypeStruct((TOK, 512), BF)] * 2
        + [jax.ShapeDtypeStruct((K, 512), BF)] * 3
        + [jax.ShapeDtypeStruct((32, 16, K), BF)],
        compiler_params=params(),
        cost_estimate=pl.CostEstimate(
            flops=2 * CH * N * (2 * TOK + 2 * K), bytes_accessed=5 << 20, transcendentals=0
        ),
    )(core, mix, tokens, sig_freq, own, lag)


def conv_kernel(freq_ref, tap_ref, forward_ref, inv_ref, tap_freq_ref, conv_ref):
    upper, lower = tap_ref[0], tap_ref[1]
    high, low = forward_ref[0], forward_ref[1]
    tap_freq = dot(high, upper, LANES) + dot(low, upper, LANES) + dot(high, lower, LANES)
    tap_freq_ref[...] = tap_freq
    conv_ref[...] = both_sides(inv_ref, times(freq_ref[...], tap_freq))


def wide_tile(rows):
    return pl.BlockSpec((rows, 2 * L), lambda j: (0, j))


def conv_part(sig_freq, taps, forward, inv):
    return pl.pallas_call(
        conv_kernel,
        grid=(TILES,),
        in_specs=[
            wide_tile(N),
            pl.BlockSpec((2, 2 * L, K), lambda j: (0, j, 0)),
            whole((2, N, K)),
            whole((2, TOK, N)),
        ],
        out_specs=[wide_tile(N), wide_tile(TOK)],
        out_shape=[jax.ShapeDtypeStruct((N, CH), F32), jax.ShapeDtypeStruct((TOK, CH), F32)],
        compiler_params=params(),
        cost_estimate=pl.CostEstimate(flops=1024, bytes_accessed=1024, transcendentals=0),
    )(sig_freq, taps, forward, inv)


def out_kernel(
    core_ref,
    keep_ref,
    other_ref,
    inner_ref,
    near_ref,
    far_ref,
    gate_in_ref,
    conv_ref,
    tap_freq_ref,
    forward_ref,
    inv_ref,
    place_ref,
    gate_ref,
    sig_ref,
):
    is_first = core_ref[0] == 0

    def joined(left, right):
        return jnp.concatenate(
            [
                dot(
                    jnp.concatenate([left[:, i : i + K], right[:, i : i + K]], axis=1),
                    place_ref[...],
                )
                for i in range(0, L, K)
            ],
            axis=1,
        )

    keep, other = keep_ref[...], other_ref[...]
    mixed = joined(jnp.where(is_first, keep, other), jnp.where(is_first, other, keep))
    near = near_ref[...]
    halo = joined(
        jnp.where(is_first, inner_ref[...], near), jnp.where(is_first, near, far_ref[...])
    ).astype(BF)
    gate_ref[...] = (mixed * conv_ref[...]).astype(BF)
    conv_grad = (mixed * gate_in_ref[...].astype(F32)).astype(BF)
    full = exact_side(forward_ref, jnp.concatenate([conv_grad, halo], axis=0))
    sig_ref[...] = both_sides(inv_ref, times_conj(full, tap_freq_ref[...])).astype(BF)


def out_part(core, keep, other, inner, near, far, gate, conv, tap_freq, forward, inv, place):
    head = pl.BlockSpec((K, L), lambda j: (0, j))
    half = pl.BlockSpec((TOK, L), lambda j: (0, j))
    return pl.pallas_call(
        out_kernel,
        grid=(TILES,),
        in_specs=[
            scalar(),
            half,
            half,
            head,
            head,
            head,
            wide_tile(TOK),
            wide_tile(TOK),
            wide_tile(N),
            whole((2, N, N)),
            whole((2, TOK, N)),
            whole((2 * K, 2 * K)),
        ],
        out_specs=[wide_tile(TOK), wide_tile(TOK)],
        out_shape=[jax.ShapeDtypeStruct((TOK, CH), BF)] * 2,
        compiler_params=params(),
        cost_estimate=pl.CostEstimate(flops=1024, bytes_accessed=1024, transcendentals=0),
    )(core, keep, other, inner, near, far, gate, conv, tap_freq, forward, inv, place)


def chooser():
    source = np.arange(2 * K).reshape(8, 2, 16).transpose(1, 0, 2).reshape(-1)
    matrix = np.zeros((2 * K, 2 * K), np.float32)
    matrix[source, np.arange(2 * K)] = 1.0
    return matrix.astype(jnp.bfloat16)


def send_kernel(weight_ref, tap_ref, place_ref, out_ref):
    out_ref[...] = jnp.zeros_like(out_ref)
    taps = tap_ref[...]
    high = taps.astype(BF)
    low = (taps - high.astype(F32)).astype(BF)
    for c in range(2):
        out_ref[c, 64:, :K] = high
        out_ref[c, 64:, K : 2 * K] = low
    for i in range(4):
        lanes = slice(i * 2 * K, (i + 1) * 2 * K)
        chosen = dot(weight_ref[:, lanes], place_ref[...]).astype(BF)
        out_ref[0, :64, i * K : (i + 1) * K] = chosen[:, :K]
        out_ref[1, :64, i * K : (i + 1) * K] = chosen[:, K:]


def send_part(weights, taps, place):
    return pl.pallas_call(
        send_kernel,
        out_shape=jax.ShapeDtypeStruct((2, 80, 512), BF),
        compiler_params=pltpu.CompilerParams(vmem_limit_bytes=VMEM),
        cost_estimate=pl.CostEstimate(flops=1 << 25, bytes_accessed=1 << 19, transcendentals=0),
    )(weights, taps, place)


def by_core(values, place):
    rows = values.shape[0]
    chosen = dot(values.reshape(rows * 4, 2 * K), place).astype(BF)
    return chosen.reshape(rows, 4, 2, K).transpose(2, 0, 1, 3).reshape(2, rows, 512)


def on_device(out_grad, out_weight, signal, gate_input, filter_taps):
    chips, ctx = ("z", "h"), ("z", "h", "c")
    period = SPAN // TOK
    fwd, inv = transforms()
    place = chooser()
    core = lax.axis_index("c").reshape(1)

    message = send_part(out_weight.T, filter_taps.T, place)
    block = lax.all_to_all(message, "c", split_axis=0, concat_axis=0)

    cols = out_grad.reshape(TOK, 2, 2, K).transpose(2, 1, 0, 3)
    block, cols, signal, gate_input = lax.optimization_barrier((block, cols, signal, gate_input))
    weights = lax.all_gather(block, "z", axis=0, tiled=False)
    cols = lax.all_to_all(cols, "h", split_axis=0, concat_axis=0)

    ahead = [(i, i + 1) for i in range(63) if (i + 1) % period]
    window = jnp.concatenate([lax.ppermute(signal[TOK - K :], ctx, ahead), signal], axis=0)
    sig_freq = plain_part(window, fwd[:, :, :N])
    tokens = jnp.concatenate([by_core(signal, place), by_core(gate_input, place)], axis=1)
    tokens = lax.all_to_all(
        tokens.reshape(2, 2, TOK, 512), "c", split_axis=0, concat_axis=0
    )
    ahead = [(i, i + 1) for i in range(31) if (i + 1) % (period // 2)]
    sig_halo = lax.ppermute(tokens[1, 0, TOK - K :], chips, ahead)
    own_freq = front_part(sig_halo, tokens, fwd[:, :, :N])

    cols, sig_freq, own_freq = lax.optimization_barrier((cols, sig_freq, own_freq))
    cols = lax.all_to_all(
        jnp.broadcast_to(cols[None], (8, 2, 2, TOK, K)), ("x", "l"), split_axis=0, concat_axis=0
    )
    cols = lax.all_to_all(
        jnp.broadcast_to(cols[None], (2, 8, 2, 2, TOK, K)), "c", split_axis=0, concat_axis=0
    )

    partial = product(cols, weights)
    weights, partial = lax.optimization_barrier((weights, partial))
    mix = lax.all_to_all(
        partial.reshape(2, 2, TOK, 512), "h", split_axis=0, concat_axis=0
    )
    keep, send, first, inner, cross, tap_grad = grad_part(
        core, mix, tokens, own_freq, fwd[:, :, K:N], inv[:, :K]
    )
    tap_grad = lax.all_to_all(tap_grad, chips, split_axis=0, concat_axis=0)
    filter_grad = jnp.sum(tap_grad.astype(F32), axis=0).T

    other = lax.ppermute(send, "c", [(0, 1), (1, 0)])
    follows = [(2 * i + 2, 2 * i + 1) for i in range(31) if (i + 1) % (period // 2)]
    near = lax.ppermute(cross, ctx, follows + [(2 * i + 1, 2 * i) for i in range(32)])
    far = lax.ppermute(first, ctx, [(i + 1, j) for i, j in follows])

    taps = weights[:, :, 64:, : 2 * K].reshape(16, 2, 16, 2, K).transpose(3, 0, 1, 2, 4)
    more = lax.ppermute(taps, "h", [(0, 1), (1, 0)])
    upper_half = lax.axis_index("h") == 0
    taps = jnp.stack(
        [jnp.where(upper_half, taps, more), jnp.where(upper_half, more, taps)], axis=2
    ).reshape(2, CH, K)

    tap_freq, conv = conv_part(sig_freq, taps, fwd[:, :, :K], inv[:, K:])
    gate_grad, signal_grad = out_part(
        core,
        keep,
        other,
        inner,
        near,
        far,
        gate_input,
        conv,
        tap_freq,
        fwd[:, :, K:],
        inv[:, K:],
        place.T,
    )
    return signal_grad, gate_grad, filter_grad


def solution(mesh):
    fine = Mesh(mesh.devices.reshape(16, 2, 2, 4, 2), ("z", "h", "c", "x", "l"))
    ctx, tp = ("z", "h", "c"), ("x", "l")
    in_specs = (P(ctx, tp), P(tp, ctx), P(ctx, tp), P(ctx, tp), P(None, tp + ctx))
    out_specs = (P(ctx, tp), P(ctx, tp), P(None, tp + ctx))
    return jax.shard_map(
        on_device, mesh=fine, in_specs=in_specs, out_specs=out_specs, check_vma=False
    )
```

```python
import jax
import jax.numpy as jnp
import numpy as np
from jax import lax
from jax.experimental import pallas as pl
from jax.experimental.pallas import tpu as pltpu
from jax.sharding import Mesh, PartitionSpec as P

K = 128
TOK = 256
CH = 1024
SPAN = 8192
N = K + TOK
HALF = N // 2
TILE = 256
VMEM = 60 * 1024 * 1024

BF = jnp.bfloat16
F32 = jnp.float32
ROWS = ((1,), (0,))
LANES = ((1,), (1,))


def transforms():
    freq = 2.0 * np.pi * (np.arange(HALF) + 0.5) / N
    angle = freq[:, None] * np.arange(N + K)[None, :]
    forward = np.concatenate([np.cos(angle), -np.sin(angle)], axis=0)
    angle = angle[:, :N].T
    inverse = np.concatenate([np.cos(angle), -np.sin(angle)], axis=1) * (2.0 / N)
    return two(forward), two(inverse)


def two(values):
    values = np.asarray(values, np.float32)
    upper = values.astype(jnp.bfloat16)
    lower = (values - upper.astype(np.float32)).astype(jnp.bfloat16)
    return np.stack([upper, lower])


def dot(a, b, dims=ROWS):
    return lax.dot_general(a, b, (dims, ((), ())), preferred_element_type=F32)


def exact_side(matrix, values):
    return dot(
        jnp.concatenate([matrix[0], matrix[1]], axis=1),
        jnp.concatenate([values, values], axis=0),
    )


def both_sides(matrix, values):
    high = values.astype(BF)
    low = (values - high.astype(F32)).astype(BF)
    return dot(
        jnp.concatenate([matrix[0], matrix[1], matrix[0]], axis=1),
        jnp.concatenate([high, high, low], axis=0),
    )


def times(a, b):
    ar, ai, br, bi = a[:HALF], a[HALF:], b[:HALF], b[HALF:]
    return jnp.concatenate([ar * br - ai * bi, ar * bi + ai * br], axis=0)


def times_conj(a, b):
    ar, ai, br, bi = a[:HALF], a[HALF:], b[:HALF], b[HALF:]
    return jnp.concatenate([ar * br + ai * bi, ai * br - ar * bi], axis=0)


def params(limit=VMEM):
    return pltpu.CompilerParams(
        dimension_semantics=("arbitrary",), vmem_limit_bytes=limit
    )


def product_kernel(cols_ref, weight_ref, out_ref):
    weight = weight_ref[:, :, :64].reshape(16 * K, 512)
    for b in range(2):
        rows = jnp.concatenate([cols_ref[b, i, 0, j] for i in range(8) for j in range(2)], axis=1)
        out_ref[b] = dot(rows, weight).astype(BF)


def product(cols, weights):
    return pl.pallas_call(
        product_kernel,
        grid=(2,),
        in_specs=[
            pl.BlockSpec((2, 8, 1, 2, TOK, K), lambda i: (0, 0, i, 0, 0, 0)),
            pl.BlockSpec((16, 2, 80, 512), lambda i: (0, 0, 0, 0)),
        ],
        out_specs=pl.BlockSpec((2, TOK, 512), lambda i: (i, 0, 0)),
        out_shape=jax.ShapeDtypeStruct((4, TOK, 512), BF),
        compiler_params=params(),
        cost_estimate=pl.CostEstimate(
            flops=2 * 1024 * 2048 * 512, bytes_accessed=8 << 20, transcendentals=0
        ),
    )(cols, weights)


def whole(shape):
    return pl.BlockSpec(shape, lambda j: (0,) * len(shape))


def scalar():
    return pl.BlockSpec(memory_space=pltpu.SMEM)


L = 256
TILES = 512 // L
PAIR = pl.BlockSpec((1, TOK, 2 * K), lambda j: (j, 0, 0))
FREQ = pl.BlockSpec((1, N, 2 * L), lambda j: (j, 0, 0))


def plain_kernel(window_ref, forward_ref, freq_ref):
    freq_ref[...] = exact_side(forward_ref, window_ref[...])


def plain_part(window, forward):
    tile = pl.BlockSpec((N, 2 * L), lambda j: (0, j))
    return pl.pallas_call(
        plain_kernel,
        grid=(TILES,),
        in_specs=[tile, whole((2, N, N))],
        out_specs=tile,
        out_shape=jax.ShapeDtypeStruct((N, CH), F32),
        compiler_params=params(),
        cost_estimate=pl.CostEstimate(
            flops=2 * CH * N * 2 * N, bytes_accessed=3 << 20, transcendentals=0
        ),
    )(window, forward)


def front_kernel(halo_ref, tok_ref, forward_ref, freq_ref):
    first, second = tok_ref[0, 0], tok_ref[1, 0]
    window = jnp.concatenate(
        [
            jnp.concatenate([halo_ref[...], first[K:]], axis=1),
            jnp.concatenate([first[:K], second[:K]], axis=1),
            jnp.concatenate([first[K:], second[K:]], axis=1),
        ],
        axis=0,
    )
    freq_ref[0] = exact_side(forward_ref, window)


def front_part(halo, tokens, forward):
    return pl.pallas_call(
        front_kernel,
        grid=(TILES,),
        in_specs=[
            pl.BlockSpec((K, L), lambda j: (0, j)),
            pl.BlockSpec((2, 1, TOK, L), lambda j: (0, 0, 0, j)),
            whole((2, N, N)),
        ],
        out_specs=FREQ,
        out_shape=jax.ShapeDtypeStruct((TILES, N, 2 * L), F32),
        compiler_params=params(),
        cost_estimate=pl.CostEstimate(
            flops=2 * CH * N * 2 * N, bytes_accessed=3 << 20, transcendentals=0
        ),
    )(halo, tokens, forward)


def grad_kernel(
    core_ref,
    mix_ref,
    tok_ref,
    freq_ref,
    own_ref,
    lag_ref,
    keep_ref,
    send_ref,
    first_ref,
    inner_ref,
    cross_ref,
    tap_ref,
):
    is_first = core_ref[0] == 0
    early = (mix_ref[0, 0].astype(F32) + mix_ref[1, 0].astype(F32)).astype(BF).astype(F32)
    late = (mix_ref[0, 1].astype(F32) + mix_ref[1, 1].astype(F32)).astype(BF).astype(F32)
    keep_ref[...] = jnp.where(is_first, early, late).astype(BF)
    send_ref[...] = jnp.where(is_first, late, early).astype(BF)
    early = early * tok_ref[0, 0].astype(F32)
    late = late * tok_ref[1, 0].astype(F32)
    first_ref[...] = early[:K].astype(BF)
    inner_ref[...] = late[:K].astype(BF)
    cross_ref[...] = jnp.where(is_first, early[:K], late[:K]).astype(BF)
    conv_grad = jnp.concatenate([early, late], axis=1).astype(BF)
    cross = times_conj(exact_side(own_ref, conv_grad), freq_ref[0])
    taps = both_sides(lag_ref, cross[:, :L] + cross[:, L:])
    tap_ref[...] = taps.T.reshape(L // 16, 16, K).astype(tap_ref.dtype)


def grad_part(core, mix, tokens, sig_freq, own, lag):
    head = pl.BlockSpec((K, L), lambda j: (0, j))
    half = pl.BlockSpec((TOK, L), lambda j: (0, j))
    return pl.pallas_call(
        grad_kernel,
        grid=(TILES,),
        in_specs=[
            scalar(),
            pl.BlockSpec((2, 2, TOK, L), lambda j: (0, 0, 0, j)),
            pl.BlockSpec((2, 1, TOK, L), lambda j: (0, 1, 0, j)),
            FREQ,
            whole((2, N, TOK)),
            whole((2, K, N)),
        ],
        out_specs=[half, half, head, head, head, pl.BlockSpec((L // 16, 16, K), lambda j: (j, 0, 0))],
        out_shape=[jax.ShapeDtypeStruct((TOK, 512), BF)] * 2
        + [jax.ShapeDtypeStruct((K, 512), BF)] * 3
        + [jax.ShapeDtypeStruct((32, 16, K), BF)],
        compiler_params=params(),
        cost_estimate=pl.CostEstimate(
            flops=2 * CH * N * (2 * TOK + 2 * K), bytes_accessed=5 << 20, transcendentals=0
        ),
    )(core, mix, tokens, sig_freq, own, lag)


def conv_kernel(freq_ref, tap_ref, forward_ref, inv_ref, tap_freq_ref, conv_ref):
    upper, lower = tap_ref[0], tap_ref[1]
    high, low = forward_ref[0], forward_ref[1]
    tap_freq = dot(high, upper, LANES) + dot(low, upper, LANES) + dot(high, lower, LANES)
    tap_freq_ref[...] = tap_freq
    conv_ref[...] = both_sides(inv_ref, times(freq_ref[...], tap_freq))


def wide_tile(rows):
    return pl.BlockSpec((rows, 2 * L), lambda j: (0, j))


def conv_part(sig_freq, taps, forward, inv):
    return pl.pallas_call(
        conv_kernel,
        grid=(TILES,),
        in_specs=[
            wide_tile(N),
            pl.BlockSpec((2, 2 * L, K), lambda j: (0, j, 0)),
            whole((2, N, K)),
            whole((2, TOK, N)),
        ],
        out_specs=[wide_tile(N), wide_tile(TOK)],
        out_shape=[jax.ShapeDtypeStruct((N, CH), F32), jax.ShapeDtypeStruct((TOK, CH), F32)],
        compiler_params=params(),
        cost_estimate=pl.CostEstimate(flops=1024, bytes_accessed=1024, transcendentals=0),
    )(sig_freq, taps, forward, inv)


def out_kernel(
    core_ref,
    keep_ref,
    other_ref,
    inner_ref,
    near_ref,
    far_ref,
    gate_in_ref,
    conv_ref,
    tap_freq_ref,
    forward_ref,
    inv_ref,
    place_ref,
    gate_ref,
    sig_ref,
):
    is_first = core_ref[0] == 0

    def joined(left, right):
        return jnp.concatenate(
            [
                dot(
                    jnp.concatenate([left[:, i : i + K], right[:, i : i + K]], axis=1),
                    place_ref[...],
                )
                for i in range(0, L, K)
            ],
            axis=1,
        )

    keep, other = keep_ref[...], other_ref[...]
    mixed = joined(jnp.where(is_first, keep, other), jnp.where(is_first, other, keep))
    near = near_ref[...]
    halo = joined(
        jnp.where(is_first, inner_ref[...], near), jnp.where(is_first, near, far_ref[...])
    ).astype(BF)
    gate_ref[...] = (mixed * conv_ref[...]).astype(BF)
    conv_grad = (mixed * gate_in_ref[...].astype(F32)).astype(BF)
    full = exact_side(forward_ref, jnp.concatenate([conv_grad, halo], axis=0))
    sig_ref[...] = both_sides(inv_ref, times_conj(full, tap_freq_ref[...])).astype(BF)


def out_part(core, keep, other, inner, near, far, gate, conv, tap_freq, forward, inv, place):
    head = pl.BlockSpec((K, L), lambda j: (0, j))
    half = pl.BlockSpec((TOK, L), lambda j: (0, j))
    return pl.pallas_call(
        out_kernel,
        grid=(TILES,),
        in_specs=[
            scalar(),
            half,
            half,
            head,
            head,
            head,
            wide_tile(TOK),
            wide_tile(TOK),
            wide_tile(N),
            whole((2, N, N)),
            whole((2, TOK, N)),
            whole((2 * K, 2 * K)),
        ],
        out_specs=[wide_tile(TOK), wide_tile(TOK)],
        out_shape=[jax.ShapeDtypeStruct((TOK, CH), BF)] * 2,
        compiler_params=params(),
        cost_estimate=pl.CostEstimate(flops=1024, bytes_accessed=1024, transcendentals=0),
    )(core, keep, other, inner, near, far, gate, conv, tap_freq, forward, inv, place)


def chooser():
    source = np.arange(2 * K).reshape(8, 2, 16).transpose(1, 0, 2).reshape(-1)
    matrix = np.zeros((2 * K, 2 * K), np.float32)
    matrix[source, np.arange(2 * K)] = 1.0
    return matrix.astype(jnp.bfloat16)


def send_kernel(weight_ref, tap_ref, place_ref, out_ref):
    out_ref[...] = jnp.zeros_like(out_ref)
    taps = tap_ref[...]
    high = taps.astype(BF)
    low = (taps - high.astype(F32)).astype(BF)
    for c in range(2):
        out_ref[c, 64:, :K] = high
        out_ref[c, 64:, K : 2 * K] = low
    for i in range(4):
        lanes = slice(i * 2 * K, (i + 1) * 2 * K)
        chosen = dot(weight_ref[:, lanes], place_ref[...]).astype(BF)
        out_ref[0, :64, i * K : (i + 1) * K] = chosen[:, :K]
        out_ref[1, :64, i * K : (i + 1) * K] = chosen[:, K:]


def send_part(weights, taps, place):
    return pl.pallas_call(
        send_kernel,
        out_shape=jax.ShapeDtypeStruct((2, 80, 512), BF),
        compiler_params=pltpu.CompilerParams(vmem_limit_bytes=VMEM),
        cost_estimate=pl.CostEstimate(flops=1 << 25, bytes_accessed=1 << 19, transcendentals=0),
    )(weights, taps, place)


def by_core(values, place):
    rows = values.shape[0]
    chosen = dot(values.reshape(rows * 4, 2 * K), place).astype(BF)
    return chosen.reshape(rows, 4, 2, K).transpose(2, 0, 1, 3).reshape(2, rows, 512)


def on_device(out_grad, out_weight, signal, gate_input, filter_taps):
    chips, ctx = ("z", "h"), ("z", "h", "c")
    period = SPAN // TOK
    fwd, inv = transforms()
    place = chooser()
    core = lax.axis_index("c").reshape(1)

    message = send_part(out_weight.T, filter_taps.T, place)
    block = lax.all_to_all(message, "c", split_axis=0, concat_axis=0)

    block, out_grad, signal, gate_input = lax.optimization_barrier(
        (block, out_grad, signal, gate_input)
    )
    cols = out_grad.reshape(TOK, 2, 2, K).transpose(2, 1, 0, 3)
    weights = lax.all_gather(block, "z", axis=0, tiled=False)
    cols = lax.all_to_all(cols, "h", split_axis=0, concat_axis=0)

    ahead = [(i, i + 1) for i in range(63) if (i + 1) % period]
    window = jnp.concatenate([lax.ppermute(signal[TOK - K :], ctx, ahead), signal], axis=0)
    sig_freq = plain_part(window, fwd[:, :, :N])
    tokens = jnp.concatenate([by_core(signal, place), by_core(gate_input, place)], axis=1)
    tokens = lax.all_to_all(
        tokens.reshape(2, 2, TOK, 512), "c", split_axis=0, concat_axis=0
    )
    ahead = [(i, i + 1) for i in range(31) if (i + 1) % (period // 2)]
    sig_halo = lax.ppermute(tokens[1, 0, TOK - K :], chips, ahead)
    own_freq = front_part(sig_halo, tokens, fwd[:, :, :N])

    cols, sig_freq, own_freq = lax.optimization_barrier((cols, sig_freq, own_freq))
    cols = lax.all_to_all(
        jnp.broadcast_to(cols[None], (8, 2, 2, TOK, K)), ("x", "l"), split_axis=0, concat_axis=0
    )
    cols = lax.all_to_all(
        jnp.broadcast_to(cols[None], (2, 8, 2, 2, TOK, K)), "c", split_axis=0, concat_axis=0
    )

    partial = product(cols, weights)
    weights, partial = lax.optimization_barrier((weights, partial))
    mix = lax.all_to_all(
        partial.reshape(2, 2, TOK, 512), "h", split_axis=0, concat_axis=0
    )
    keep, send, first, inner, cross, tap_grad = grad_part(
        core, mix, tokens, own_freq, fwd[:, :, K:N], inv[:, :K]
    )
    tap_grad = lax.all_to_all(tap_grad, chips, split_axis=0, concat_axis=0)
    filter_grad = jnp.sum(tap_grad.astype(F32), axis=0).T

    other = lax.ppermute(send, "c", [(0, 1), (1, 0)])
    follows = [(2 * i + 2, 2 * i + 1) for i in range(31) if (i + 1) % (period // 2)]
    near = lax.ppermute(cross, ctx, follows + [(2 * i + 1, 2 * i) for i in range(32)])
    far = lax.ppermute(first, ctx, [(i + 1, j) for i, j in follows])

    taps = weights[:, :, 64:, : 2 * K].reshape(16, 2, 16, 2, K).transpose(3, 0, 1, 2, 4)
    more = lax.ppermute(taps, "h", [(0, 1), (1, 0)])
    upper_half = lax.axis_index("h") == 0
    taps = jnp.stack(
        [jnp.where(upper_half, taps, more), jnp.where(upper_half, more, taps)], axis=2
    ).reshape(2, CH, K)

    tap_freq, conv = conv_part(sig_freq, taps, fwd[:, :, :K], inv[:, K:])
    gate_grad, signal_grad = out_part(
        core,
        keep,
        other,
        inner,
        near,
        far,
        gate_input,
        conv,
        tap_freq,
        fwd[:, :, K:],
        inv[:, K:],
        place.T,
    )
    return signal_grad, gate_grad, filter_grad


def solution(mesh):
    fine = Mesh(mesh.devices.reshape(16, 2, 2, 4, 2), ("z", "h", "c", "x", "l"))
    ctx, tp = ("z", "h", "c"), ("x", "l")
    in_specs = (P(ctx, tp), P(tp, ctx), P(ctx, tp), P(ctx, tp), P(None, tp + ctx))
    out_specs = (P(ctx, tp), P(ctx, tp), P(None, tp + ctx))
    return jax.shard_map(
        on_device, mesh=fine, in_specs=in_specs, out_specs=out_specs, check_vma=False
    )
```

```python
import jax
import jax.numpy as jnp
import numpy as np
from jax import lax
from jax.experimental import pallas as pl
from jax.experimental.pallas import tpu as pltpu
from jax.sharding import Mesh, PartitionSpec as P

K = 128
TOK = 256
CH = 1024
SPAN = 8192
N = K + TOK
HALF = N // 2
TILE = 256
VMEM = 60 * 1024 * 1024

BF = jnp.bfloat16
F32 = jnp.float32
ROWS = ((1,), (0,))
LANES = ((1,), (1,))


def transforms():
    freq = 2.0 * np.pi * (np.arange(HALF) + 0.5) / N
    angle = freq[:, None] * np.arange(N + K)[None, :]
    forward = np.concatenate([np.cos(angle), -np.sin(angle)], axis=0)
    angle = angle[:, :N].T
    inverse = np.concatenate([np.cos(angle), -np.sin(angle)], axis=1) * (2.0 / N)
    return two(forward), two(inverse)


def two(values):
    values = np.asarray(values, np.float32)
    upper = values.astype(jnp.bfloat16)
    lower = (values - upper.astype(np.float32)).astype(jnp.bfloat16)
    return np.stack([upper, lower])


def dot(a, b, dims=ROWS):
    return lax.dot_general(a, b, (dims, ((), ())), preferred_element_type=F32)


def exact_side(matrix, values):
    return dot(
        jnp.concatenate([matrix[0], matrix[1]], axis=1),
        jnp.concatenate([values, values], axis=0),
    )


def both_sides(matrix, values):
    high = values.astype(BF)
    low = (values - high.astype(F32)).astype(BF)
    return dot(
        jnp.concatenate([matrix[0], matrix[1], matrix[0]], axis=1),
        jnp.concatenate([high, high, low], axis=0),
    )


def times(a, b):
    ar, ai, br, bi = a[:HALF], a[HALF:], b[:HALF], b[HALF:]
    return jnp.concatenate([ar * br - ai * bi, ar * bi + ai * br], axis=0)


def times_conj(a, b):
    ar, ai, br, bi = a[:HALF], a[HALF:], b[:HALF], b[HALF:]
    return jnp.concatenate([ar * br + ai * bi, ai * br - ar * bi], axis=0)


def params(limit=VMEM):
    return pltpu.CompilerParams(
        dimension_semantics=("arbitrary",), vmem_limit_bytes=limit
    )


def product_kernel(h_ref, cols_ref, weight_ref, out_ref):
    weight = weight_ref[:, :, :64].reshape(16 * K, 512)
    rows = jnp.concatenate([cols_ref[0, i, 0, j] for i in range(8) for j in range(2)], axis=1)
    out_ref[0] = dot(rows, weight).astype(BF)


def product(h, cols, weights):
    return pl.pallas_call(
        product_kernel,
        grid_spec=pltpu.PrefetchScalarGridSpec(
            num_scalar_prefetch=1,
            grid=(2,),
            in_specs=[
                pl.BlockSpec((1, 8, 1, 2, TOK, K), lambda i, h: (i, 0, h[0], 0, 0, 0)),
                pl.BlockSpec((16, 2, 80, 512), lambda i, h: (0, 0, 0, 0)),
            ],
            out_specs=pl.BlockSpec((1, TOK, 512), lambda i, h: (i, 0, 0)),
        ),
        out_shape=jax.ShapeDtypeStruct((2, TOK, 512), BF),
        compiler_params=params(),
        cost_estimate=pl.CostEstimate(
            flops=1024 * 2048 * 512, bytes_accessed=5 << 20, transcendentals=0
        ),
    )(h, cols, weights)


def whole(shape):
    return pl.BlockSpec(shape, lambda j: (0,) * len(shape))


def scalar():
    return pl.BlockSpec(memory_space=pltpu.SMEM)


L = 256
TILES = 512 // L
PAIR = pl.BlockSpec((1, TOK, 2 * K), lambda j: (j, 0, 0))
FREQ = pl.BlockSpec((1, N, 2 * L), lambda j: (j, 0, 0))


def plain_kernel(window_ref, forward_ref, freq_ref):
    freq_ref[...] = exact_side(forward_ref, window_ref[...])


def plain_part(window, forward):
    tile = pl.BlockSpec((N, 2 * L), lambda j: (0, j))
    return pl.pallas_call(
        plain_kernel,
        grid=(TILES,),
        in_specs=[tile, whole((2, N, N))],
        out_specs=tile,
        out_shape=jax.ShapeDtypeStruct((N, CH), F32),
        compiler_params=params(),
        cost_estimate=pl.CostEstimate(
            flops=2 * CH * N * 2 * N, bytes_accessed=3 << 20, transcendentals=0
        ),
    )(window, forward)


def front_kernel(halo_ref, tok_ref, forward_ref, freq_ref):
    first, second = tok_ref[0, 0], tok_ref[1, 0]
    window = jnp.concatenate(
        [
            jnp.concatenate([halo_ref[...], first[K:]], axis=1),
            jnp.concatenate([first[:K], second[:K]], axis=1),
            jnp.concatenate([first[K:], second[K:]], axis=1),
        ],
        axis=0,
    )
    freq_ref[0] = exact_side(forward_ref, window)


def front_part(halo, tokens, forward):
    return pl.pallas_call(
        front_kernel,
        grid=(TILES,),
        in_specs=[
            pl.BlockSpec((K, L), lambda j: (0, j)),
            pl.BlockSpec((2, 1, TOK, L), lambda j: (0, 0, 0, j)),
            whole((2, N, N)),
        ],
        out_specs=FREQ,
        out_shape=jax.ShapeDtypeStruct((TILES, N, 2 * L), F32),
        compiler_params=params(),
        cost_estimate=pl.CostEstimate(
            flops=2 * CH * N * 2 * N, bytes_accessed=3 << 20, transcendentals=0
        ),
    )(halo, tokens, forward)


def grad_kernel(
    core_ref,
    mix_ref,
    more_ref,
    tok_ref,
    freq_ref,
    own_ref,
    lag_ref,
    keep_ref,
    send_ref,
    first_ref,
    inner_ref,
    cross_ref,
    tap_ref,
):
    is_first = core_ref[0] == 0
    early = (mix_ref[0].astype(F32) + more_ref[0].astype(F32)).astype(BF).astype(F32)
    late = (mix_ref[1].astype(F32) + more_ref[1].astype(F32)).astype(BF).astype(F32)
    keep_ref[...] = jnp.where(is_first, early, late).astype(BF)
    send_ref[...] = jnp.where(is_first, late, early).astype(BF)
    early = early * tok_ref[0, 0].astype(F32)
    late = late * tok_ref[1, 0].astype(F32)
    first_ref[...] = early[:K].astype(BF)
    inner_ref[...] = late[:K].astype(BF)
    cross_ref[...] = jnp.where(is_first, early[:K], late[:K]).astype(BF)
    conv_grad = jnp.concatenate([early, late], axis=1).astype(BF)
    cross = times_conj(exact_side(own_ref, conv_grad), freq_ref[0])
    taps = both_sides(lag_ref, cross[:, :L] + cross[:, L:])
    tap_ref[...] = taps.T.reshape(L // 16, 16, K).astype(tap_ref.dtype)


def grad_part(core, mix, more, tokens, sig_freq, own, lag):
    head = pl.BlockSpec((K, L), lambda j: (0, j))
    half = pl.BlockSpec((TOK, L), lambda j: (0, j))
    return pl.pallas_call(
        grad_kernel,
        grid=(TILES,),
        in_specs=[
            scalar(),
            pl.BlockSpec((2, TOK, L), lambda j: (0, 0, j)),
            pl.BlockSpec((2, TOK, L), lambda j: (0, 0, j)),
            pl.BlockSpec((2, 1, TOK, L), lambda j: (0, 1, 0, j)),
            FREQ,
            whole((2, N, TOK)),
            whole((2, K, N)),
        ],
        out_specs=[half, half, head, head, head, pl.BlockSpec((L // 16, 16, K), lambda j: (j, 0, 0))],
        out_shape=[jax.ShapeDtypeStruct((TOK, 512), BF)] * 2
        + [jax.ShapeDtypeStruct((K, 512), BF)] * 3
        + [jax.ShapeDtypeStruct((32, 16, K), BF)],
        compiler_params=params(),
        cost_estimate=pl.CostEstimate(
            flops=2 * CH * N * (2 * TOK + 2 * K), bytes_accessed=5 << 20, transcendentals=0
        ),
    )(core, mix, more, tokens, sig_freq, own, lag)


def conv_kernel(freq_ref, tap_ref, forward_ref, inv_ref, tap_freq_ref, conv_ref):
    upper, lower = tap_ref[0], tap_ref[1]
    high, low = forward_ref[0], forward_ref[1]
    tap_freq = dot(high, upper, LANES) + dot(low, upper, LANES) + dot(high, lower, LANES)
    tap_freq_ref[...] = tap_freq
    conv_ref[...] = both_sides(inv_ref, times(freq_ref[...], tap_freq))


def wide_tile(rows):
    return pl.BlockSpec((rows, 2 * L), lambda j: (0, j))


def conv_part(sig_freq, taps, forward, inv):
    return pl.pallas_call(
        conv_kernel,
        grid=(TILES,),
        in_specs=[
            wide_tile(N),
            pl.BlockSpec((2, 2 * L, K), lambda j: (0, j, 0)),
            whole((2, N, K)),
            whole((2, TOK, N)),
        ],
        out_specs=[wide_tile(N), wide_tile(TOK)],
        out_shape=[jax.ShapeDtypeStruct((N, CH), F32), jax.ShapeDtypeStruct((TOK, CH), F32)],
        compiler_params=params(),
        cost_estimate=pl.CostEstimate(flops=1024, bytes_accessed=1024, transcendentals=0),
    )(sig_freq, taps, forward, inv)


def out_kernel(
    core_ref,
    keep_ref,
    other_ref,
    inner_ref,
    near_ref,
    far_ref,
    gate_in_ref,
    conv_ref,
    tap_freq_ref,
    forward_ref,
    inv_ref,
    place_ref,
    gate_ref,
    sig_ref,
):
    is_first = core_ref[0] == 0

    def joined(left, right):
        return jnp.concatenate(
            [
                dot(
                    jnp.concatenate([left[:, i : i + K], right[:, i : i + K]], axis=1),
                    place_ref[...],
                )
                for i in range(0, L, K)
            ],
            axis=1,
        )

    keep, other = keep_ref[...], other_ref[...]
    mixed = joined(jnp.where(is_first, keep, other), jnp.where(is_first, other, keep))
    near = near_ref[...]
    halo = joined(
        jnp.where(is_first, inner_ref[...], near), jnp.where(is_first, near, far_ref[...])
    ).astype(BF)
    gate_ref[...] = (mixed * conv_ref[...]).astype(BF)
    conv_grad = (mixed * gate_in_ref[...].astype(F32)).astype(BF)
    full = exact_side(forward_ref, jnp.concatenate([conv_grad, halo], axis=0))
    sig_ref[...] = both_sides(inv_ref, times_conj(full, tap_freq_ref[...])).astype(BF)


def out_part(core, keep, other, inner, near, far, gate, conv, tap_freq, forward, inv, place):
    head = pl.BlockSpec((K, L), lambda j: (0, j))
    half = pl.BlockSpec((TOK, L), lambda j: (0, j))
    return pl.pallas_call(
        out_kernel,
        grid=(TILES,),
        in_specs=[
            scalar(),
            half,
            half,
            head,
            head,
            head,
            wide_tile(TOK),
            wide_tile(TOK),
            wide_tile(N),
            whole((2, N, N)),
            whole((2, TOK, N)),
            whole((2 * K, 2 * K)),
        ],
        out_specs=[wide_tile(TOK), wide_tile(TOK)],
        out_shape=[jax.ShapeDtypeStruct((TOK, CH), BF)] * 2,
        compiler_params=params(),
        cost_estimate=pl.CostEstimate(flops=1024, bytes_accessed=1024, transcendentals=0),
    )(core, keep, other, inner, near, far, gate, conv, tap_freq, forward, inv, place)


def chooser():
    source = np.arange(2 * K).reshape(8, 2, 16).transpose(1, 0, 2).reshape(-1)
    matrix = np.zeros((2 * K, 2 * K), np.float32)
    matrix[source, np.arange(2 * K)] = 1.0
    return matrix.astype(jnp.bfloat16)


def send_kernel(weight_ref, tap_ref, place_ref, out_ref):
    out_ref[...] = jnp.zeros_like(out_ref)
    taps = tap_ref[...]
    high = taps.astype(BF)
    low = (taps - high.astype(F32)).astype(BF)
    for c in range(2):
        out_ref[c, 64:, :K] = high
        out_ref[c, 64:, K : 2 * K] = low
    for i in range(4):
        lanes = slice(i * 2 * K, (i + 1) * 2 * K)
        chosen = dot(weight_ref[:, lanes], place_ref[...]).astype(BF)
        out_ref[0, :64, i * K : (i + 1) * K] = chosen[:, :K]
        out_ref[1, :64, i * K : (i + 1) * K] = chosen[:, K:]


def send_part(weights, taps, place):
    return pl.pallas_call(
        send_kernel,
        out_shape=jax.ShapeDtypeStruct((2, 80, 512), BF),
        compiler_params=pltpu.CompilerParams(vmem_limit_bytes=VMEM),
        cost_estimate=pl.CostEstimate(flops=1 << 25, bytes_accessed=1 << 19, transcendentals=0),
    )(weights, taps, place)


def by_core(values, place):
    rows = values.shape[0]
    chosen = dot(values.reshape(rows * 4, 2 * K), place).astype(BF)
    return chosen.reshape(rows, 4, 2, K).transpose(2, 0, 1, 3).reshape(2, rows, 512)


def on_device(out_grad, out_weight, signal, gate_input, filter_taps):
    chips, ctx = ("z", "h"), ("z", "h", "c")
    period = SPAN // TOK
    fwd, inv = transforms()
    place = chooser()
    core = lax.axis_index("c").reshape(1)

    message = send_part(out_weight.T, filter_taps.T, place)
    block = lax.all_to_all(message, "c", split_axis=0, concat_axis=0)

    block, out_grad, signal, gate_input = lax.optimization_barrier(
        (block, out_grad, signal, gate_input)
    )
    cols = out_grad.reshape(TOK, 2, 2, K).transpose(2, 1, 0, 3)
    weights = lax.all_gather(block, "z", axis=0, tiled=False)
    cols = lax.all_to_all(cols, "h", split_axis=0, concat_axis=0)

    ahead = [(i, i + 1) for i in range(63) if (i + 1) % period]
    window = jnp.concatenate([lax.ppermute(signal[TOK - K :], ctx, ahead), signal], axis=0)
    sig_freq = plain_part(window, fwd[:, :, :N])
    tokens = jnp.concatenate([by_core(signal, place), by_core(gate_input, place)], axis=1)
    tokens = lax.all_to_all(
        tokens.reshape(2, 2, TOK, 512), "c", split_axis=0, concat_axis=0
    )
    ahead = [(i, i + 1) for i in range(31) if (i + 1) % (period // 2)]
    sig_halo = lax.ppermute(tokens[1, 0, TOK - K :], chips, ahead)
    own_freq = front_part(sig_halo, tokens, fwd[:, :, :N])

    cols, sig_freq, own_freq = lax.optimization_barrier((cols, sig_freq, own_freq))
    cols = lax.all_to_all(
        jnp.broadcast_to(cols[None], (8, 2, 2, TOK, K)), ("x", "l"), split_axis=0, concat_axis=0
    )
    cols = lax.all_to_all(
        jnp.broadcast_to(cols[None], (2, 8, 2, 2, TOK, K)), "c", split_axis=0, concat_axis=0
    )

    h = lax.axis_index("h").reshape(1)
    partial = product(1 - h, cols, weights)
    weights, partial = lax.optimization_barrier((weights, partial))
    more = lax.ppermute(partial, "h", [(0, 1), (1, 0)])
    mix = product(h, cols, weights)
    keep, send, first, inner, cross, tap_grad = grad_part(
        core, mix, more, tokens, own_freq, fwd[:, :, K:N], inv[:, :K]
    )
    tap_grad = lax.all_to_all(tap_grad, chips, split_axis=0, concat_axis=0)
    filter_grad = jnp.sum(tap_grad.astype(F32), axis=0).T

    other = lax.ppermute(send, "c", [(0, 1), (1, 0)])
    follows = [(2 * i + 2, 2 * i + 1) for i in range(31) if (i + 1) % (period // 2)]
    near = lax.ppermute(cross, ctx, follows + [(2 * i + 1, 2 * i) for i in range(32)])
    far = lax.ppermute(first, ctx, [(i + 1, j) for i, j in follows])

    taps = weights[:, :, 64:, : 2 * K].reshape(16, 2, 16, 2, K).transpose(3, 0, 1, 2, 4)
    others = lax.ppermute(taps, "h", [(0, 1), (1, 0)])
    upper_half = lax.axis_index("h") == 0
    taps = jnp.stack(
        [jnp.where(upper_half, taps, others), jnp.where(upper_half, others, taps)], axis=2
    ).reshape(2, CH, K)

    tap_freq, conv = conv_part(sig_freq, taps, fwd[:, :, :K], inv[:, K:])
    gate_grad, signal_grad = out_part(
        core,
        keep,
        other,
        inner,
        near,
        far,
        gate_input,
        conv,
        tap_freq,
        fwd[:, :, K:],
        inv[:, K:],
        place.T,
    )
    return signal_grad, gate_grad, filter_grad


def solution(mesh):
    fine = Mesh(mesh.devices.reshape(16, 2, 2, 4, 2), ("z", "h", "c", "x", "l"))
    ctx, tp = ("z", "h", "c"), ("x", "l")
    in_specs = (P(ctx, tp), P(tp, ctx), P(ctx, tp), P(ctx, tp), P(None, tp + ctx))
    out_specs = (P(ctx, tp), P(ctx, tp), P(None, tp + ctx))
    return jax.shard_map(
        on_device, mesh=fine, in_specs=in_specs, out_specs=out_specs, check_vma=False
    )
```

```python
import jax
import jax.numpy as jnp
import numpy as np
from jax import lax
from jax.experimental import pallas as pl
from jax.experimental.pallas import tpu as pltpu
from jax.sharding import Mesh, PartitionSpec as P

K = 128
TOK = 256
CH = 1024
SPAN = 8192
N = K + TOK
HALF = N // 2
TILE = 256
VMEM = 60 * 1024 * 1024

BF = jnp.bfloat16
F32 = jnp.float32
ROWS = ((1,), (0,))
LANES = ((1,), (1,))


def transforms():
    freq = 2.0 * np.pi * (np.arange(HALF) + 0.5) / N
    angle = freq[:, None] * np.arange(N + K)[None, :]
    forward = np.concatenate([np.cos(angle), -np.sin(angle)], axis=0)
    angle = angle[:, :N].T
    inverse = np.concatenate([np.cos(angle), -np.sin(angle)], axis=1) * (2.0 / N)
    return two(forward), two(inverse)


def two(values):
    values = np.asarray(values, np.float32)
    upper = values.astype(jnp.bfloat16)
    lower = (values - upper.astype(np.float32)).astype(jnp.bfloat16)
    return np.stack([upper, lower])


def dot(a, b, dims=ROWS):
    return lax.dot_general(a, b, (dims, ((), ())), preferred_element_type=F32)


def exact_side(matrix, values):
    return dot(
        jnp.concatenate([matrix[0], matrix[1]], axis=1),
        jnp.concatenate([values, values], axis=0),
    )


def both_sides(matrix, values):
    high = values.astype(BF)
    low = (values - high.astype(F32)).astype(BF)
    return dot(
        jnp.concatenate([matrix[0], matrix[1], matrix[0]], axis=1),
        jnp.concatenate([high, high, low], axis=0),
    )


def times(a, b):
    ar, ai, br, bi = a[:HALF], a[HALF:], b[:HALF], b[HALF:]
    return jnp.concatenate([ar * br - ai * bi, ar * bi + ai * br], axis=0)


def times_conj(a, b):
    ar, ai, br, bi = a[:HALF], a[HALF:], b[:HALF], b[HALF:]
    return jnp.concatenate([ar * br + ai * bi, ai * br - ar * bi], axis=0)


def params(limit=VMEM):
    return pltpu.CompilerParams(
        dimension_semantics=("arbitrary",), vmem_limit_bytes=limit
    )


def product_kernel(h_ref, cols_ref, weight_ref, out_ref):
    weight = weight_ref[:, :, :64].reshape(16 * K, 512)
    rows = jnp.concatenate([cols_ref[0, i, 0, j] for i in range(8) for j in range(2)], axis=1)
    out_ref[0] = dot(rows, weight).astype(BF)


def product(h, cols, weights):
    return pl.pallas_call(
        product_kernel,
        grid_spec=pltpu.PrefetchScalarGridSpec(
            num_scalar_prefetch=1,
            grid=(2,),
            in_specs=[
                pl.BlockSpec((1, 8, 1, 2, TOK, K), lambda i, h: (i, 0, h[0], 0, 0, 0)),
                pl.BlockSpec((16, 2, 80, 512), lambda i, h: (0, 0, 0, 0)),
            ],
            out_specs=pl.BlockSpec((1, TOK, 512), lambda i, h: (i, 0, 0)),
        ),
        out_shape=jax.ShapeDtypeStruct((2, TOK, 512), BF),
        compiler_params=params(),
        cost_estimate=pl.CostEstimate(
            flops=1024 * 2048 * 512, bytes_accessed=5 << 20, transcendentals=0
        ),
    )(h, cols, weights)


def whole(shape):
    return pl.BlockSpec(shape, lambda j: (0,) * len(shape))


def scalar():
    return pl.BlockSpec(memory_space=pltpu.SMEM)


L = 256
TILES = 512 // L
PAIR = pl.BlockSpec((1, TOK, 2 * K), lambda j: (j, 0, 0))
FREQ = pl.BlockSpec((1, N, 2 * L), lambda j: (j, 0, 0))


def plain_kernel(window_ref, forward_ref, freq_ref):
    freq_ref[...] = exact_side(forward_ref, window_ref[...])


def plain_part(window, forward):
    tile = pl.BlockSpec((N, 2 * L), lambda j: (0, j))
    return pl.pallas_call(
        plain_kernel,
        grid=(TILES,),
        in_specs=[tile, whole((2, N, N))],
        out_specs=tile,
        out_shape=jax.ShapeDtypeStruct((N, CH), F32),
        compiler_params=params(),
        cost_estimate=pl.CostEstimate(
            flops=2 * CH * N * 2 * N, bytes_accessed=3 << 20, transcendentals=0
        ),
    )(window, forward)


def front_kernel(halo_ref, tok_ref, forward_ref, freq_ref):
    first, second = tok_ref[0, 0], tok_ref[1, 0]
    window = jnp.concatenate(
        [
            jnp.concatenate([halo_ref[...], first[K:]], axis=1),
            jnp.concatenate([first[:K], second[:K]], axis=1),
            jnp.concatenate([first[K:], second[K:]], axis=1),
        ],
        axis=0,
    )
    freq_ref[0] = exact_side(forward_ref, window)


def front_part(halo, tokens, forward):
    return pl.pallas_call(
        front_kernel,
        grid=(TILES,),
        in_specs=[
            pl.BlockSpec((K, L), lambda j: (0, j)),
            pl.BlockSpec((2, 1, TOK, L), lambda j: (0, 0, 0, j)),
            whole((2, N, N)),
        ],
        out_specs=FREQ,
        out_shape=jax.ShapeDtypeStruct((TILES, N, 2 * L), F32),
        compiler_params=params(),
        cost_estimate=pl.CostEstimate(
            flops=2 * CH * N * 2 * N, bytes_accessed=3 << 20, transcendentals=0
        ),
    )(halo, tokens, forward)


def grad_kernel(
    core_ref,
    mix_ref,
    more_ref,
    tok_ref,
    freq_ref,
    own_ref,
    lag_ref,
    keep_ref,
    send_ref,
    first_ref,
    inner_ref,
    cross_ref,
    tap_ref,
):
    is_first = core_ref[0] == 0
    early = (mix_ref[0].astype(F32) + more_ref[0].astype(F32)).astype(BF).astype(F32)
    late = (mix_ref[1].astype(F32) + more_ref[1].astype(F32)).astype(BF).astype(F32)
    keep_ref[...] = jnp.where(is_first, early, late).astype(BF)
    send_ref[...] = jnp.where(is_first, late, early).astype(BF)
    early = early * tok_ref[0, 0].astype(F32)
    late = late * tok_ref[1, 0].astype(F32)
    first_ref[...] = early[:K].astype(BF)
    inner_ref[...] = late[:K].astype(BF)
    cross_ref[...] = jnp.where(is_first, early[:K], late[:K]).astype(BF)
    conv_grad = jnp.concatenate([early, late], axis=1).astype(BF)
    cross = times_conj(exact_side(own_ref, conv_grad), freq_ref[0])
    taps = both_sides(lag_ref, cross[:, :L] + cross[:, L:])
    tap_ref[...] = taps.T.reshape(L // 16, 16, K).astype(tap_ref.dtype)


def grad_part(core, mix, more, tokens, sig_freq, own, lag):
    head = pl.BlockSpec((K, L), lambda j: (0, j))
    half = pl.BlockSpec((TOK, L), lambda j: (0, j))
    return pl.pallas_call(
        grad_kernel,
        grid=(TILES,),
        in_specs=[
            scalar(),
            pl.BlockSpec((2, TOK, L), lambda j: (0, 0, j)),
            pl.BlockSpec((2, TOK, L), lambda j: (0, 0, j)),
            pl.BlockSpec((2, 1, TOK, L), lambda j: (0, 1, 0, j)),
            FREQ,
            whole((2, N, TOK)),
            whole((2, K, N)),
        ],
        out_specs=[half, half, head, head, head, pl.BlockSpec((L // 16, 16, K), lambda j: (j, 0, 0))],
        out_shape=[jax.ShapeDtypeStruct((TOK, 512), BF)] * 2
        + [jax.ShapeDtypeStruct((K, 512), BF)] * 3
        + [jax.ShapeDtypeStruct((32, 16, K), BF)],
        compiler_params=params(),
        cost_estimate=pl.CostEstimate(
            flops=2 * CH * N * (2 * TOK + 2 * K), bytes_accessed=5 << 20, transcendentals=0
        ),
    )(core, mix, more, tokens, sig_freq, own, lag)


def conv_kernel(freq_ref, tap_ref, forward_ref, inv_ref, tap_freq_ref, conv_ref):
    upper, lower = tap_ref[0], tap_ref[1]
    high, low = forward_ref[0], forward_ref[1]
    tap_freq = dot(high, upper, LANES) + dot(low, upper, LANES) + dot(high, lower, LANES)
    tap_freq_ref[...] = tap_freq
    conv_ref[...] = both_sides(inv_ref, times(freq_ref[...], tap_freq))


def wide_tile(rows):
    return pl.BlockSpec((rows, 2 * L), lambda j: (0, j))


def conv_part(sig_freq, taps, forward, inv):
    return pl.pallas_call(
        conv_kernel,
        grid=(TILES,),
        in_specs=[
            wide_tile(N),
            pl.BlockSpec((2, 2 * L, K), lambda j: (0, j, 0)),
            whole((2, N, K)),
            whole((2, TOK, N)),
        ],
        out_specs=[wide_tile(N), wide_tile(TOK)],
        out_shape=[jax.ShapeDtypeStruct((N, CH), F32), jax.ShapeDtypeStruct((TOK, CH), F32)],
        compiler_params=params(),
        cost_estimate=pl.CostEstimate(flops=1024, bytes_accessed=1024, transcendentals=0),
    )(sig_freq, taps, forward, inv)


def out_kernel(
    core_ref,
    keep_ref,
    other_ref,
    inner_ref,
    near_ref,
    far_ref,
    gate_in_ref,
    conv_ref,
    tap_freq_ref,
    forward_ref,
    inv_ref,
    place_ref,
    gate_ref,
    sig_ref,
):
    is_first = core_ref[0] == 0

    def joined(left, right):
        return jnp.concatenate(
            [
                dot(
                    jnp.concatenate([left[:, i : i + K], right[:, i : i + K]], axis=1),
                    place_ref[...],
                )
                for i in range(0, L, K)
            ],
            axis=1,
        )

    keep, other = keep_ref[...], other_ref[...]
    mixed = joined(jnp.where(is_first, keep, other), jnp.where(is_first, other, keep))
    near = near_ref[...]
    halo = joined(
        jnp.where(is_first, inner_ref[...], near), jnp.where(is_first, near, far_ref[...])
    ).astype(BF)
    gate_ref[...] = (mixed * conv_ref[...]).astype(BF)
    conv_grad = (mixed * gate_in_ref[...].astype(F32)).astype(BF)
    full = exact_side(forward_ref, jnp.concatenate([conv_grad, halo], axis=0))
    sig_ref[...] = both_sides(inv_ref, times_conj(full, tap_freq_ref[...])).astype(BF)


def out_part(core, keep, other, inner, near, far, gate, conv, tap_freq, forward, inv, place):
    head = pl.BlockSpec((K, L), lambda j: (0, j))
    half = pl.BlockSpec((TOK, L), lambda j: (0, j))
    return pl.pallas_call(
        out_kernel,
        grid=(TILES,),
        in_specs=[
            scalar(),
            half,
            half,
            head,
            head,
            head,
            wide_tile(TOK),
            wide_tile(TOK),
            wide_tile(N),
            whole((2, N, N)),
            whole((2, TOK, N)),
            whole((2 * K, 2 * K)),
        ],
        out_specs=[wide_tile(TOK), wide_tile(TOK)],
        out_shape=[jax.ShapeDtypeStruct((TOK, CH), BF)] * 2,
        compiler_params=params(),
        cost_estimate=pl.CostEstimate(flops=1024, bytes_accessed=1024, transcendentals=0),
    )(core, keep, other, inner, near, far, gate, conv, tap_freq, forward, inv, place)


def chooser():
    source = np.arange(2 * K).reshape(8, 2, 16).transpose(1, 0, 2).reshape(-1)
    matrix = np.zeros((2 * K, 2 * K), np.float32)
    matrix[source, np.arange(2 * K)] = 1.0
    return matrix.astype(jnp.bfloat16)


def send_kernel(weight_ref, tap_ref, place_ref, out_ref):
    out_ref[...] = jnp.zeros_like(out_ref)
    taps = tap_ref[...]
    high = taps.astype(BF)
    low = (taps - high.astype(F32)).astype(BF)
    for c in range(2):
        out_ref[c, 64:, :K] = high
        out_ref[c, 64:, K : 2 * K] = low
    for i in range(4):
        lanes = slice(i * 2 * K, (i + 1) * 2 * K)
        chosen = dot(weight_ref[:, lanes], place_ref[...]).astype(BF)
        out_ref[0, :64, i * K : (i + 1) * K] = chosen[:, :K]
        out_ref[1, :64, i * K : (i + 1) * K] = chosen[:, K:]


def send_part(weights, taps, place):
    return pl.pallas_call(
        send_kernel,
        out_shape=jax.ShapeDtypeStruct((2, 80, 512), BF),
        compiler_params=pltpu.CompilerParams(vmem_limit_bytes=VMEM),
        cost_estimate=pl.CostEstimate(flops=1 << 25, bytes_accessed=1 << 19, transcendentals=0),
    )(weights, taps, place)


def by_core(values, place):
    rows = values.shape[0]
    chosen = dot(values.reshape(rows * 4, 2 * K), place).astype(BF)
    return chosen.reshape(rows, 4, 2, K).transpose(2, 0, 1, 3).reshape(2, rows, 512)


def on_device(out_grad, out_weight, signal, gate_input, filter_taps):
    chips, ctx = ("z", "h"), ("z", "h", "c")
    period = SPAN // TOK
    fwd, inv = transforms()
    place = chooser()
    core = lax.axis_index("c").reshape(1)

    message = send_part(out_weight.T, filter_taps.T, place)
    block = lax.all_to_all(message, "c", split_axis=0, concat_axis=0)

    block, out_grad, signal, gate_input = lax.optimization_barrier(
        (block, out_grad, signal, gate_input)
    )
    cols = out_grad.reshape(TOK, 2, 2, K).transpose(2, 1, 0, 3)
    weights = lax.all_gather(block, "z", axis=0, tiled=False)
    cols = lax.all_to_all(cols, "h", split_axis=0, concat_axis=0)

    ahead = [(i, i + 1) for i in range(63) if (i + 1) % period]
    window = jnp.concatenate([lax.ppermute(signal[TOK - K :], ctx, ahead), signal], axis=0)
    sig_freq = plain_part(window, fwd[:, :, :N])
    tokens = jnp.concatenate([by_core(signal, place), by_core(gate_input, place)], axis=1)
    tokens = lax.all_to_all(
        tokens.reshape(2, 2, TOK, 512), "c", split_axis=0, concat_axis=0
    )
    ahead = [(i, i + 1) for i in range(31) if (i + 1) % (period // 2)]
    sig_halo = lax.ppermute(tokens[1, 0, TOK - K :], chips, ahead)
    own_freq = front_part(sig_halo, tokens, fwd[:, :, :N])

    cols, sig_freq, own_freq = lax.optimization_barrier((cols, sig_freq, own_freq))
    cols = lax.all_to_all(
        jnp.broadcast_to(cols[None], (8, 2, 2, TOK, K)), ("x", "l"), split_axis=0, concat_axis=0
    )
    cols = lax.all_to_all(
        jnp.broadcast_to(cols[None], (2, 8, 2, 2, TOK, K)), "c", split_axis=0, concat_axis=0
    )

    h = lax.axis_index("h").reshape(1)
    partial = product(1 - h, cols, weights)
    weights, partial = lax.optimization_barrier((weights, partial))
    more = lax.ppermute(partial, "h", [(0, 1), (1, 0)])
    mix = product(h, cols, weights)
    keep, send, first, inner, cross, tap_grad = grad_part(
        core, mix, more, tokens, own_freq, fwd[:, :, K:N], inv[:, :K]
    )
    tap_grad = lax.all_to_all(tap_grad, chips, split_axis=0, concat_axis=0)
    filter_grad = jnp.sum(tap_grad.astype(F32), axis=0).T

    other = lax.ppermute(send, "c", [(0, 1), (1, 0)])
    follows = [(2 * i + 2, 2 * i + 1) for i in range(31) if (i + 1) % (period // 2)]
    near = lax.ppermute(cross, ctx, follows + [(2 * i + 1, 2 * i) for i in range(32)])
    far = lax.ppermute(first, ctx, [(i + 1, j) for i, j in follows])

    taps = weights[:, :, 64:, : 2 * K].reshape(16, 2, 16, 2, K).transpose(3, 0, 1, 2, 4)
    taps, keep = lax.optimization_barrier((taps, keep))
    others = lax.ppermute(taps, "h", [(0, 1), (1, 0)])
    upper_half = lax.axis_index("h") == 0
    taps = jnp.stack(
        [jnp.where(upper_half, taps, others), jnp.where(upper_half, others, taps)], axis=2
    ).reshape(2, CH, K)

    tap_freq, conv = conv_part(sig_freq, taps, fwd[:, :, :K], inv[:, K:])
    gate_grad, signal_grad = out_part(
        core,
        keep,
        other,
        inner,
        near,
        far,
        gate_input,
        conv,
        tap_freq,
        fwd[:, :, K:],
        inv[:, K:],
        place.T,
    )
    return signal_grad, gate_grad, filter_grad


def solution(mesh):
    fine = Mesh(mesh.devices.reshape(16, 2, 2, 4, 2), ("z", "h", "c", "x", "l"))
    ctx, tp = ("z", "h", "c"), ("x", "l")
    in_specs = (P(ctx, tp), P(tp, ctx), P(ctx, tp), P(ctx, tp), P(None, tp + ctx))
    out_specs = (P(ctx, tp), P(ctx, tp), P(None, tp + ctx))
    return jax.shard_map(
        on_device, mesh=fine, in_specs=in_specs, out_specs=out_specs, check_vma=False
    )
```

```python
import jax
import jax.numpy as jnp
import numpy as np
from jax import lax
from jax.experimental import pallas as pl
from jax.experimental.pallas import tpu as pltpu
from jax.sharding import Mesh, PartitionSpec as P

K = 128
TOK = 256
CH = 1024
SPAN = 8192
N = K + TOK
HALF = N // 2
TILE = 256
VMEM = 60 * 1024 * 1024

BF = jnp.bfloat16
F32 = jnp.float32
ROWS = ((1,), (0,))
LANES = ((1,), (1,))


def transforms():
    freq = 2.0 * np.pi * (np.arange(HALF) + 0.5) / N
    angle = freq[:, None] * np.arange(N + K)[None, :]
    forward = np.concatenate([np.cos(angle), -np.sin(angle)], axis=0)
    angle = angle[:, :N].T
    inverse = np.concatenate([np.cos(angle), -np.sin(angle)], axis=1) * (2.0 / N)
    return two(forward), two(inverse)


def two(values):
    values = np.asarray(values, np.float32)
    upper = values.astype(jnp.bfloat16)
    lower = (values - upper.astype(np.float32)).astype(jnp.bfloat16)
    return np.stack([upper, lower])


def dot(a, b, dims=ROWS):
    return lax.dot_general(a, b, (dims, ((), ())), preferred_element_type=F32)


def exact_side(matrix, values):
    return dot(
        jnp.concatenate([matrix[0], matrix[1]], axis=1),
        jnp.concatenate([values, values], axis=0),
    )


def both_sides(matrix, values):
    high = values.astype(BF)
    low = (values - high.astype(F32)).astype(BF)
    return dot(
        jnp.concatenate([matrix[0], matrix[1], matrix[0]], axis=1),
        jnp.concatenate([high, high, low], axis=0),
    )


def times(a, b):
    ar, ai, br, bi = a[:HALF], a[HALF:], b[:HALF], b[HALF:]
    return jnp.concatenate([ar * br - ai * bi, ar * bi + ai * br], axis=0)


def times_conj(a, b):
    ar, ai, br, bi = a[:HALF], a[HALF:], b[:HALF], b[HALF:]
    return jnp.concatenate([ar * br + ai * bi, ai * br - ar * bi], axis=0)


def params(limit=VMEM):
    return pltpu.CompilerParams(
        dimension_semantics=("arbitrary",), vmem_limit_bytes=limit
    )


def product_kernel(cols_ref, weight_ref, out_ref):
    weight = weight_ref[:, :, :64].reshape(16 * K, 512)
    for b in range(2):
        rows = jnp.concatenate([cols_ref[b, i, 0, j] for i in range(8) for j in range(2)], axis=1)
        out_ref[b] = dot(rows, weight).astype(BF)


def product(cols, weights):
    return pl.pallas_call(
        product_kernel,
        grid=(2,),
        in_specs=[
            pl.BlockSpec((2, 8, 1, 2, TOK, K), lambda i: (0, 0, i, 0, 0, 0)),
            pl.BlockSpec((16, 2, 80, 512), lambda i: (0, 0, 0, 0)),
        ],
        out_specs=pl.BlockSpec((2, TOK, 512), lambda i: (i, 0, 0)),
        out_shape=jax.ShapeDtypeStruct((4, TOK, 512), BF),
        compiler_params=params(),
        cost_estimate=pl.CostEstimate(
            flops=2 * 1024 * 2048 * 512, bytes_accessed=8 << 20, transcendentals=0
        ),
    )(cols, weights)


def whole(shape):
    return pl.BlockSpec(shape, lambda j: (0,) * len(shape))


def scalar():
    return pl.BlockSpec(memory_space=pltpu.SMEM)


L = 256
TILES = 512 // L
PAIR = pl.BlockSpec((1, TOK, 2 * K), lambda j: (j, 0, 0))
FREQ = pl.BlockSpec((1, N, 2 * L), lambda j: (j, 0, 0))


def plain_kernel(window_ref, forward_ref, freq_ref):
    freq_ref[...] = exact_side(forward_ref, window_ref[...])


def plain_part(window, forward):
    tile = pl.BlockSpec((N, 2 * L), lambda j: (0, j))
    return pl.pallas_call(
        plain_kernel,
        grid=(TILES,),
        in_specs=[tile, whole((2, N, N))],
        out_specs=tile,
        out_shape=jax.ShapeDtypeStruct((N, CH), F32),
        compiler_params=params(),
        cost_estimate=pl.CostEstimate(
            flops=2 * CH * N * 2 * N, bytes_accessed=3 << 20, transcendentals=0
        ),
    )(window, forward)


def front_kernel(halo_ref, tok_ref, forward_ref, freq_ref):
    first, second = tok_ref[0, 0], tok_ref[1, 0]
    window = jnp.concatenate(
        [
            jnp.concatenate([halo_ref[...], first[K:]], axis=1),
            jnp.concatenate([first[:K], second[:K]], axis=1),
            jnp.concatenate([first[K:], second[K:]], axis=1),
        ],
        axis=0,
    )
    freq_ref[0] = exact_side(forward_ref, window)


def front_part(halo, tokens, forward):
    return pl.pallas_call(
        front_kernel,
        grid=(TILES,),
        in_specs=[
            pl.BlockSpec((K, L), lambda j: (0, j)),
            pl.BlockSpec((2, 1, TOK, L), lambda j: (0, 0, 0, j)),
            whole((2, N, N)),
        ],
        out_specs=FREQ,
        out_shape=jax.ShapeDtypeStruct((TILES, N, 2 * L), F32),
        compiler_params=params(),
        cost_estimate=pl.CostEstimate(
            flops=2 * CH * N * 2 * N, bytes_accessed=3 << 20, transcendentals=0
        ),
    )(halo, tokens, forward)


def grad_kernel(
    core_ref,
    mix_ref,
    tok_ref,
    freq_ref,
    own_ref,
    lag_ref,
    keep_ref,
    send_ref,
    first_ref,
    inner_ref,
    cross_ref,
    tap_ref,
):
    is_first = core_ref[0] == 0
    early = (mix_ref[0, 0].astype(F32) + mix_ref[1, 0].astype(F32)).astype(BF).astype(F32)
    late = (mix_ref[0, 1].astype(F32) + mix_ref[1, 1].astype(F32)).astype(BF).astype(F32)
    keep_ref[...] = jnp.where(is_first, early, late).astype(BF)
    send_ref[...] = jnp.where(is_first, late, early).astype(BF)
    early = early * tok_ref[0, 0].astype(F32)
    late = late * tok_ref[1, 0].astype(F32)
    first_ref[...] = early[:K].astype(BF)
    inner_ref[...] = late[:K].astype(BF)
    cross_ref[...] = jnp.where(is_first, early[:K], late[:K]).astype(BF)
    conv_grad = jnp.concatenate([early, late], axis=1).astype(BF)
    cross = times_conj(exact_side(own_ref, conv_grad), freq_ref[0])
    taps = both_sides(lag_ref, cross[:, :L] + cross[:, L:])
    tap_ref[...] = taps.T.reshape(L // 16, 16, K).astype(tap_ref.dtype)


def grad_part(core, mix, tokens, sig_freq, own, lag):
    head = pl.BlockSpec((K, L), lambda j: (0, j))
    half = pl.BlockSpec((TOK, L), lambda j: (0, j))
    return pl.pallas_call(
        grad_kernel,
        grid=(TILES,),
        in_specs=[
            scalar(),
            pl.BlockSpec((2, 2, TOK, L), lambda j: (0, 0, 0, j)),
            pl.BlockSpec((2, 1, TOK, L), lambda j: (0, 1, 0, j)),
            FREQ,
            whole((2, N, TOK)),
            whole((2, K, N)),
        ],
        out_specs=[half, half, head, head, head, pl.BlockSpec((L // 16, 16, K), lambda j: (j, 0, 0))],
        out_shape=[jax.ShapeDtypeStruct((TOK, 512), BF)] * 2
        + [jax.ShapeDtypeStruct((K, 512), BF)] * 3
        + [jax.ShapeDtypeStruct((32, 16, K), BF)],
        compiler_params=params(),
        cost_estimate=pl.CostEstimate(
            flops=2 * CH * N * (2 * TOK + 2 * K), bytes_accessed=5 << 20, transcendentals=0
        ),
    )(core, mix, tokens, sig_freq, own, lag)


def conv_kernel(
    h_ref, freq_ref, tap_ref, more_ref, forward_ref, inv_ref, tap_freq_ref, conv_ref
):
    is_first = h_ref[0] == 0
    taps, more = tap_ref[...].astype(F32), more_ref[...].astype(F32)
    taps = jnp.stack(
        [jnp.where(is_first, taps, more), jnp.where(is_first, more, taps)], axis=2
    ).astype(BF)
    upper, lower = taps[0].reshape(2 * L, K), taps[1].reshape(2 * L, K)
    high, low = forward_ref[0], forward_ref[1]
    tap_freq = dot(high, upper, LANES) + dot(low, upper, LANES) + dot(high, lower, LANES)
    tap_freq_ref[...] = tap_freq
    conv_ref[...] = both_sides(inv_ref, times(freq_ref[...], tap_freq))


def wide_tile(rows):
    return pl.BlockSpec((rows, 2 * L), lambda j: (0, j))


def conv_part(h, sig_freq, taps, more, forward, inv):
    tap = pl.BlockSpec((2, L // 32, 2, 16, K), lambda j: (0, j, 0, 0, 0))
    return pl.pallas_call(
        conv_kernel,
        grid=(TILES,),
        in_specs=[
            scalar(),
            wide_tile(N),
            tap,
            tap,
            whole((2, N, K)),
            whole((2, TOK, N)),
        ],
        out_specs=[wide_tile(N), wide_tile(TOK)],
        out_shape=[jax.ShapeDtypeStruct((N, CH), F32), jax.ShapeDtypeStruct((TOK, CH), F32)],
        compiler_params=params(),
        cost_estimate=pl.CostEstimate(flops=1024, bytes_accessed=1024, transcendentals=0),
    )(h, sig_freq, taps, more, forward, inv)


def out_kernel(
    core_ref,
    keep_ref,
    other_ref,
    inner_ref,
    near_ref,
    far_ref,
    gate_in_ref,
    conv_ref,
    tap_freq_ref,
    forward_ref,
    inv_ref,
    place_ref,
    gate_ref,
    sig_ref,
):
    is_first = core_ref[0] == 0

    def joined(left, right):
        return jnp.concatenate(
            [
                dot(
                    jnp.concatenate([left[:, i : i + K], right[:, i : i + K]], axis=1),
                    place_ref[...],
                )
                for i in range(0, L, K)
            ],
            axis=1,
        )

    keep, other = keep_ref[...], other_ref[...]
    mixed = joined(jnp.where(is_first, keep, other), jnp.where(is_first, other, keep))
    near = near_ref[...]
    halo = joined(
        jnp.where(is_first, inner_ref[...], near), jnp.where(is_first, near, far_ref[...])
    ).astype(BF)
    gate_ref[...] = (mixed * conv_ref[...]).astype(BF)
    conv_grad = (mixed * gate_in_ref[...].astype(F32)).astype(BF)
    full = exact_side(forward_ref, jnp.concatenate([conv_grad, halo], axis=0))
    sig_ref[...] = both_sides(inv_ref, times_conj(full, tap_freq_ref[...])).astype(BF)


def out_part(core, keep, other, inner, near, far, gate, conv, tap_freq, forward, inv, place):
    head = pl.BlockSpec((K, L), lambda j: (0, j))
    half = pl.BlockSpec((TOK, L), lambda j: (0, j))
    return pl.pallas_call(
        out_kernel,
        grid=(TILES,),
        in_specs=[
            scalar(),
            half,
            half,
            head,
            head,
            head,
            wide_tile(TOK),
            wide_tile(TOK),
            wide_tile(N),
            whole((2, N, N)),
            whole((2, TOK, N)),
            whole((2 * K, 2 * K)),
        ],
        out_specs=[wide_tile(TOK), wide_tile(TOK)],
        out_shape=[jax.ShapeDtypeStruct((TOK, CH), BF)] * 2,
        compiler_params=params(),
        cost_estimate=pl.CostEstimate(flops=1024, bytes_accessed=1024, transcendentals=0),
    )(core, keep, other, inner, near, far, gate, conv, tap_freq, forward, inv, place)


def chooser():
    source = np.arange(2 * K).reshape(8, 2, 16).transpose(1, 0, 2).reshape(-1)
    matrix = np.zeros((2 * K, 2 * K), np.float32)
    matrix[source, np.arange(2 * K)] = 1.0
    return matrix.astype(jnp.bfloat16)


def send_kernel(weight_ref, tap_ref, place_ref, out_ref):
    out_ref[...] = jnp.zeros_like(out_ref)
    taps = tap_ref[...]
    high = taps.astype(BF)
    low = (taps - high.astype(F32)).astype(BF)
    for c in range(2):
        out_ref[c, 64:, :K] = high
        out_ref[c, 64:, K : 2 * K] = low
    for i in range(4):
        lanes = slice(i * 2 * K, (i + 1) * 2 * K)
        chosen = dot(weight_ref[:, lanes], place_ref[...]).astype(BF)
        out_ref[0, :64, i * K : (i + 1) * K] = chosen[:, :K]
        out_ref[1, :64, i * K : (i + 1) * K] = chosen[:, K:]


def send_part(weights, taps, place):
    return pl.pallas_call(
        send_kernel,
        out_shape=jax.ShapeDtypeStruct((2, 80, 512), BF),
        compiler_params=pltpu.CompilerParams(vmem_limit_bytes=VMEM),
        cost_estimate=pl.CostEstimate(flops=1 << 25, bytes_accessed=1 << 19, transcendentals=0),
    )(weights, taps, place)


def by_core(values, place):
    rows = values.shape[0]
    chosen = dot(values.reshape(rows * 4, 2 * K), place).astype(BF)
    return chosen.reshape(rows, 4, 2, K).transpose(2, 0, 1, 3).reshape(2, rows, 512)


def on_device(out_grad, out_weight, signal, gate_input, filter_taps):
    chips, ctx = ("z", "h"), ("z", "h", "c")
    period = SPAN // TOK
    fwd, inv = transforms()
    place = chooser()
    core = lax.axis_index("c").reshape(1)

    message = send_part(out_weight.T, filter_taps.T, place)
    block = lax.all_to_all(message, "c", split_axis=0, concat_axis=0)

    block, out_grad, signal, gate_input = lax.optimization_barrier(
        (block, out_grad, signal, gate_input)
    )
    cols = out_grad.reshape(TOK, 2, 2, K).transpose(2, 1, 0, 3)
    weights = lax.all_gather(block, "z", axis=0, tiled=False)
    cols = lax.all_to_all(cols, "h", split_axis=0, concat_axis=0)

    ahead = [(i, i + 1) for i in range(63) if (i + 1) % period]
    window = jnp.concatenate([lax.ppermute(signal[TOK - K :], ctx, ahead), signal], axis=0)
    sig_freq = plain_part(window, fwd[:, :, :N])
    tokens = jnp.concatenate([by_core(signal, place), by_core(gate_input, place)], axis=1)
    tokens = lax.all_to_all(
        tokens.reshape(2, 2, TOK, 512), "c", split_axis=0, concat_axis=0
    )
    ahead = [(i, i + 1) for i in range(31) if (i + 1) % (period // 2)]
    sig_halo = lax.ppermute(tokens[1, 0, TOK - K :], chips, ahead)
    own_freq = front_part(sig_halo, tokens, fwd[:, :, :N])

    cols, sig_freq, own_freq = lax.optimization_barrier((cols, sig_freq, own_freq))
    cols = lax.all_to_all(
        jnp.broadcast_to(cols[None], (8, 2, 2, TOK, K)), ("x", "l"), split_axis=0, concat_axis=0
    )
    cols = lax.all_to_all(
        jnp.broadcast_to(cols[None], (2, 8, 2, 2, TOK, K)), "c", split_axis=0, concat_axis=0
    )

    partial = product(cols, weights)
    weights, partial = lax.optimization_barrier((weights, partial))
    mix = lax.all_to_all(
        partial.reshape(2, 2, TOK, 512), "h", split_axis=0, concat_axis=0
    )
    taps = weights[:, :, 64:, : 2 * K].reshape(16, 2, 16, 2, K).transpose(3, 0, 1, 2, 4)
    more = lax.ppermute(taps, "h", [(0, 1), (1, 0)])
    mix, more = lax.optimization_barrier((mix, more))
    keep, send, first, inner, cross, tap_grad = grad_part(
        core, mix, tokens, own_freq, fwd[:, :, K:N], inv[:, :K]
    )
    tap_grad = lax.all_to_all(tap_grad, chips, split_axis=0, concat_axis=0)
    filter_grad = jnp.sum(tap_grad.astype(F32), axis=0).T

    other = lax.ppermute(send, "c", [(0, 1), (1, 0)])
    follows = [(2 * i + 2, 2 * i + 1) for i in range(31) if (i + 1) % (period // 2)]
    near = lax.ppermute(cross, ctx, follows + [(2 * i + 1, 2 * i) for i in range(32)])
    far = lax.ppermute(first, ctx, [(i + 1, j) for i, j in follows])

    tap_freq, conv = conv_part(
        lax.axis_index("h").reshape(1), sig_freq, taps, more, fwd[:, :, :K], inv[:, K:]
    )
    gate_grad, signal_grad = out_part(
        core,
        keep,
        other,
        inner,
        near,
        far,
        gate_input,
        conv,
        tap_freq,
        fwd[:, :, K:],
        inv[:, K:],
        place.T,
    )
    return signal_grad, gate_grad, filter_grad


def solution(mesh):
    fine = Mesh(mesh.devices.reshape(16, 2, 2, 4, 2), ("z", "h", "c", "x", "l"))
    ctx, tp = ("z", "h", "c"), ("x", "l")
    in_specs = (P(ctx, tp), P(tp, ctx), P(ctx, tp), P(ctx, tp), P(None, tp + ctx))
    out_specs = (P(ctx, tp), P(ctx, tp), P(None, tp + ctx))
    return jax.shard_map(
        on_device, mesh=fine, in_specs=in_specs, out_specs=out_specs, check_vma=False
    )
```
